32 devices in a mesh: dp: 16 (over z, x, core), mp: 2 (over y).
Axes of the slice: x: 2, y: 2, z: 4, core: 2. Of those that a mesh axis runs over, the one named last changes fastest.
Arguments:
- tokens: bfloat16 [16384, 768], P(('dp', 'mp')), may hold values from -6 to 6
- pair_left: bfloat16 [16384, 256], P(('dp', 'mp')), may hold values from -6 to 6
- pair_right: bfloat16 [16384, 256], P(('dp', 'mp')), may hold values from -6 to 6
- chain_len: int32 [16, 8], P('dp'), may hold values from 0 to 800, as said below
- chain_time: float32 [16, 8], P('dp'), may hold values from 0 to 1
- chain_arch: int32 [16, 8], P('dp'), may hold values from 0 to 42
- cath_table: bfloat16 [43, 256], replicated, may hold values from -6 to 6
- time_weight: bfloat16 [256, 256], replicated, may hold values from -0.375 to 0.375
- mod_weight: bfloat16 [256, 4608], replicated, may hold values from -0.1875 to 0.1875
- mod_bias: bfloat16 [4608], replicated, may hold values from -3 to 3
- qkv_weight: bfloat16 [3, 768, 768], P(None, None, 'mp'), may hold values from -0.21875 to 0.21875
- pair_weight: bfloat16 [256, 12], P(None, 'mp'), may hold values from -0.375 to 0.375
- out_weight: bfloat16 [768, 768], P('mp'), may hold values from -1.25 to 1.25
- gate_up_weight: bfloat16 [2, 768, 3072], P(None, None, 'mp'), may hold values from -0.21875 to 0.21875
- down_weight: bfloat16 [3072, 768], P('mp'), may hold values from -0.21875 to 0.21875
- cotangent: bfloat16 [16384, 768], P(('dp', 'mp')), may hold values from -6 to 6
Outputs:
- mixed: bfloat16 [16384, 768], P(('dp', 'mp'))
- tokens_grad: bfloat16 [16384, 768], P(('dp', 'mp'))
- left_grad: bfloat16 [16384, 256], P(('dp', 'mp'))
- right_grad: bfloat16 [16384, 256], P(('dp', 'mp'))
- cath_grad: float32 [43, 256], replicated
- time_grad: float32 [256, 256], replicated
- mod_weight_grad: float32 [256, 4608], replicated
- mod_bias_grad: float32 [4608], replicated
- qkv_grad: float32 [3, 768, 768], P(None, 'dp', 'mp')
- pair_weight_grad: float32 [256, 12], P('dp', 'mp')
- out_weight_grad: float32 [768, 768], P('mp', 'dp')
- gate_up_grad: float32 [2, 768, 3072], P(None, 'dp', 'mp')
- down_grad: float32 [3072, 768], P('mp', 'dp')
The draws below stay inside these ranges and needn't reach their ends.
Inputs may be any that keep to these rules, and one draw needn't show every extreme that they name: `chain_len`: row g gives the lengths of the chains packed one after another from the first position of group g; the first is the row's longest and exceeds 1024/2; zeros are empty slots; a row sums to at most 1024, positions after its sum are padding; some row's first length is exactly 800.
All inputs are finite; a program needn't handle non-finite values.
Results may differ from the reference program's by a relative error of at most 0.019.
Values may be sent and summed in bfloat16 or wider, within the bound.
No kernel may reach another device: no remote copies, remote signals or barrier semaphores. Data moves between devices by JAX's collectives and lax.ppermute only.
A program may use at most 192 MiB of HBM per device.

```python
import math
import jax
import jax.numpy as jnp
from jax import lax

D = 768
HEADS = 12
HEAD = 64
PAIR = 256
FF = 3072
COND = 256
NARCH = 43
MAXCH = 8
TOK_DEV = 512
LONGEST = 800
TOKENS = 16384
N_DP = 16
N_MP = 2


def draw_chain_len(key, part):
    key = jax.random.fold_in(key, 7)
    key_first, key_pick, key_rest, key_pad = jax.random.split(key, 4)
    group_rows = TOK_DEV * N_MP
    first_len = jax.random.randint(key_first, (N_DP,), group_rows // 2 + 1, LONGEST + 1)
    chosen = jax.random.randint(key_pick, (), 0, N_DP)
    first_len = jnp.where(jnp.arange(N_DP) == chosen, LONGEST, first_len)
    least_len = max(1, group_rows * 50 // 1024)
    most_len = max(least_len + 1, group_rows * 250 // 1024)
    rest_len = jax.random.randint(key_rest, (N_DP, MAXCH - 1), least_len, most_len + 1)
    padding = jax.random.randint(key_pad, (N_DP,), 0, group_rows // 32 + 1)
    room_left = group_rows - first_len - padding
    rest_ends = jnp.cumsum(rest_len, axis=1)
    rest_starts = rest_ends - rest_len
    rest_len = jnp.clip(jnp.minimum(rest_ends, room_left[:, None]) - rest_starts, 0, None)
    return jnp.concatenate([first_len[:, None], rest_len], axis=1).astype(jnp.int32)


def set_ends(values, rng, smallest, high):
    index_at = [jax.random.randint(jax.random.fold_in(rng, axis), (), 0, length) for axis, length in enumerate(values.shape)]
    widest = values.shape.index(max(values.shape))
    beside = index_at[:widest] + [(index_at[widest] + 1) % values.shape[widest]] + index_at[widest + 1:]
    return values.at[tuple(index_at)].set(smallest).at[tuple(beside)].set(high)


def raised(array, rng, source, target, shards_of, factor):
    def block_of(dim):
        return (jnp.arange(array.shape[dim]) // (array.shape[dim] // shards_of)).reshape((-1,) + (1,) * (array.ndim - 1 - dim))

    near = jax.random.permutation(rng, shards_of)[block_of(target)]
    other_side = (block_of(target) + shards_of // 2) % shards_of
    return jnp.where((block_of(source) == near) | (block_of(source) == other_side), factor * array, array)


def shard_levels(rng, shape, cuts, smallest, high):
    def one(axis_at, shards_of):
        heights = jax.random.uniform(jax.random.fold_in(jax.random.fold_in(rng, 6), axis_at), (shards_of,), jnp.float32, smallest / len(cuts), high / len(cuts))
        return jnp.repeat(jnp.exp(heights), shape[axis_at] // shards_of).reshape((-1,) + (1,) * (len(shape) - axis_at - 1))

    factor_of = one(*cuts[0])
    for cut in cuts[1:]:
        factor_of = factor_of * one(*cut)
    return factor_of


def bell_draw(rng, shape, deviation, reach, cuts=(), kind=jnp.bfloat16):
    array = jax.random.normal(rng, shape, jnp.float32) * deviation
    if len(cuts) > 0:
        array = shard_levels(rng, shape, cuts, -0.22, 0.18) * array
    return jnp.clip(array, min=-reach, max=reach).astype(kind)


def gaussian_with(rng, shape, scale, limit, cuts, heavy, kind=jnp.bfloat16):
    array = scale * jax.random.normal(rng, shape, jnp.float32)
    if cuts:
        array = array * shard_levels(rng, shape, cuts, -0.22, 0.18)
    return jnp.clip(raised(array, jax.random.fold_in(rng, 3), *heavy), -limit, limit).astype(kind)


def setup_inputs(seed: int = 0) -> dict:
    splits = jax.random.split(jax.random.key(seed), 17)
    tokens = bell_draw(splits[0], (TOKENS, D), 1.0, 6.0, ((0, 32),))
    pair_left = bell_draw(splits[1], (TOKENS, PAIR), 1.0, 6.0, ((0, 32),))
    pair_right = bell_draw(splits[2], (TOKENS, PAIR), 1.0, 6.0, ((0, 32),))
    chain_len = draw_chain_len(jax.random.fold_in(splits[16], 71), 0)
    chain_time = jnp.clip(1.0 * jax.random.uniform(splits[4], (N_DP, MAXCH), jnp.float32) ** shard_levels(splits[4], (N_DP, MAXCH), ((0, 16),), -0.2, 0.2), 0.0, 1.0)
    chain_arch = set_ends(jax.random.randint(splits[5], (N_DP, MAXCH), 0, NARCH), jax.random.fold_in(splits[5], 1), 0, NARCH - 1).astype(jnp.int32)
    cath_table = bell_draw(splits[6], (NARCH, COND), 1.0, 6.0)
    time_weight = bell_draw(splits[7], (COND, COND), COND ** -0.5, 0.375)
    mod_weight = bell_draw(splits[8], (COND, 6 * D), (4 * COND) ** -0.5, 0.1875)
    mod_bias = bell_draw(splits[9], (6 * D,), 0.5, 3.0)
    qkv_weight = bell_draw(splits[10], (3, D, D), D ** -0.5, 0.21875, ((2, 2),))
    pair_weight = bell_draw(splits[11], (PAIR, HEADS), PAIR ** -0.5, 0.375, ((1, 2),))
    out_weight = bell_draw(splits[12], (D, D), (D // 32) ** -0.5, 1.25, ((0, 2),))
    gate_up_weight = bell_draw(splits[13], (2, D, FF), D ** -0.5, 0.21875, ((2, 2),))
    down_weight = bell_draw(splits[14], (FF, D), (FF // 4) ** -0.5, 0.21875, ((0, 2),))
    cotangent = gaussian_with(splits[15], (TOKENS, D), 1.0, 6.0, ((0, 32),), (0, 1, 32, 2.75))
    return {"tokens": tokens, "pair_left": pair_left, "pair_right": pair_right, "chain_len": chain_len, "chain_time": chain_time, "chain_arch": chain_arch, "cath_table": cath_table, "time_weight": time_weight, "mod_weight": mod_weight, "mod_bias": mod_bias, "qkv_weight": qkv_weight, "pair_weight": pair_weight, "out_weight": out_weight, "gate_up_weight": gate_up_weight, "down_weight": down_weight, "cotangent": cotangent}


EPSILON = 1e-06

@jax.custom_vjp
def low(v):
    return lax.optimization_barrier(v.astype(jnp.bfloat16)).astype(jnp.float32)

@jax.custom_vjp
def low_back(v):
    return v

def low_keep(v):
    return (low(v), None)

def low_pass(kept, grad):
    return (grad,)

def back_keep(v):
    return (v, None)

def back_low(kept, grad):
    return (low(grad),)
low.defvjp(low_keep, low_pass)
low_back.defvjp(back_keep, back_low)

def highest_dot(left_side, right_side):
    return jnp.dot(left_side, right_side, precision=lax.Precision.HIGHEST)

def apply_norm(values):
    centered = values - lax.optimization_barrier(jnp.mean(values, axis=-1, keepdims=True))
    return centered * lax.rsqrt(lax.optimization_barrier(jnp.mean(centered * centered, axis=-1, keepdims=True)) + EPSILON)

def swish(values):
    return values * jax.nn.sigmoid(values)

def group_layer(weight_set, group_x, group_left, group_right, chain_lens, chain_times, chain_archs):
    cath_rows, time_mix, mod_mix, mod_shift, qkv_mix, pair_mix, out_mix, gate_up_mix, down_mix = weight_set
    group_rows = group_x.shape[0]
    chain_ends = jnp.cumsum(chain_lens).astype(jnp.int32)
    positions = jnp.arange(group_rows, dtype=jnp.int32)
    chain_ids = lax.optimization_barrier(jnp.sum((positions[:, None] >= chain_ends[None, :]).astype(jnp.int32), axis=1))
    membership = (chain_ids[:, None] == jnp.arange(MAXCH, dtype=jnp.int32)[None, :]).astype(jnp.float32)
    valid_rows = (chain_ids < MAXCH).astype(jnp.float32)[:, None]
    half_cond = COND // 2
    frequency = jnp.exp(jnp.arange(half_cond, dtype=jnp.float32) * (-math.log(10000.0) / half_cond))
    angles = chain_times[:, None] * 1000.0 * frequency[None, :]
    time_embed = low(jnp.concatenate([jnp.sin(angles), jnp.cos(angles)], axis=1))
    arch_onehot = (chain_archs[:, None] == jnp.arange(NARCH, dtype=jnp.int32)[None, :]).astype(jnp.float32)
    cond_pre = highest_dot(time_embed, time_mix) + highest_dot(arch_onehot, cath_rows)
    cond_act = low(swish(cond_pre))
    chain_mod = highest_dot(cond_act, mod_mix) + mod_shift[None, :]
    token_mod = highest_dot(membership, chain_mod)
    attention_offset, attention_scale, gate_attn, feedforward_offset, feedforward_scale, gate_ffn = jnp.split(token_mod, 6, axis=1)
    attention_normed = low(apply_norm(group_x) * (1.0 + attention_scale) + attention_offset)
    queries = low(low_back(highest_dot(attention_normed, qkv_mix[0]))).reshape(group_rows, HEADS, HEAD)
    keys_all = low(low_back(highest_dot(attention_normed, qkv_mix[1]))).reshape(group_rows, HEADS, HEAD)
    values_all = low(low_back(highest_dot(attention_normed, qkv_mix[2]))).reshape(group_rows, HEADS, HEAD)
    pair_query = low(group_left[:, None, :] * jnp.transpose(pair_mix)[None, :, :])
    score_scale = HEAD ** (-0.5)
    scores = score_scale * jnp.einsum('qhd,khd->hqk', queries, keys_all, precision=lax.Precision.HIGHEST)
    scores = scores + jnp.einsum('qhc,kc->hqk', pair_query, group_right, precision=lax.Precision.HIGHEST)
    scores = low_back(scores)
    same_chain = chain_ids[:, None] == chain_ids[None, :]
    scores = jnp.where(same_chain[None, :, :], scores, -1e+30)
    row_max = lax.optimization_barrier(jnp.max(scores, axis=-1, keepdims=True))
    exponent = jnp.exp(scores - row_max)
    probs_full = exponent / lax.optimization_barrier(jnp.sum(exponent, axis=-1, keepdims=True))
    attended = jnp.einsum('hqk,khd->qhd', low(probs_full), values_all, precision=lax.Precision.HIGHEST)
    attended = low(low_back(attended.reshape(group_rows, HEADS * HEAD)))
    attn_branch = low_back(highest_dot(attended, out_mix))
    middle_residual = group_x + valid_rows * gate_attn * attn_branch
    feedforward_normed = low(apply_norm(middle_residual) * (1.0 + feedforward_scale) + feedforward_offset)
    gate_act = low_back(highest_dot(feedforward_normed, gate_up_mix[0]))
    up_act = low_back(highest_dot(feedforward_normed, gate_up_mix[1]))
    hidden = low(swish(gate_act) * up_act)
    ffn_branch = low_back(highest_dot(hidden, down_mix))
    return middle_residual + valid_rows * gate_ffn * ffn_branch

def reference(tokens, pair_left, pair_right, chain_len, chain_time, chain_arch, cath_table, time_weight, mod_weight, mod_bias, qkv_weight, pair_weight, out_weight, gate_up_weight, down_weight, cotangent):
    group_rows = TOK_DEV * N_MP
    weight_set = tuple((item.astype(jnp.float32) for item in (cath_table, time_weight, mod_weight, mod_bias, qkv_weight, pair_weight, out_weight, gate_up_weight, down_weight)))

    def forward(layer_input, inputs_left, inputs_right, weights_in):
        stacked = (layer_input.reshape(N_DP, group_rows, D), inputs_left.reshape(N_DP, group_rows, PAIR), inputs_right.reshape(N_DP, group_rows, PAIR), chain_len, chain_time, chain_arch)

        def per_group(item):
            return jax.checkpoint(group_layer)(weights_in, *item)
        return lax.map(per_group, stacked).reshape(N_DP * group_rows, D)
    mixed, pullback = jax.vjp(forward, tokens.astype(jnp.float32), pair_left.astype(jnp.float32), pair_right.astype(jnp.float32), weight_set)
    grad_x, grad_left, grad_right, grad_weights = pullback(cotangent.astype(jnp.float32))
    return (mixed.astype(jnp.bfloat16), grad_x.astype(jnp.bfloat16), grad_left.astype(jnp.bfloat16), grad_right.astype(jnp.bfloat16), grad_weights[0], grad_weights[1], grad_weights[2], grad_weights[3], grad_weights[4], grad_weights[5], grad_weights[6], grad_weights[7], grad_weights[8])
```

```python
import math

import jax
import jax.numpy as jnp
from jax import lax
from jax.sharding import PartitionSpec as P

EPSILON = 1e-06
AXES = ("dp", "mp")
BF16 = jnp.bfloat16
F32 = jnp.float32


def apply_norm(values):
    centered = values - jnp.mean(values, axis=-1, keepdims=True)
    inverse = lax.rsqrt(jnp.mean(centered * centered, axis=-1, keepdims=True) + EPSILON)
    return (centered * inverse, inverse)


def norm_backward(d_hat, x_hat, inverse):
    return inverse * (
        d_hat
        - jnp.mean(d_hat, axis=-1, keepdims=True)
        - x_hat * jnp.mean(d_hat * x_hat, axis=-1, keepdims=True)
    )


def highest_dot(left_side, right_side):
    return jnp.dot(left_side, right_side, precision=lax.Precision.HIGHEST)


def silu_parts(values):
    sigma = jax.nn.sigmoid(values)
    return (values * sigma, sigma * (1.0 + values * (1.0 - sigma)))


def dot_f32(left_side, right_side):
    return jnp.dot(left_side, right_side, preferred_element_type=F32)


def dot_nt(left_side, right_side):
    return lax.dot_general(
        left_side, right_side, (((1,), (1,)), ((), ())), preferred_element_type=F32
    )


def make_moves(dp_count):
    def pairs(target):
        moved = []
        for d in range(dp_count):
            for m in range(2):
                to_d, to_m = target(d, m)
                moved.append((d * 2 + m, to_d * 2 + to_m))
        return moved

    def mover(target):
        table = pairs(target)
        return lambda array: lax.ppermute(array, AXES, table)

    turn = mover(lambda d, m: ((d & ~1) | m, d & 1))
    across = mover(lambda d, m: (d, 1 - m))

    def flip(bit):
        return mover(lambda d, m: (d ^ (1 << bit), m))

    return turn, across, flip


def shards(
    tokens,
    pair_left,
    pair_right,
    chain_len,
    chain_time,
    chain_arch,
    cath_table,
    time_weight,
    mod_weight,
    mod_bias,
    qkv_weight,
    pair_weight,
    out_weight,
    gate_up_weight,
    down_weight,
    cotangent,
):
    dp_count = lax.axis_size("dp")
    bits = dp_count.bit_length() - 1
    turn, across, flip = make_moves(dp_count)
    core_swap = flip(0)
    dp_at = lax.axis_index("dp")
    mp_at = lax.axis_index("mp")
    core = dp_at & 1
    rows, width = tokens.shape
    slots = chain_len.shape[1]
    half_heads = pair_weight.shape[1]
    heads = 2 * half_heads
    head_width = qkv_weight.shape[2] // half_heads
    cond_width = time_weight.shape[0]
    score_scale = head_width ** (-0.5)

    held_chains = jnp.concatenate(
        [chain_len.astype(F32), chain_time, chain_arch.astype(F32)], axis=0
    )
    near_chains = core_swap(held_chains)
    chains = jnp.where(core == mp_at, held_chains, near_chains)
    lengths = chains[0].astype(jnp.int32)
    times = chains[1]
    arches = chains[2].astype(jnp.int32)
    ends = jnp.cumsum(lengths)

    def ids_of(half):
        positions = jnp.arange(rows, dtype=jnp.int32) + half * rows
        return jnp.sum((positions[:, None] >= ends[None, :]).astype(jnp.int32), axis=1)

    own_ids = ids_of(core)
    key_ids = jnp.concatenate([own_ids, ids_of(1 - core)])
    membership = own_ids[:, None] == jnp.arange(slots, dtype=jnp.int32)[None, :]
    member_low = membership.astype(BF16)
    membership = membership.astype(F32)
    valid = (own_ids < slots).astype(F32)[:, None]

    half_cond = cond_width // 2
    frequency = jnp.exp(jnp.arange(half_cond, dtype=F32) * (-math.log(10000.0) / half_cond))
    angles = times[:, None] * 1000.0 * frequency[None, :]
    time_embed = jnp.concatenate([jnp.sin(angles), jnp.cos(angles)], axis=1).astype(BF16)
    arch_onehot = (
        arches[:, None] == jnp.arange(cath_table.shape[0], dtype=jnp.int32)[None, :]
    ).astype(F32)
    cond_pre = dot_f32(time_embed, time_weight) + highest_dot(arch_onehot, cath_table.astype(F32))
    cond_value, cond_slope = silu_parts(cond_pre)
    cond_act = cond_value.astype(BF16)
    chain_mod = dot_f32(cond_act, mod_weight) + mod_bias.astype(F32)[None, :]
    token_mod = highest_dot(membership, chain_mod)
    shift_a, scale_a, gate_a, shift_f, scale_f, gate_f = jnp.split(token_mod, 6, axis=1)

    layer_in = turn(tokens).astype(F32)
    pair_own = turn(jnp.concatenate([pair_left, pair_right], axis=1))
    left_own, right_own = jnp.split(pair_own, 2, axis=1)
    dout = turn(cotangent).astype(F32)

    def other_half(weight, axis):
        size = weight.shape[axis] // 2
        piece = lax.dynamic_slice_in_dim(weight, core * size, size, axis)
        mine = across(piece)
        near = core_swap(mine)
        return jnp.where(
            core == 0,
            jnp.concatenate([mine, near], axis=axis),
            jnp.concatenate([near, mine], axis=axis),
        )

    qkv_all = jnp.concatenate([qkv_weight, other_half(qkv_weight, 2)], axis=2)
    pair_mix = jnp.concatenate([pair_weight, across(pair_weight)], axis=1).astype(F32)
    out_all = jnp.concatenate([out_weight, other_half(out_weight, 0)], axis=0)
    gate_up_all = jnp.concatenate([gate_up_weight, other_half(gate_up_weight, 2)], axis=2)
    down_all = jnp.concatenate([down_weight, other_half(down_weight, 0)], axis=0)

    x_hat, x_inverse = apply_norm(layer_in)
    normed_a = (x_hat * (1.0 + scale_a) + shift_a).astype(BF16)
    projected = jnp.einsum("td,kdf->ktf", normed_a, qkv_all, preferred_element_type=F32).astype(
        BF16
    )
    sent = jnp.concatenate([projected[1], projected[2], right_own], axis=1)
    near = core_swap(sent)
    keys = jnp.concatenate([projected[1], near[:, :width]]).reshape(-1, heads, head_width)
    values = jnp.concatenate([projected[2], near[:, width : 2 * width]]).reshape(
        -1, heads, head_width
    )
    right_all = jnp.concatenate([right_own, near[:, 2 * width :]])
    queries = projected[0].reshape(rows, heads, head_width)
    pair_query = (
        left_own.astype(F32)[:, None, :] * jnp.transpose(pair_mix)[None, :, :]
    ).astype(BF16)
    scores = score_scale * jnp.einsum("qhd,khd->hqk", queries, keys, preferred_element_type=F32)
    scores = scores + jnp.einsum(
        "qhc,kc->hqk", pair_query, right_all, preferred_element_type=F32
    )
    allowed = own_ids[:, None] == key_ids[None, :]
    scores = jnp.where(allowed[None], scores, -1e30)
    exponent = jnp.exp(scores - jnp.max(scores, axis=-1, keepdims=True))
    probs = (exponent / jnp.sum(exponent, axis=-1, keepdims=True)).astype(BF16)
    attended = (
        jnp.einsum("hqk,khd->qhd", probs, values, preferred_element_type=F32)
        .astype(BF16)
        .reshape(rows, width)
    )
    attn_branch = dot_f32(attended, out_all)
    middle = layer_in + valid * gate_a * attn_branch

    m_hat, m_inverse = apply_norm(middle)
    normed_f = (m_hat * (1.0 + scale_f) + shift_f).astype(BF16)
    d_ffn = (valid * gate_f * dout).astype(BF16)
    gate_act = dot_f32(normed_f, gate_up_all[0])
    up_act = dot_f32(normed_f, gate_up_all[1])
    gate_value, gate_slope = silu_parts(gate_act)
    hidden = (gate_value * up_act).astype(BF16)
    ffn_branch = dot_f32(hidden, down_all)
    mixed = turn((middle + valid * gate_f * ffn_branch).astype(BF16))
    d_hidden = dot_nt(d_ffn, down_all)
    d_gate = (d_hidden * up_act * gate_slope).astype(BF16)
    d_up = (d_hidden * gate_value).astype(BF16)
    d_normed_f = dot_nt(d_gate, gate_up_all[0]) + dot_nt(d_up, gate_up_all[1])

    order = [int(format(p, "0%db" % bits)[::-1], 2) for p in range(dp_count)]
    block_at = jnp.array(order, jnp.int32) ^ dp_at

    def row_blocks(array):
        turned = jnp.transpose(array).reshape(dp_count, width // dp_count, rows)
        return jnp.take(turned, block_at, axis=0).reshape(width, rows)

    def reduce_grad(left_t, right_side, y_first):
        half = width // 2
        far = core_swap(dot_f32(left_t[half:], right_side).astype(BF16))
        total = (dot_f32(left_t[:half], right_side) + far.astype(F32)).astype(BF16)
        columns = right_side.shape[1] // 2

        def y_step(total):
            received = across(total[:, columns:])
            return (total[:, :columns].astype(F32) + received.astype(F32)).astype(BF16)

        if y_first:
            total = y_step(total)
        for bit in range(1, bits):
            half = total.shape[0] // 2
            received = flip(bit)(total[half:])
            total = (total[:half].astype(F32) + received.astype(F32)).astype(BF16)
        if not y_first:
            total = y_step(total)
        return total.astype(F32)

    def halves_first(arrays):
        cut = arrays[0].shape[1] // 2
        return jnp.concatenate([a[:, :cut] for a in arrays] + [a[:, cut:] for a in arrays], axis=1)

    gate_up_sum = reduce_grad(row_blocks(normed_f), halves_first([d_gate, d_up]), True)
    down_sum = reduce_grad(row_blocks(d_ffn), hidden, False)

    d_middle = dout + norm_backward(d_normed_f * (1.0 + scale_f), m_hat, m_inverse)
    d_attn = (valid * gate_a * d_middle).astype(BF16)
    d_attended = dot_nt(d_attn, out_all).astype(BF16).reshape(rows, heads, head_width)
    out_sum = reduce_grad(row_blocks(d_attn), attended, False)
    probs_wide = probs.astype(F32)
    d_probs = jnp.einsum("qhd,khd->hqk", d_attended, values, preferred_element_type=F32)
    row_dot = jnp.sum(probs_wide * d_probs, axis=-1, keepdims=True)
    d_scores = (probs_wide * (d_probs - row_dot)).astype(BF16)
    d_values = jnp.einsum("hqk,qhd->khd", probs, d_attended, preferred_element_type=F32)
    d_queries = score_scale * jnp.einsum(
        "hqk,khd->qhd", d_scores, keys, preferred_element_type=F32
    )
    d_keys = score_scale * jnp.einsum(
        "hqk,qhd->khd", d_scores, queries, preferred_element_type=F32
    )
    d_pair_query = jnp.einsum("hqk,kc->qhc", d_scores, right_all, preferred_element_type=F32)
    d_right = jnp.einsum("hqk,qhc->kc", d_scores, pair_query, preferred_element_type=F32)
    d_keyed = jnp.concatenate(
        [d_keys.reshape(-1, width), d_values.reshape(-1, width), d_right], axis=1
    )
    d_keyed = d_keyed[:rows] + core_swap(d_keyed[rows:].astype(BF16)).astype(F32)
    d_keyed = d_keyed.astype(BF16)
    d_proj = [
        d_queries.reshape(rows, width).astype(BF16),
        d_keyed[:, :width],
        d_keyed[:, width : 2 * width],
    ]
    d_left = jnp.sum(d_pair_query * jnp.transpose(pair_mix)[None], axis=1).astype(BF16)
    d_pair = turn(jnp.concatenate([d_left, d_keyed[:, 2 * width :]], axis=1))
    d_pair_weight = jnp.einsum(
        "thc,tc->ch", d_pair_query, left_own.astype(F32), precision=lax.Precision.HIGHEST
    )
    d_pair_weight = jnp.concatenate(
        [d_pair_weight[:, :half_heads], across(d_pair_weight[:, half_heads:])], axis=1
    )
    d_pair_weight = d_pair_weight[:, :half_heads] + d_pair_weight[:, half_heads:]
    pair_sum = lax.psum_scatter(d_pair_weight, "dp", scatter_dimension=0, tiled=True)
    d_normed_a = (
        dot_nt(d_proj[0], qkv_all[0]) + dot_nt(d_proj[1], qkv_all[1]) + dot_nt(d_proj[2], qkv_all[2])
    )
    qkv_sum = reduce_grad(row_blocks(normed_a), halves_first(d_proj), True)
    token_gradient = turn(
        (d_middle + norm_backward(d_normed_a * (1.0 + scale_a), x_hat, x_inverse)).astype(BF16)
    )

    d_token_mod = jnp.concatenate(
        [
            d_normed_a,
            d_normed_a * x_hat,
            valid * d_middle * attn_branch,
            d_normed_f,
            d_normed_f * m_hat,
            valid * dout * ffn_branch,
        ],
        axis=1,
    ).astype(BF16)
    d_chain_mod = dot_f32(jnp.transpose(member_low), d_token_mod)
    d_chain_mod = d_chain_mod + core_swap(d_chain_mod)
    arch_low = (
        arches[:, None] == jnp.arange(cath_table.shape[0], dtype=jnp.int32)[None, :]
    ).astype(BF16)
    gathered = jnp.concatenate(
        [d_chain_mod.astype(BF16), cond_act, time_embed, cond_slope.astype(BF16), arch_low], axis=1
    )
    gathered = jnp.concatenate([gathered, across(gathered)], axis=0)
    for bit in range(1, bits):
        gathered = jnp.concatenate([gathered, flip(bit)(gathered)], axis=0)
    modded = mod_weight.shape[1]
    cuts = [modded, modded + cond_width, modded + 2 * cond_width, modded + 3 * cond_width]
    d_all, cond_all, time_all, slope_all, arch_all = jnp.split(gathered, cuts, axis=1)
    mod_bias_sum = jnp.sum(d_all.astype(F32), axis=0)
    mod_weight_sum = dot_f32(jnp.transpose(cond_all), d_all)
    d_cond_pre = dot_nt(d_all, mod_weight) * slope_all.astype(F32)
    time_sum = highest_dot(jnp.transpose(time_all.astype(F32)), d_cond_pre)
    cath_sum = highest_dot(jnp.transpose(arch_all.astype(F32)), d_cond_pre)

    hidden_half = down_weight.shape[0]
    proj_half = qkv_weight.shape[2]
    return (
        mixed,
        token_gradient,
        d_pair[:, : pair_left.shape[1]],
        d_pair[:, pair_left.shape[1] :],
        cath_sum,
        time_sum,
        mod_weight_sum,
        mod_bias_sum,
        jnp.stack([qkv_sum[:, k * proj_half : (k + 1) * proj_half] for k in range(3)]),
        pair_sum,
        jnp.transpose(out_sum),
        jnp.stack([gate_up_sum[:, k * hidden_half : (k + 1) * hidden_half] for k in range(2)]),
        jnp.transpose(down_sum),
    )


def solution(mesh):
    by_rows = P(AXES, None)
    placed = (
        by_rows,
        by_rows,
        by_rows,
        P("dp", None),
        P("dp", None),
        P("dp", None),
        P(),
        P(),
        P(),
        P(),
        P(None, None, "mp"),
        P(None, "mp"),
        P("mp", None),
        P(None, None, "mp"),
        P("mp", None),
        by_rows,
    )
    return jax.shard_map(
        shards,
        mesh=mesh,
        in_specs=placed,
        out_specs=(
            by_rows,
            by_rows,
            by_rows,
            by_rows,
            P(),
            P(),
            P(),
            P(),
            P(None, "dp", "mp"),
            P("dp", "mp"),
            P("mp", "dp"),
            P(None, "dp", "mp"),
            P("mp", "dp"),
        ),
        check_vma=False,
    )
```

```python
import math

import jax
import jax.numpy as jnp
from jax import lax
from jax.experimental import pallas as pl
from jax.experimental.pallas import tpu as pltpu
from jax.sharding import PartitionSpec as P

EPSILON = 1e-06
AXES = ("dp", "mp")
BF16 = jnp.bfloat16
F32 = jnp.float32
VMEM_LIMIT = 48 * 1024 * 1024


def apply_norm(values):
    centered = values - jnp.mean(values, axis=-1, keepdims=True)
    inverse = lax.rsqrt(jnp.mean(centered * centered, axis=-1, keepdims=True) + EPSILON)
    return (centered * inverse, inverse)


def norm_backward(d_hat, x_hat, inverse):
    return inverse * (
        d_hat
        - jnp.mean(d_hat, axis=-1, keepdims=True)
        - x_hat * jnp.mean(d_hat * x_hat, axis=-1, keepdims=True)
    )


def highest_dot(left_side, right_side):
    return jnp.dot(left_side, right_side, precision=lax.Precision.HIGHEST)


def silu_parts(values):
    sigma = jax.nn.sigmoid(values)
    return (values * sigma, sigma * (1.0 + values * (1.0 - sigma)))


def dot_f32(left_side, right_side):
    return jnp.dot(left_side, right_side, preferred_element_type=F32)


def dot_nt(left_side, right_side):
    return lax.dot_general(
        left_side, right_side, (((1,), (1,)), ((), ())), preferred_element_type=F32
    )

def lane_mix(first, second, odd):
    lane = lax.broadcasted_iota(jnp.int32, first.shape, 1)
    keep = (lane >= 64) if odd else (lane < 64)
    return jnp.where(keep, first, second)


def nt(left_side, right_side):
    return lax.dot_general(
        left_side, right_side, (((1,), (1,)), ((), ())), preferred_element_type=F32
    )


def attention_forward_body(
    pair_mix_ref, q_ref, left_ref, hot_ref, k_own_ref, k_near_ref, v_own_ref, v_near_ref,
    right_own_ref, right_near_ref, pen_own_ref, pen_near_ref,
    attended_ref, inverse_ref, probs_ref,
):
    rows = q_ref.shape[0]
    step = 256
    out_tiles = []
    left = left_ref[...].astype(F32)
    for odd in range(2):
        mix = pair_mix_ref[0, odd : odd + 1, :]
        left_mixed = (left * mix).astype(BF16)
        q_side = jnp.concatenate([left_mixed, lane_mix(q_ref[...], hot_ref[...], odd)], axis=1)
        k_own = jnp.concatenate(
            [right_own_ref[...], lane_mix(k_own_ref[...], pen_own_ref[...], odd)], axis=1
        )
        k_near = jnp.concatenate(
            [right_near_ref[...], lane_mix(k_near_ref[...], pen_near_ref[...], odd)], axis=1
        )
        v_own = lane_mix(v_own_ref[...], jnp.ones_like(v_own_ref[...]), odd)
        v_near = lane_mix(v_near_ref[...], jnp.ones_like(v_near_ref[...]), odd)
        tiles = []
        for start in range(0, rows, step):
            block = q_side[start : start + step]
            s_own = nt(block, k_own)
            s_near = nt(block, k_near)
            top = jnp.maximum(
                jnp.max(s_own, axis=1, keepdims=True), jnp.max(s_near, axis=1, keepdims=True)
            )
            e_own = jnp.exp(s_own - top).astype(BF16)
            e_near = jnp.exp(s_near - top).astype(BF16)
            probs_ref[odd, start : start + step, :rows] = e_own
            probs_ref[odd, start : start + step, rows:] = e_near
            tiles.append(
                jnp.dot(e_own, v_own, preferred_element_type=F32)
                + jnp.dot(e_near, v_near, preferred_element_type=F32)
            )
        out_tiles.append(jnp.concatenate(tiles, axis=0))
    sums = lane_mix(out_tiles[1], out_tiles[0], False)
    sums = pltpu.roll(sums, 64, 1)
    inverse = 1.0 / sums
    attended_ref[...] = (lane_mix(out_tiles[0], out_tiles[1], False) * inverse).astype(BF16)
    inverse_ref[...] = inverse


def attention_backward_body(
    pair_mix_ref, grad_ref, attended_ref, inverse_ref, probs_ref, q_ref, left_ref, left_t_ref,
    k_own_ref, k_near_ref, v_own_ref, v_near_ref, right_own_ref, right_near_ref,
    pen_own_ref, pen_near_ref,
    d_q_ref, d_k_ref, d_v_ref, d_right_ref, d_left_ref, d_mix_ref,
    scores_ref, right_sum_ref, left_sum_ref,
):
    pair = pl.program_id(0)
    rows = q_ref.shape[0]
    step = 256

    @pl.when(pair == 0)
    def _():
        right_sum_ref[...] = jnp.zeros_like(right_sum_ref)
        left_sum_ref[...] = jnp.zeros_like(left_sum_ref)

    scaled = (grad_ref[...].astype(F32) * inverse_ref[...]).astype(BF16)
    products = scaled.astype(F32) * attended_ref[...].astype(F32)
    scaled_t = scaled.T
    q_t = q_ref[...].T
    lane = lax.broadcasted_iota(jnp.int32, products.shape, 1)
    left = left_ref[...].astype(F32)
    left_t = left_t_ref[...].astype(F32)
    d_q, dk_t, dv_t = [], [], []
    for odd in range(2):
        mine = (lane >= 64) if odd else (lane < 64)
        delta = -jnp.sum(jnp.where(mine, products, 0.0), axis=1, keepdims=True)
        high = delta.astype(BF16).astype(F32)
        low = delta - high
        first = 0 if odd else 64
        extra = jnp.where(lane == first, high, jnp.where(lane == first + 1, low, 0.0)).astype(BF16)
        grad_side = jnp.where(mine, scaled, extra)
        mix = pair_mix_ref[0, odd : odd + 1, :]
        k_own = jnp.concatenate(
            [right_own_ref[...], lane_mix(k_own_ref[...], pen_own_ref[...], odd)], axis=1
        )
        k_near = jnp.concatenate(
            [right_near_ref[...], lane_mix(k_near_ref[...], pen_near_ref[...], odd)], axis=1
        )
        v_own = lane_mix(v_own_ref[...], jnp.ones_like(v_own_ref[...]), odd)
        v_near = lane_mix(v_near_ref[...], jnp.ones_like(v_near_ref[...]), odd)
        for start in range(0, rows, step):
            block = grad_side[start : start + step]
            own = nt(block, v_own).astype(BF16) * probs_ref[odd, start : start + step, :rows]
            near = nt(block, v_near).astype(BF16) * probs_ref[odd, start : start + step, rows:]
            scores_ref[start : start + step, :rows] = own
            scores_ref[start : start + step, rows:] = near
        d_query = jnp.dot(
            scores_ref[:, :rows], k_own, preferred_element_type=F32
        ) + jnp.dot(scores_ref[:, rows:], k_near, preferred_element_type=F32)
        width = left.shape[1]
        d_q.append(d_query[:, width:])
        d_pair = d_query[:, :width]
        left_sum_ref[...] += d_pair * mix
        d_mix_ref[0, odd : odd + 1, :] = jnp.sum(d_pair * left, axis=0, keepdims=True)
        mixed_t = (left_t * jnp.transpose(mix)).astype(BF16)
        low_row = 64 * odd
        q_side = jnp.concatenate([mixed_t, q_t[low_row : low_row + 64]], axis=0)
        d_key = jnp.dot(q_side, scores_ref[...], preferred_element_type=F32)
        right_sum_ref[...] += d_key[:width]
        dk_t.append(d_key[width:])
        dv_t.append(
            jnp.dot(
                scaled_t[low_row : low_row + 64], probs_ref[odd], preferred_element_type=F32
            )
        )
    d_q_ref[...] = (lane_mix(d_q[0], d_q[1], False) * 0.125).astype(BF16)
    d_k_ref[...] = jnp.concatenate(dk_t, axis=0).T.astype(BF16)
    d_v_ref[...] = jnp.concatenate(dv_t, axis=0).T.astype(BF16)

    @pl.when(pair == pl.num_programs(0) - 1)
    def _():
        d_right_ref[...] = right_sum_ref[...].T.astype(BF16)
        d_left_ref[...] = left_sum_ref[...].astype(BF16)


def whole(array):
    zeros = (0,) * array.ndim
    return pl.BlockSpec(array.shape, lambda *_: zeros)


def attention_forward(pair_mix, queries, left, hot, kvr_own, kvr_near, pen_own, pen_near):
    rows, width = queries.shape
    pairs = width // 128
    pair_width = left.shape[1]
    column = pl.BlockSpec((rows, 128), lambda p: (0, p))
    value_column = pl.BlockSpec((rows, 128), lambda p: (0, pairs + p))
    right = pl.BlockSpec((rows, pair_width), lambda p: (0, 2 * width // pair_width))
    flops = 2 * 2 * pairs * rows * 2 * rows * 512
    return pl.pallas_call(
        attention_forward_body,
        grid=(pairs,),
        in_specs=[
            pl.BlockSpec((1, 2, pair_width), lambda p: (p, 0, 0)),
            column,
            whole(left),
            whole(hot),
            column,
            column,
            value_column,
            value_column,
            right,
            right,
            whole(pen_own),
            whole(pen_near),
        ],
        out_specs=[column, column, pl.BlockSpec((2, rows, 2 * rows), lambda p: (p, 0, 0))],
        out_shape=[
            jax.ShapeDtypeStruct((rows, width), BF16),
            jax.ShapeDtypeStruct((rows, width), F32),
            jax.ShapeDtypeStruct((2 * pairs, rows, 2 * rows), BF16),
        ],
        compiler_params=pltpu.CompilerParams(vmem_limit_bytes=VMEM_LIMIT),
        cost_estimate=pl.CostEstimate(
            flops=flops, bytes_accessed=4 * pairs * rows * rows * 2, transcendentals=0
        ),
        name="attention_forward",
    )(
        pair_mix, queries, left, hot, kvr_own, kvr_near, kvr_own, kvr_near, kvr_own, kvr_near,
        pen_own, pen_near,
    )


def attention_backward(
    pair_mix, grad, attended, inverse, probs, queries, left, kvr_own, kvr_near, pen_own, pen_near
):
    rows, width = queries.shape
    pairs = width // 128
    pair_width = left.shape[1]
    left_t = jnp.transpose(left)
    column = pl.BlockSpec((rows, 128), lambda p: (0, p))
    value_column = pl.BlockSpec((rows, 128), lambda p: (0, pairs + p))
    right = pl.BlockSpec((rows, pair_width), lambda p: (0, 2 * width // pair_width))
    key_column = pl.BlockSpec((2 * rows, 128), lambda p: (0, p))
    mix = pl.BlockSpec((1, 2, pair_width), lambda p: (p, 0, 0))
    flops = 2 * 2 * pairs * rows * 2 * rows * 1000
    return pl.pallas_call(
        attention_backward_body,
        grid=(pairs,),
        in_specs=[
            mix,
            column,
            column,
            column,
            pl.BlockSpec((2, rows, 2 * rows), lambda p: (p, 0, 0)),
            column,
            whole(left),
            whole(left_t),
            column,
            column,
            value_column,
            value_column,
            right,
            right,
            whole(pen_own),
            whole(pen_near),
        ],
        out_specs=[
            column,
            key_column,
            key_column,
            pl.BlockSpec((2 * rows, pair_width), lambda p: (0, 0)),
            pl.BlockSpec((rows, pair_width), lambda p: (0, 0)),
            mix,
        ],
        out_shape=[
            jax.ShapeDtypeStruct((rows, width), BF16),
            jax.ShapeDtypeStruct((2 * rows, width), BF16),
            jax.ShapeDtypeStruct((2 * rows, width), BF16),
            jax.ShapeDtypeStruct((2 * rows, pair_width), BF16),
            jax.ShapeDtypeStruct((rows, pair_width), BF16),
            jax.ShapeDtypeStruct((pairs, 2, pair_width), F32),
        ],
        scratch_shapes=[
            pltpu.VMEM((rows, 2 * rows), BF16),
            pltpu.VMEM((pair_width, 2 * rows), F32),
            pltpu.VMEM((rows, pair_width), F32),
        ],
        compiler_params=pltpu.CompilerParams(vmem_limit_bytes=VMEM_LIMIT),
        cost_estimate=pl.CostEstimate(
            flops=flops, bytes_accessed=4 * pairs * rows * rows * 2, transcendentals=0
        ),
        name="attention_backward",
    )(
        pair_mix, grad, attended, inverse, probs, queries, left, left_t, kvr_own, kvr_near,
        kvr_own, kvr_near, kvr_own, kvr_near, pen_own, pen_near,
    )


def make_moves(dp_count):
    def pairs(target):
        moved = []
        for d in range(dp_count):
            for m in range(2):
                to_d, to_m = target(d, m)
                moved.append((d * 2 + m, to_d * 2 + to_m))
        return moved

    def mover(target):
        table = pairs(target)
        return lambda array: lax.ppermute(array, AXES, table)

    turn = mover(lambda d, m: ((d & ~1) | m, d & 1))
    across = mover(lambda d, m: (d, 1 - m))

    def flip(bit):
        return mover(lambda d, m: (d ^ (1 << bit), m))

    return turn, across, flip


def shards(
    tokens,
    pair_left,
    pair_right,
    chain_len,
    chain_time,
    chain_arch,
    cath_table,
    time_weight,
    mod_weight,
    mod_bias,
    qkv_weight,
    pair_weight,
    out_weight,
    gate_up_weight,
    down_weight,
    cotangent,
):
    dp_count = lax.axis_size("dp")
    bits = dp_count.bit_length() - 1
    turn, across, flip = make_moves(dp_count)
    core_swap = flip(0)
    dp_at = lax.axis_index("dp")
    mp_at = lax.axis_index("mp")
    core = dp_at & 1
    rows, width = tokens.shape
    slots = chain_len.shape[1]
    half_heads = pair_weight.shape[1]
    heads = 2 * half_heads
    head_width = qkv_weight.shape[2] // half_heads
    cond_width = time_weight.shape[0]
    score_scale = head_width ** (-0.5)

    held_chains = jnp.concatenate(
        [chain_len.astype(F32), chain_time, chain_arch.astype(F32)], axis=0
    )
    near_chains = core_swap(held_chains)
    chains = jnp.where(core == mp_at, held_chains, near_chains)
    lengths = chains[0].astype(jnp.int32)
    times = chains[1]
    arches = chains[2].astype(jnp.int32)
    ends = jnp.cumsum(lengths)

    def ids_of(half):
        positions = jnp.arange(rows, dtype=jnp.int32) + half * rows
        return jnp.sum((positions[:, None] >= ends[None, :]).astype(jnp.int32), axis=1)

    own_ids = ids_of(core)
    key_ids = jnp.concatenate([own_ids, ids_of(1 - core)])
    membership = own_ids[:, None] == jnp.arange(slots, dtype=jnp.int32)[None, :]
    member_low = membership.astype(BF16)
    membership = membership.astype(F32)
    valid = (own_ids < slots).astype(F32)[:, None]

    half_cond = cond_width // 2
    frequency = jnp.exp(jnp.arange(half_cond, dtype=F32) * (-math.log(10000.0) / half_cond))
    angles = times[:, None] * 1000.0 * frequency[None, :]
    time_embed = jnp.concatenate([jnp.sin(angles), jnp.cos(angles)], axis=1).astype(BF16)
    arch_onehot = (
        arches[:, None] == jnp.arange(cath_table.shape[0], dtype=jnp.int32)[None, :]
    ).astype(F32)
    cond_pre = dot_f32(time_embed, time_weight) + highest_dot(arch_onehot, cath_table.astype(F32))
    cond_value, cond_slope = silu_parts(cond_pre)
    cond_act = cond_value.astype(BF16)
    chain_mod = dot_f32(cond_act, mod_weight) + mod_bias.astype(F32)[None, :]
    token_mod = highest_dot(membership, chain_mod)
    shift_a, scale_a, gate_a, shift_f, scale_f, gate_f = jnp.split(token_mod, 6, axis=1)

    layer_in = turn(tokens).astype(F32)
    pair_own = turn(jnp.concatenate([pair_left, pair_right], axis=1))
    left_own, right_own = jnp.split(pair_own, 2, axis=1)
    dout = turn(cotangent).astype(F32)

    def other_half(weight, axis):
        size = weight.shape[axis] // 2
        piece = lax.dynamic_slice_in_dim(weight, core * size, size, axis)
        mine = across(piece)
        near = core_swap(mine)
        return jnp.where(
            core == 0,
            jnp.concatenate([mine, near], axis=axis),
            jnp.concatenate([near, mine], axis=axis),
        )

    qkv_all = jnp.concatenate([qkv_weight, other_half(qkv_weight, 2)], axis=2)
    pair_mix = jnp.concatenate([pair_weight, across(pair_weight)], axis=1).astype(F32)
    out_all = jnp.concatenate([out_weight, other_half(out_weight, 0)], axis=0)
    gate_up_all = jnp.concatenate([gate_up_weight, other_half(gate_up_weight, 2)], axis=2)
    down_all = jnp.concatenate([down_weight, other_half(down_weight, 0)], axis=0)

    x_hat, x_inverse = apply_norm(layer_in)
    normed_a = (x_hat * (1.0 + scale_a) + shift_a).astype(BF16)
    projected = jnp.einsum("td,kdf->ktf", normed_a, qkv_all, preferred_element_type=F32).astype(
        BF16
    )
    kvr_own = jnp.concatenate([projected[1], projected[2], right_own], axis=1)
    kvr_near = core_swap(kvr_own)
    queries = (projected[0].astype(F32) * score_scale).astype(BF16)
    mix_rows = jnp.transpose(pair_mix).reshape(half_heads, 2, -1)
    lanes = jnp.arange(128, dtype=jnp.int32)[None, :] & 63
    hot = (own_ids[:, None] == lanes).astype(BF16)
    pens = jnp.where((key_ids[:, None] != lanes) & (lanes <= slots), -1e30, 0.0).astype(BF16)
    pen_own, pen_near = pens[:rows], pens[rows:]
    attended, inverse, probs = attention_forward(
        mix_rows, queries, left_own, hot, kvr_own, kvr_near, pen_own, pen_near
    )
    attn_branch = dot_f32(attended, out_all)
    middle = layer_in + valid * gate_a * attn_branch

    m_hat, m_inverse = apply_norm(middle)
    normed_f = (m_hat * (1.0 + scale_f) + shift_f).astype(BF16)
    d_ffn = (valid * gate_f * dout).astype(BF16)
    gate_act = dot_f32(normed_f, gate_up_all[0])
    up_act = dot_f32(normed_f, gate_up_all[1])
    gate_value, gate_slope = silu_parts(gate_act)
    hidden = (gate_value * up_act).astype(BF16)
    ffn_branch = dot_f32(hidden, down_all)
    mixed = turn((middle + valid * gate_f * ffn_branch).astype(BF16))
    d_hidden = dot_nt(d_ffn, down_all)
    d_gate = (d_hidden * up_act * gate_slope).astype(BF16)
    d_up = (d_hidden * gate_value).astype(BF16)
    d_normed_f = dot_nt(d_gate, gate_up_all[0]) + dot_nt(d_up, gate_up_all[1])

    order = [int(format(p, "0%db" % bits)[::-1], 2) for p in range(dp_count)]
    block_at = jnp.array(order, jnp.int32) ^ dp_at

    def row_blocks(array):
        turned = jnp.transpose(array).reshape(dp_count, width // dp_count, rows)
        return jnp.take(turned, block_at, axis=0).reshape(width, rows)

    def reduce_grad(left_t, right_side, y_first):
        half = width // 2
        far = core_swap(dot_f32(left_t[half:], right_side).astype(BF16))
        total = (dot_f32(left_t[:half], right_side) + far.astype(F32)).astype(BF16)
        columns = right_side.shape[1] // 2

        def y_step(total):
            received = across(total[:, columns:])
            return (total[:, :columns].astype(F32) + received.astype(F32)).astype(BF16)

        if y_first:
            total = y_step(total)
        for bit in range(1, bits):
            half = total.shape[0] // 2
            received = flip(bit)(total[half:])
            total = (total[:half].astype(F32) + received.astype(F32)).astype(BF16)
        if not y_first:
            total = y_step(total)
        return total.astype(F32)

    def halves_first(arrays):
        cut = arrays[0].shape[1] // 2
        return jnp.concatenate([a[:, :cut] for a in arrays] + [a[:, cut:] for a in arrays], axis=1)

    gate_up_sum = reduce_grad(row_blocks(normed_f), halves_first([d_gate, d_up]), True)
    down_sum = reduce_grad(row_blocks(d_ffn), hidden, False)

    d_middle = dout + norm_backward(d_normed_f * (1.0 + scale_f), m_hat, m_inverse)
    d_attn = (valid * gate_a * d_middle).astype(BF16)
    d_attended = dot_nt(d_attn, out_all).astype(BF16)
    out_sum = reduce_grad(row_blocks(d_attn), attended, False)
    d_query, d_keys, d_values, d_right, d_left, d_mix = attention_backward(
        mix_rows, d_attended, attended, inverse, probs, queries, left_own, kvr_own, kvr_near,
        pen_own, pen_near,
    )
    d_keyed = jnp.concatenate([d_keys, d_values, d_right], axis=1)
    d_keyed = (
        d_keyed[:rows].astype(F32) + core_swap(d_keyed[rows:]).astype(F32)
    ).astype(BF16)
    d_proj = [d_query, d_keyed[:, :width], d_keyed[:, width : 2 * width]]
    d_pair = turn(jnp.concatenate([d_left, d_keyed[:, 2 * width :]], axis=1))
    d_mix = d_mix.reshape(heads, -1)
    d_normed_a = (
        dot_nt(d_proj[0], qkv_all[0]) + dot_nt(d_proj[1], qkv_all[1]) + dot_nt(d_proj[2], qkv_all[2])
    )
    qkv_sum = reduce_grad(row_blocks(normed_a), halves_first(d_proj), True)
    token_gradient = turn(
        (d_middle + norm_backward(d_normed_a * (1.0 + scale_a), x_hat, x_inverse)).astype(BF16)
    )

    d_token_mod = jnp.concatenate(
        [
            d_normed_a,
            d_normed_a * x_hat,
            valid * d_middle * attn_branch,
            d_normed_f,
            d_normed_f * m_hat,
            valid * dout * ffn_branch,
        ],
        axis=1,
    ).astype(BF16)
    d_chain_mod = dot_f32(jnp.transpose(member_low), d_token_mod)
    modded = mod_weight.shape[1]
    d_mix_own = jnp.concatenate(
        [jnp.where(mp_at == 0, d_mix[:half_heads], d_mix[half_heads:]),
         jnp.where(mp_at == 0, d_mix[half_heads:], d_mix[:half_heads])], axis=0
    )
    d_mix_own = d_mix_own.reshape(slots, -1)
    summed = jnp.concatenate([d_chain_mod, d_mix_own], axis=1)
    summed = summed + core_swap(summed)
    arch_low = (
        arches[:, None] == jnp.arange(cath_table.shape[0], dtype=jnp.int32)[None, :]
    ).astype(BF16)
    gathered = jnp.concatenate(
        [summed.astype(BF16), cond_act, time_embed, cond_slope.astype(BF16), arch_low], axis=1
    )
    gathered = jnp.concatenate([gathered, across(gathered)], axis=0)
    for bit in range(1, bits):
        gathered = jnp.concatenate([gathered, flip(bit)(gathered)], axis=0)
    mixed_to = modded + d_mix_own.shape[1]
    cuts = [modded, mixed_to, mixed_to + cond_width, mixed_to + 2 * cond_width, mixed_to + 3 * cond_width]
    d_all, mix_all, cond_all, time_all, slope_all, arch_all = jnp.split(gathered, cuts, axis=1)
    mix_sum = jnp.sum(mix_all.astype(F32).reshape(dp_count, heads, -1), axis=0)
    mix_sum = jnp.where(mp_at == 0, mix_sum[:half_heads], mix_sum[half_heads:])
    taken = mix_sum.shape[1] // dp_count
    pair_sum = jnp.transpose(lax.dynamic_slice_in_dim(mix_sum, dp_at * taken, taken, 1))
    mod_bias_sum = jnp.sum(d_all.astype(F32), axis=0)
    mod_weight_sum = dot_f32(jnp.transpose(cond_all), d_all)
    d_cond_pre = dot_nt(d_all, mod_weight) * slope_all.astype(F32)
    time_sum = highest_dot(jnp.transpose(time_all.astype(F32)), d_cond_pre)
    cath_sum = highest_dot(jnp.transpose(arch_all.astype(F32)), d_cond_pre)

    hidden_half = down_weight.shape[0]
    proj_half = qkv_weight.shape[2]
    return (
        mixed,
        token_gradient,
        d_pair[:, : pair_left.shape[1]],
        d_pair[:, pair_left.shape[1] :],
        cath_sum,
        time_sum,
        mod_weight_sum,
        mod_bias_sum,
        jnp.stack([qkv_sum[:, k * proj_half : (k + 1) * proj_half] for k in range(3)]),
        pair_sum,
        jnp.transpose(out_sum),
        jnp.stack([gate_up_sum[:, k * hidden_half : (k + 1) * hidden_half] for k in range(2)]),
        jnp.transpose(down_sum),
    )


def solution(mesh):
    by_rows = P(AXES, None)
    placed = (
        by_rows,
        by_rows,
        by_rows,
        P("dp", None),
        P("dp", None),
        P("dp", None),
        P(),
        P(),
        P(),
        P(),
        P(None, None, "mp"),
        P(None, "mp"),
        P("mp", None),
        P(None, None, "mp"),
        P("mp", None),
        by_rows,
    )
    return jax.shard_map(
        shards,
        mesh=mesh,
        in_specs=placed,
        out_specs=(
            by_rows,
            by_rows,
            by_rows,
            by_rows,
            P(),
            P(),
            P(),
            P(),
            P(None, "dp", "mp"),
            P("dp", "mp"),
            P("mp", "dp"),
            P(None, "dp", "mp"),
            P("mp", "dp"),
        ),
        check_vma=False,
    )
```

```python
import functools
import math

import jax
import jax.numpy as jnp
from jax import lax
from jax.experimental import pallas as pl
from jax.experimental.pallas import tpu as pltpu
from jax.sharding import PartitionSpec as P

EPSILON = 1e-06
AXES = ("dp", "mp")
BF16 = jnp.bfloat16
F32 = jnp.float32
VMEM_LIMIT = 60 * 1024 * 1024
FFN_BLOCK = 384
BACK_PARTS = 1
COST_CUT = 20


def highest_dot(left_side, right_side):
    return jnp.dot(left_side, right_side, precision=lax.Precision.HIGHEST)


def silu_parts(values):
    sigma = jax.nn.sigmoid(values)
    return (values * sigma, sigma * (1.0 + values * (1.0 - sigma)))


def dot_f32(left_side, right_side):
    return jnp.dot(left_side, right_side, preferred_element_type=F32)


def dot_nt(left_side, right_side):
    return lax.dot_general(
        left_side, right_side, (((1,), (1,)), ((), ())), preferred_element_type=F32
    )

def lane_mix(first, second, odd):
    lane = lax.broadcasted_iota(jnp.int32, first.shape, 1)
    keep = (lane >= 64) if odd else (lane < 64)
    return jnp.where(keep, first, second)


def nt(left_side, right_side):
    return lax.dot_general(
        left_side, right_side, (((1,), (1,)), ((), ())), preferred_element_type=F32
    )


def attention_forward_body(
    pair_mix_ref, q_ref, left_ref, hot_ref, k_own_ref, k_near_ref, v_own_ref, v_near_ref,
    right_own_ref, right_near_ref, pen_own_ref, pen_near_ref,
    attended_ref, inverse_ref, probs_ref,
):
    rows = q_ref.shape[0]
    step = 256
    out_tiles = []
    left = left_ref[...].astype(F32)
    for odd in range(2):
        mix = pair_mix_ref[0, odd : odd + 1, :]
        left_mixed = (left * mix).astype(BF16)
        q_side = jnp.concatenate([left_mixed, lane_mix(q_ref[...], hot_ref[...], odd)], axis=1)
        k_own = jnp.concatenate(
            [right_own_ref[...], lane_mix(k_own_ref[...], pen_own_ref[...], odd)], axis=1
        )
        k_near = jnp.concatenate(
            [right_near_ref[...], lane_mix(k_near_ref[...], pen_near_ref[...], odd)], axis=1
        )
        v_own = lane_mix(v_own_ref[...], jnp.ones_like(v_own_ref[...]), odd)
        v_near = lane_mix(v_near_ref[...], jnp.ones_like(v_near_ref[...]), odd)
        tiles = []
        for start in range(0, rows, step):
            block = q_side[start : start + step]
            s_own = nt(block, k_own)
            s_near = nt(block, k_near)
            top = jnp.maximum(
                jnp.max(s_own, axis=1, keepdims=True), jnp.max(s_near, axis=1, keepdims=True)
            )
            e_own = jnp.exp(s_own - top).astype(BF16)
            e_near = jnp.exp(s_near - top).astype(BF16)
            probs_ref[odd, start : start + step, :rows] = e_own
            probs_ref[odd, start : start + step, rows:] = e_near
            tiles.append(
                jnp.dot(e_own, v_own, preferred_element_type=F32)
                + jnp.dot(e_near, v_near, preferred_element_type=F32)
            )
        out_tiles.append(jnp.concatenate(tiles, axis=0))
    sums = lane_mix(out_tiles[1], out_tiles[0], False)
    sums = pltpu.roll(sums, 64, 1)
    inverse = 1.0 / sums
    attended_ref[...] = (lane_mix(out_tiles[0], out_tiles[1], False) * inverse).astype(BF16)
    inverse_ref[...] = inverse


def attention_backward_body(
    first, last, pair_mix_ref, grad_ref, attended_ref, inverse_ref, probs_ref, q_ref, left_ref,
    k_own_ref, k_near_ref, v_own_ref, v_near_ref, right_own_ref, right_near_ref,
    pen_own_ref, pen_near_ref, *rest
):
    if not first:
        right_start, left_start = rest[:2]
        rest = rest[2:]
    d_q_ref, own_out, near_out, right_out, left_out, d_mix_ref = rest[:6]
    scores_ref, right_sum_ref, left_sum_ref, left_t_ref = rest[-4:]
    pair = pl.program_id(0)
    rows = q_ref.shape[0]
    step = 256
    wide = own_out.shape[1] // 2

    @pl.when(pair == 0)
    def _():
        left_t_ref[...] = left_ref[...].T
        right_sum_ref[...] = jnp.zeros_like(right_sum_ref) if first else right_start[...]
        left_sum_ref[...] = jnp.zeros_like(left_sum_ref) if first else left_start[...]

    scaled = (grad_ref[...].astype(F32) * inverse_ref[...]).astype(BF16)
    products = scaled.astype(F32) * attended_ref[...].astype(F32)
    scaled_t = scaled.T
    q_t = q_ref[...].T
    lane = lax.broadcasted_iota(jnp.int32, products.shape, 1)
    left = left_ref[...].astype(F32)
    left_t = left_t_ref[...].astype(F32)
    d_q, dk_t, dv_t = [], [], []
    for odd in range(2):
        mine = (lane >= 64) if odd else (lane < 64)
        delta = -jnp.sum(jnp.where(mine, products, 0.0), axis=1, keepdims=True)
        high = delta.astype(BF16).astype(F32)
        low = delta - high
        at = 0 if odd else 64
        extra = jnp.where(lane == at, high, jnp.where(lane == at + 1, low, 0.0)).astype(BF16)
        grad_side = jnp.where(mine, scaled, extra)
        mix = pair_mix_ref[0, odd : odd + 1, :]
        k_own = jnp.concatenate(
            [right_own_ref[...], lane_mix(k_own_ref[...], pen_own_ref[...], odd)], axis=1
        )
        k_near = jnp.concatenate(
            [right_near_ref[...], lane_mix(k_near_ref[...], pen_near_ref[...], odd)], axis=1
        )
        v_own = lane_mix(v_own_ref[...], jnp.ones_like(v_own_ref[...]), odd)
        v_near = lane_mix(v_near_ref[...], jnp.ones_like(v_near_ref[...]), odd)
        for start in range(0, rows, step):
            block = grad_side[start : start + step]
            own = nt(block, v_own).astype(BF16) * probs_ref[odd, start : start + step, :rows]
            near = nt(block, v_near).astype(BF16) * probs_ref[odd, start : start + step, rows:]
            scores_ref[start : start + step, :rows] = own
            scores_ref[start : start + step, rows:] = near
        d_query = jnp.dot(
            scores_ref[:, :rows], k_own, preferred_element_type=F32
        ) + jnp.dot(scores_ref[:, rows:], k_near, preferred_element_type=F32)
        width = left.shape[1]
        d_q.append(d_query[:, width:])
        d_pair = d_query[:, :width]
        left_sum_ref[...] += d_pair * mix
        d_mix_ref[0, odd : odd + 1, :] = jnp.sum(d_pair * left, axis=0, keepdims=True)
        mixed_t = (left_t * jnp.transpose(mix)).astype(BF16)
        low_row = 64 * odd
        q_side = jnp.concatenate([mixed_t, q_t[low_row : low_row + 64]], axis=0)
        d_key = jnp.dot(q_side, scores_ref[...], preferred_element_type=F32)
        right_sum_ref[...] += d_key[:width]
        dk_t.append(d_key[width:])
        dv_t.append(
            jnp.dot(
                scaled_t[low_row : low_row + 64], probs_ref[odd], preferred_element_type=F32
            )
        )
    d_q_ref[...] = (lane_mix(d_q[0], d_q[1], False) * 0.125).astype(BF16)
    for base, parts in ((0, dk_t), (wide, dv_t)):
        both = jnp.concatenate(parts, axis=0).T.astype(BF16)
        column = pl.multiple_of(base + pair * 128, 128)
        own_out[:, pl.ds(column, 128)] = both[:rows]
        near_out[:, pl.ds(column, 128)] = both[rows:]

    @pl.when(pair == pl.num_programs(0) - 1)
    def _():
        if last:
            right_out[...] = right_sum_ref[...].T.astype(BF16)
        else:
            right_out[...] = right_sum_ref[...]
        left_out[...] = left_sum_ref[...].astype(left_out.dtype)


def whole(array):
    zeros = (0,) * array.ndim
    return pl.BlockSpec(array.shape, lambda *_: zeros)


def attention_forward(
    pair_mix, queries, left, hot, kv_own, kv_near, right_own, right_near, pen_own, pen_near
):
    rows, width = queries.shape
    pairs = width // 128
    pair_width = left.shape[1]
    column = pl.BlockSpec((rows, 128), lambda p: (0, p))
    value_column = pl.BlockSpec((rows, 128), lambda p: (0, pairs + p))
    operands = [
        pair_mix, queries, left, hot, kv_own, kv_near, kv_own, kv_near, right_own, right_near,
        pen_own, pen_near,
    ]
    return call(
        attention_forward_body,
        operands,
        [
            pl.BlockSpec((1, 2, pair_width), lambda p: (p, 0, 0)), column, whole(left), whole(hot),
            column, column, value_column, value_column, whole(right_own), whole(right_near),
            whole(pen_own), whole(pen_near),
        ],
        [
            shaped((rows, width)), shaped((rows, width), F32),
            shaped((2 * pairs, rows, 2 * rows)),
        ],
        [column, column, pl.BlockSpec((2, rows, 2 * rows), lambda p: (p, 0, 0))],
        [],
        2 * 2 * pairs * rows * 2 * rows * 512,
        "attention_forward",
        (pairs,),
    )


def attention_backward(
    part, parts, pair_mix, grad, attended, inverse, probs, queries, left, kv_own, kv_near,
    right_own, right_near, pen_own, pen_near, *starts
):
    rows, width = queries.shape
    pairs = width // 128
    here = pairs // parts
    pair_width = left.shape[1]
    first, last = part == 0, part == parts - 1
    at = lambda p: part * here + p
    column = pl.BlockSpec((rows, 128), lambda p: (0, at(p)))
    value_column = pl.BlockSpec((rows, 128), lambda p: (0, pairs + at(p)))
    own_column = pl.BlockSpec((rows, 128), lambda p: (0, p))
    mix = pl.BlockSpec((1, 2, pair_width), lambda p: (at(p), 0, 0))
    mix_out = pl.BlockSpec((1, 2, pair_width), lambda p: (p, 0, 0))
    both = shaped((rows, 2 * 128 * here))
    if last:
        sums = [shaped((2 * rows, pair_width)), shaped((rows, pair_width))]
    else:
        sums = [shaped((pair_width, 2 * rows), F32), shaped((rows, pair_width), F32)]
    operands = [
        pair_mix, grad, attended, inverse, probs, queries, left, kv_own, kv_near, kv_own,
        kv_near, right_own, right_near, pen_own, pen_near, *starts,
    ]
    return call(
        functools.partial(attention_backward_body, first, last),
        operands,
        [
            mix, column, column, column,
            pl.BlockSpec((2, rows, 2 * rows), lambda p: (at(p), 0, 0)),
            column, whole(left), column, column, value_column, value_column,
            whole(right_own), whole(right_near), whole(pen_own), whole(pen_near),
        ]
        + [whole(a) for a in starts],
        [shaped((rows, 128 * here)), both, both, *sums, shaped((here, 2, pair_width), F32)],
        [own_column, whole(both), whole(both), *[whole(a) for a in sums], mix_out],
        [
            pltpu.VMEM((rows, 2 * rows), BF16),
            pltpu.VMEM((pair_width, 2 * rows), F32),
            pltpu.VMEM((rows, pair_width), F32),
            pltpu.VMEM((pair_width, rows), BF16),
        ],
        2 * 2 * here * rows * 2 * rows * 1000,
        "attention_backward",
        (here,),
    )


def norm_parts(values):
    centered = values - jnp.mean(values, axis=-1, keepdims=True)
    inverse = lax.rsqrt(jnp.mean(centered * centered, axis=-1, keepdims=True) + EPSILON)
    return centered * inverse, inverse


def tn(left_side, right_side):
    return lax.dot_general(
        left_side, right_side, (((0,), (0,)), ((), ())), preferred_element_type=F32
    )


def fetch(pieces, target, sems, at_ref, cut):
    copies = []
    for r, piece in enumerate(pieces):
        row = pl.multiple_of((at_ref[0] ^ r) * cut, cut)
        copy = pltpu.make_async_copy(piece, target.at[..., pl.ds(row, cut), :], sems.at[r])
        copy.start()
        copies.append(copy)
    return copies


def qkv_body(at_ref, x_ref, member_ref, mod_ref, own_ref, *rest):
    pieces, (q_ref, kvr_ref, normed_ref), (other, sems) = rest[:2], rest[2:5], rest[5:]
    width = x_ref.shape[1]
    half = width // 2
    copies = fetch(pieces, other, sems, at_ref, width // 2)
    mods = jnp.dot(member_ref[...], mod_ref[...], preferred_element_type=F32)
    x_hat, _ = norm_parts(x_ref[...].astype(F32))
    normed = (x_hat * (1.0 + mods[:, width:]) + mods[:, :width]).astype(BF16)
    normed_ref[...] = normed

    def put(weights, low):
        q = jnp.dot(normed, weights[0], preferred_element_type=F32).astype(BF16)
        q_ref[:, low : low + half] = (q.astype(F32) * 0.125).astype(BF16)
        for k in (1, 2):
            first = (k - 1) * width + low
            kvr_ref[:, first : first + half] = jnp.dot(
                normed, weights[k], preferred_element_type=F32
            ).astype(BF16)

    put(own_ref, 0)
    for copy in copies:
        copy.wait()
    put(other, half)


def branch_body(
    attended_ref, own_ref, other_ref, x_ref, member_ref, mod_ref, middle_ref, branch_ref, normed_ref
):
    width = x_ref.shape[1]
    half = width // 2
    member = member_ref[...]

    def mods(k):
        return jnp.dot(
            member, mod_ref[:, k * width : (k + 1) * width], preferred_element_type=F32
        )

    branch = jnp.dot(attended_ref[:, :half], own_ref[...], preferred_element_type=F32)
    branch += jnp.dot(attended_ref[:, half:], other_ref[...], preferred_element_type=F32)
    branch_ref[...] = branch
    middle = x_ref[...].astype(F32) + mods(2) * branch
    middle_ref[...] = middle
    m_hat, _ = norm_parts(middle)
    normed_ref[...] = (m_hat * (1.0 + mods(4)) + mods(3)).astype(BF16)


def ffn_body(
    normed_ref, dout_ref, member_ref, mod_ref, moved_ref, gate_up_ref, down_ref,
    ffn_out_ref, d_normed_out_ref, normed_t_ref, d_ffn_t_ref, d_gate_ref, d_up_ref, hidden_ref,
    ffn_ref, d_normed_ref, d_ffn_ref,
):
    step = pl.program_id(0)
    last = pl.num_programs(0) - 1

    @pl.when(step == 0)
    def _():
        scale = jnp.dot(member_ref[...], mod_ref[...], preferred_element_type=F32)
        d_ffn_ref[...] = (scale * dout_ref[...].astype(F32)).astype(BF16)
        normed_t_ref[...] = nt(moved_ref[...], normed_ref[...]).astype(BF16)
        d_ffn_t_ref[...] = nt(moved_ref[...], d_ffn_ref[...]).astype(BF16)

    normed, d_ffn = normed_ref[...], d_ffn_ref[...]
    w_gate, w_up, w_down = gate_up_ref[0], gate_up_ref[1], down_ref[...]
    gate = jnp.dot(normed, w_gate, preferred_element_type=F32)
    up = jnp.dot(normed, w_up, preferred_element_type=F32)
    d_hidden = nt(d_ffn, w_down)
    sigma = jax.nn.sigmoid(gate)
    value = gate * sigma
    hid = (value * up).astype(BF16)
    d_up = (d_hidden * value).astype(BF16)
    d_gate = (d_hidden * up * (sigma + value * (1.0 - sigma))).astype(BF16)
    hidden_ref[...] = hid
    d_up_ref[...] = d_up
    d_gate_ref[...] = d_gate
    ffn = jnp.dot(hid, w_down, preferred_element_type=F32)
    d_normed = nt(d_gate, w_gate) + nt(d_up, w_up)

    @pl.when(step == 0)
    def _():
        ffn_ref[...] = ffn
        d_normed_ref[...] = d_normed

    @pl.when(jnp.logical_and(step > 0, step < last))
    def _():
        ffn_ref[...] += ffn
        d_normed_ref[...] += d_normed

    @pl.when(step == last)
    def _():
        ffn_out_ref[...] = (ffn_ref[...] + ffn).astype(ffn_out_ref.dtype)
        d_normed_out_ref[...] = (d_normed_ref[...] + d_normed).astype(d_normed_out_ref.dtype)


def ffn_grad_body(
    normed_t_ref, normed_t_far_ref, d_ffn_t_ref, d_ffn_t_far_ref,
    d_gate_ref, d_gate_far_ref, d_up_ref, d_up_far_ref, hidden_ref, hidden_far_ref,
    keep_ref, send_ref,
):
    half = normed_t_ref.shape[0] // 2
    normed_t = (normed_t_ref, normed_t_far_ref)
    d_ffn_t = (d_ffn_t_ref, d_ffn_t_far_ref)
    for k, (left_t, near, far) in enumerate(
        (
            (normed_t, d_gate_ref, d_gate_far_ref),
            (normed_t, d_up_ref, d_up_far_ref),
            (d_ffn_t, hidden_ref, hidden_far_ref),
        )
    ):
        total = jnp.dot(left_t[0][...], near[...], preferred_element_type=F32) + jnp.dot(
            left_t[1][...], far[...], preferred_element_type=F32
        )
        keep_ref[k] = total[:half].astype(BF16)
        send_ref[k] = total[half:].astype(BF16)


def mix_body(middle_ref, ffn_ref, ffn_far_ref, dout_ref, member_ref, mod_ref, mixed_ref, d_mods_ref):
    member = member_ref[...]
    ffn = ffn_ref[...] + ffn_far_ref[...].astype(F32)
    scale = jnp.dot(member, mod_ref[...], preferred_element_type=F32)
    mixed_ref[...] = (middle_ref[...] + scale * ffn).astype(BF16)
    part = tn(member, (dout_ref[...].astype(F32) * ffn).astype(BF16))

    @pl.when(pl.program_id(0) == 0)
    def _():
        d_mods_ref[...] = part

    @pl.when(pl.program_id(0) > 0)
    def _():
        d_mods_ref[...] += part


def middle_back_body(
    d_normed_ref, d_normed_far_ref, middle_ref, branch_ref, dout_ref, member_ref,
    mod_ref, own_ref, other_ref, d_middle_ref, d_attended_ref, d_attn_ref, d_mods_ref
):
    step = pl.program_id(0)
    rows, width = d_normed_ref.shape
    half = width // 2

    @pl.when(step == 0)
    def _():
        d_mods_ref[...] = jnp.zeros_like(d_mods_ref)

    member = member_ref[...]

    def mods(k):
        return jnp.dot(
            member, mod_ref[:, k * width : (k + 1) * width], preferred_element_type=F32
        )

    def add_mods(k, values):
        d_mods_ref[:, k * width : (k + 1) * width] += tn(member, values.astype(BF16))

    middle = middle_ref[...]
    m_hat, inverse = norm_parts(middle)
    d_normed = d_normed_ref[...] + d_normed_far_ref[...].astype(F32)
    add_mods(1, d_normed)
    add_mods(2, d_normed * m_hat)
    d_hat = d_normed * (1.0 + mods(4))
    d_middle = dout_ref[...].astype(F32) + inverse * (
        d_hat
        - jnp.mean(d_hat, axis=-1, keepdims=True)
        - m_hat * jnp.mean(d_hat * m_hat, axis=-1, keepdims=True)
    )
    d_middle_ref[...] = d_middle
    add_mods(0, d_middle * branch_ref[...])
    d_attn = (mods(2) * d_middle).astype(BF16)
    d_attn_ref[...] = d_attn
    d_attended_ref[:, :half] = nt(d_attn, own_ref[...]).astype(BF16)

    d_attended_ref[:, half:] = nt(d_attn, other_ref[...]).astype(BF16)


def attention_grad_body(
    q_ref, own_ref, far_ref, normed_ref, d_attn_ref, attended_ref, moved_ref,
    d_proj_ref, keep_qk_ref, send_qk_ref, keep_vo_ref, send_vo_ref
):
    width = normed_ref.shape[1]
    half = width // 2
    d_proj_ref[:, :width] = q_ref[...]
    d_proj_ref[:, width:] = (own_ref[...].astype(F32) + far_ref[...].astype(F32)).astype(BF16)
    turned = nt(moved_ref[...], normed_ref[...]).astype(BF16)
    for j in range(4):
        if j == 3:
            turned = nt(moved_ref[...], d_attn_ref[...]).astype(BF16)
            right_side = attended_ref[...]
        else:
            right_side = d_proj_ref[:, j * width : (j + 1) * width]
        total = jnp.dot(turned, right_side, preferred_element_type=F32).astype(BF16)
        keep_ref, send_ref = (keep_qk_ref, send_qk_ref) if j < 2 else (keep_vo_ref, send_vo_ref)
        for k in range(2):
            keep_ref[k, j % 2] = total[:half, k * half : (k + 1) * half]
            send_ref[k, j % 2] = total[half:, k * half : (k + 1) * half]


def deliver_body(*refs):
    count = len(refs) // 2
    for k in range(count):
        refs[count + k][...] = refs[k][...]


def input_back_body(
    at_ref, d_proj_ref, x_ref, d_middle_ref, member_ref, mod_ref, own_ref, *rest
):
    pieces, (grad_ref, d_mods_ref), (other, sems) = rest[:2], rest[2:4], rest[4:]
    width = x_ref.shape[1]
    half = width // 2
    copies = fetch(pieces, other, sems, at_ref, width // 2)
    d_normed = nt(d_proj_ref[:, :half], own_ref[0])
    for j in (1, 2):
        d_normed += nt(d_proj_ref[:, j * width : j * width + half], own_ref[j])
    for copy in copies:
        copy.wait()
    for j in range(3):
        d_normed += nt(d_proj_ref[:, j * width + half : (j + 1) * width], other[j])
    member = member_ref[...]
    scale = jnp.dot(member, mod_ref[:, width:], preferred_element_type=F32)
    x_hat, inverse = norm_parts(x_ref[...].astype(F32))
    d_mods_ref[:, :width] = tn(member, d_normed.astype(BF16))
    d_mods_ref[:, width:] = tn(member, (d_normed * x_hat).astype(BF16))
    d_hat = d_normed * (1.0 + scale)
    grad_ref[...] = (
        d_middle_ref[...]
        + inverse
        * (
            d_hat
            - jnp.mean(d_hat, axis=-1, keepdims=True)
            - x_hat * jnp.mean(d_hat * x_hat, axis=-1, keepdims=True)
        )
    ).astype(BF16)


ANYWHERE = pl.BlockSpec(memory_space=pl.ANY)
IN_SMEM = pl.BlockSpec(memory_space=pltpu.SMEM)


def call(body, operands, specs, outs, out_specs, scratch, flops, name, grid=(1,)):
    moved = sum(math.prod(a.shape) * a.dtype.itemsize for a in operands) + sum(
        math.prod(o.shape) * jnp.dtype(o.dtype).itemsize for o in outs
    )
    return pl.pallas_call(
        body,
        grid=grid,
        in_specs=specs,
        out_specs=out_specs,
        out_shape=outs,
        scratch_shapes=scratch,
        compiler_params=pltpu.CompilerParams(vmem_limit_bytes=VMEM_LIMIT),
        cost_estimate=pl.CostEstimate(
            flops=flops // COST_CUT, bytes_accessed=moved // COST_CUT, transcendentals=0
        ),
        name=name,
    )(*operands)


def shaped(shape, dtype=BF16):
    return jax.ShapeDtypeStruct(shape, dtype)


def make_moves(dp_count):
    def pairs(target):
        moved = []
        for d in range(dp_count):
            for m in range(2):
                to_d, to_m = target(d, m)
                moved.append((d * 2 + m, to_d * 2 + to_m))
        return moved

    def mover(target):
        table = pairs(target)
        return lambda array: lax.ppermute(array, AXES, table)

    turn = mover(lambda d, m: ((d & ~1) | m, d & 1))
    turn_far = mover(lambda d, m: ((d & ~1) | m, 1 - (d & 1)))
    across = mover(lambda d, m: (d, 1 - m))

    def flip(bit):
        return mover(lambda d, m: (d ^ (1 << bit), m))

    def to(mask, over):
        return mover(lambda d, m: (d ^ mask, m ^ over))

    return turn, turn_far, across, flip, to


def shards(
    tokens,
    pair_left,
    pair_right,
    chain_len,
    chain_time,
    chain_arch,
    cath_table,
    time_weight,
    mod_weight,
    mod_bias,
    qkv_weight,
    pair_weight,
    out_weight,
    gate_up_weight,
    down_weight,
    cotangent,
):
    dp_count = lax.axis_size("dp")
    bits = dp_count.bit_length() - 1
    turn, turn_far, across, flip, to = make_moves(dp_count)
    core_swap = flip(0)
    dp_at = lax.axis_index("dp")
    mp_at = lax.axis_index("mp")
    core = dp_at & 1
    rows, width = tokens.shape
    slots = chain_len.shape[1]
    half_heads = pair_weight.shape[1]
    heads = 2 * half_heads
    pair_width = pair_left.shape[1]
    cond_width = time_weight.shape[0]
    half = width // 2
    hidden = down_weight.shape[0]

    def after(array, *earlier):
        return lax.optimization_barrier((array, *earlier))[0]

    def beside(made, *received):
        return lax.optimization_barrier((*made, *received))[: len(made)]

    held_chains = jnp.concatenate(
        [chain_len.astype(F32), chain_time, chain_arch.astype(F32)], axis=0
    )
    near_chains = core_swap(held_chains)

    cut = qkv_weight.shape[1] // 2
    pair_mix_other = across(pair_weight)
    qkv_y = across(lax.dynamic_slice_in_dim(qkv_weight, core * cut, cut, 1))
    x_in = turn(after(tokens, qkv_y, pair_mix_other))
    qkv_pieces = [qkv_y, core_swap(qkv_y)]
    right_own = turn(after(pair_right, x_in))
    left_in = turn(after(pair_left, x_in))
    out_other = across(after(out_weight, right_own))
    dout = turn(after(cotangent, right_own))
    dout_far = turn_far(after(cotangent, out_other))

    def ends_of(chains):
        return jnp.cumsum(chains[0].astype(jnp.int32))

    chains = jnp.where(core == mp_at, held_chains, near_chains)
    far_chains = jnp.where(core == mp_at, near_chains, held_chains)
    arches = chains[2].astype(jnp.int32)
    ends = ends_of(chains)
    times = jnp.concatenate([chains[1], far_chains[1]])

    def ids_of(part, ends=ends):
        positions = jnp.arange(rows, dtype=jnp.int32) + part * rows
        return jnp.sum((positions[:, None] >= ends[None, :]).astype(jnp.int32), axis=1)

    own_ids = ids_of(core)
    key_ids = jnp.concatenate([own_ids, ids_of(1 - core)])
    chain_numbers = jnp.arange(slots, dtype=jnp.int32)
    doubled = jnp.concatenate([chain_numbers, chain_numbers])[None, :]
    member = (own_ids[:, None] == doubled).astype(BF16)
    member_far = (ids_of(core, ends_of(far_chains))[:, None] == doubled).astype(BF16)
    lanes = jnp.arange(128, dtype=jnp.int32)[None, :] & 63
    hot = (own_ids[:, None] == lanes).astype(BF16)
    pens = jnp.where((key_ids[:, None] != lanes) & (lanes <= slots), -1e30, 0.0).astype(BF16)
    pen_own, pen_near = pens[:rows], pens[rows:]

    half_cond = cond_width // 2
    frequency = jnp.exp(jnp.arange(half_cond, dtype=F32) * (-math.log(10000.0) / half_cond))
    angles = times[:, None] * 1000.0 * frequency[None, :]
    time_embed = jnp.concatenate([jnp.sin(angles), jnp.cos(angles)], axis=1).astype(BF16)
    both_arches = jnp.concatenate([arches, far_chains[2].astype(jnp.int32)])
    arch_onehot = (
        both_arches[:, None] == jnp.arange(cath_table.shape[0], dtype=jnp.int32)[None, :]
    ).astype(F32)
    cond_pre = dot_f32(time_embed, time_weight) + highest_dot(arch_onehot, cath_table.astype(F32))
    cond_value, cond_slope = silu_parts(cond_pre)
    cond_act = cond_value.astype(BF16)
    chain_mod = dot_f32(cond_act, mod_weight) + mod_bias.astype(F32)[None, :]
    mod_high = lax.reduce_precision(chain_mod, 8, 7)
    mod_low = (chain_mod - mod_high).astype(BF16)
    mod_high = mod_high.astype(BF16)
    mods = jnp.concatenate([mod_high[:slots], mod_low[:slots]], axis=0)
    gate_far = jnp.concatenate([mod_high[slots:], mod_low[slots:]], axis=0)[:, 5 * width :]
    time_embed, cond_act, cond_slope = time_embed[:slots], cond_act[:slots], cond_slope[:slots]

    order = [int(format(p, "0%db" % bits)[::-1], 2) for p in range(dp_count)]
    block_at = jnp.array(order, jnp.int32) ^ dp_at
    block_rows = width // dp_count
    source = (block_at[:, None] * block_rows + jnp.arange(block_rows)[None, :]).reshape(-1)
    moved = (source[:, None] == jnp.arange(width)[None, :]).astype(BF16)
    at = core.reshape(1).astype(jnp.int32)
    semaphores = pltpu.SemaphoreType.DMA

    mod_a = mods[:, : 2 * width]
    pair_mix = jnp.concatenate([pair_weight, pair_mix_other], axis=1).astype(F32)
    mix_rows = jnp.transpose(pair_mix).reshape(half_heads, 2, -1)
    queries, kv_own, normed_a = call(
        qkv_body,
        [at, after(x_in, moved, mods, hot, pens, member_far, gate_far), member, mod_a, qkv_weight,
         *qkv_pieces],
        [IN_SMEM] + [whole(a) for a in (x_in, member, mod_a, qkv_weight)] + [ANYWHERE] * 2,
        [shaped((rows, width)), shaped((rows, 2 * width)), shaped((rows, width))],
        [whole(shaped((rows, width))), whole(shaped((rows, 2 * width))),
         whole(shaped((rows, width)))],
        [pltpu.VMEM(qkv_weight.shape, BF16), semaphores((2,))],
        6 * rows * width * width,
        "project",
    )
    queries, kv_own = beside((queries, kv_own), right_own, left_in, mix_rows)
    kv_near = core_swap(kv_own)
    right_near = core_swap(right_own)
    keyed = (kv_own, kv_near, right_own, right_near, pen_own, pen_near)
    attended, inverse, probs = attention_forward(mix_rows, queries, left_in, hot, *keyed)
    wide = shaped((rows, width), F32)
    thin = shaped((rows, width))
    middle, branch, normed_f = call(
        branch_body,
        [attended, out_weight, out_other, x_in, member, mods],
        [whole(a) for a in (attended, out_weight, out_other, x_in, member, mods)],
        [wide, wide, thin],
        [whole(thin)] * 3,
        [],
        2 * rows * width * width,
        "branch",
    )

    normed_far = across(normed_f)
    gate_mod = mods[:, 5 * width :]
    block = FFN_BLOCK
    active = shaped((rows, hidden))
    turned = shaped((width, rows))

    def feed_forward(normed, dout, member, gate, sum_type):
        column = pl.BlockSpec((rows, block), lambda i: (0, i))
        summed = shaped((rows, width), sum_type)
        return call(
            ffn_body,
            [normed, dout, member, gate, moved, gate_up_weight, down_weight],
            [whole(a) for a in (normed, dout, member, gate, moved)]
            + [
                pl.BlockSpec((2, width, block), lambda i: (0, 0, i)),
                pl.BlockSpec((block, width), lambda i: (i, 0)),
            ],
            [summed, summed, turned, turned, active, active, active],
            [whole(thin), whole(thin), whole(turned), whole(turned), column, column, column],
            [
                pltpu.VMEM((rows, width), F32), pltpu.VMEM((rows, width), F32),
                pltpu.VMEM((rows, width), BF16),
            ],
            12 * rows * width * hidden,
            "feed_forward",
            (hidden // block,),
        )

    made = feed_forward(normed_f, dout, member, gate_mod, F32)
    ffn, d_normed_f, normed_t, d_ffn_t, d_gate, d_up, hid = made
    (normed_far,) = lax.optimization_barrier((normed_far, *made))[:1]
    ffn_for, d_normed_for, normed_t_far, d_ffn_t_far, d_gate_far, d_up_far, hid_far = feed_forward(
        normed_far, dout_far, member_far, gate_far, BF16
    )
    d_normed_far = across(d_normed_for)

    grad = shaped((3, half, hidden))
    grad_block = pl.BlockSpec((3, half, block), lambda i: (0, 0, i))
    column = pl.BlockSpec((rows, block), lambda i: (0, i))
    operands = [normed_t, normed_t_far, d_ffn_t, d_ffn_t_far]
    made = call(
        ffn_grad_body,
        operands + [d_gate, d_gate_far, d_up, d_up_far, hid, hid_far],
        [whole(a) for a in operands] + [column] * 6,
        [grad, grad],
        [grad_block, grad_block],
        [],
        12 * rows * width * hidden,
        "feed_forward_grads",
        (hidden // block,),
    )
    keep, send = beside(made, d_normed_far)
    far = core_swap(send)
    ffn_far = across(after(ffn_for, send))

    def plus(kept, received):
        return (kept.astype(F32) + received.astype(F32)).astype(BF16)

    def halves(array, upper):
        size = array.shape[-2] // 2
        return array[..., size:, :] if upper else array[..., :size, :]

    def y_part(kept, received):
        return plus(kept[1], received[1])

    def y_rest(kept, received):
        return plus(kept[0], received[0])

    def bit_part(kept, received):
        return plus(halves(kept, True), halves(received, True))

    def bit_rest(kept, received):
        return plus(halves(kept, False), halves(received, False))

    steps = 2
    row_block = pl.BlockSpec((rows // steps, width), lambda i: (i, 0))
    member_block = pl.BlockSpec((rows // steps, 2 * slots), lambda i: (i, 0))
    mods_early = shaped((2 * slots, 3 * width), F32)
    made = call(
        middle_back_body,
        [after(d_normed_f, send), d_normed_far, middle, branch, dout, member, mods, out_weight,
         out_other],
        [row_block] * 5 + [member_block, whole(mods), whole(out_weight), whole(out_other)],
        [wide, thin, thin, mods_early],
        [row_block, row_block, row_block, whole(mods_early)],
        [],
        4 * rows * width * width,
        "middle_back",
        (steps,),
    )
    d_middle, d_attended, d_attn, d_mods = beside(made, far)
    sent, rest = bit_part(keep, far), bit_rest(keep, far)
    got = flip(1)(sent)

    def core_half(summed, others):
        summed = summed + core_swap(summed)
        held = jnp.concatenate([summed.astype(BF16), *others], axis=1)
        cut = held.shape[1] // 2
        return lax.dynamic_slice_in_dim(held, core * cut, cut, 1)

    near_bits = [-1, 1] if bits > 1 else [-1]
    far_bits = list(range(2, bits))

    def several(group):
        moves = []
        for chosen in range(1, 1 << len(group)):
            mask, over = 0, 0
            for k, bit in enumerate(group):
                if chosen >> k & 1:
                    mask, over = (mask, 1) if bit < 0 else (mask | 1 << bit, over)
            moves.append((mask, over))
        return moves

    def gather_step(group, held):
        return jnp.concatenate(
            [held] + [to(mask, over)(held) for mask, over in several(group)], axis=0
        )

    def whole_columns(held):
        near = core_swap(held)
        return jnp.concatenate(
            [jnp.where(core == 0, held, near), jnp.where(core == 0, near, held)], axis=1
        )

    d_query, d_own, d_far, d_right, d_left, d_mix = attention_backward(
        0, 1, mix_rows, after(d_attended, sent), attended, inverse, probs, queries, left_in, *keyed
    )
    d_query, d_own, d_far, d_right, d_left = beside(
        (d_query, d_own, d_far, d_right, d_left), ffn_far
    )
    far_kv = core_swap(d_far)
    far_right = core_swap(d_right[rows:])
    left_grad = turn(d_left)

    mods_gate = shaped((2 * slots, width), F32)
    mixed, d_mods_gate = call(
        mix_body,
        [after(middle, d_far), ffn, ffn_far, dout, member, gate_mod],
        [row_block] * 4 + [member_block, whole(gate_mod)],
        [thin, mods_gate],
        [row_block, whole(mods_gate)],
        [],
        4 * rows * 16 * width,
        "mix",
        (steps,),
    )
    mixed, d_mods_gate = beside((mixed, d_mods_gate), far_kv, far_right)
    mixed = turn(mixed)
    right_grad = turn(plus(d_right[:rows], far_right))

    proj_grad = shaped((rows, 3 * width))
    pair_grad = shaped((2, 2, half, half))
    operands = [d_query, d_own, far_kv, after(normed_a, d_mods_gate), d_attn, attended, moved]
    outs = [proj_grad] + [pair_grad] * 4
    made = call(
        attention_grad_body,
        operands,
        [whole(a) for a in operands],
        outs,
        [whole(a) for a in outs],
        [],
        12 * rows * width * width,
        "attention_grads",
    )
    d_proj, keep_qk, send_qk, keep_vo, send_vo = beside(made, got, left_grad, right_grad)
    far_qk, far_vo = core_swap(send_qk), core_swap(send_vo)
    sent, rest = bit_part(rest, got), bit_rest(rest, got)
    got = flip(2)(after(sent, left_grad))
    sent_qk, sent_vo = y_part(keep_qk, far_qk), bit_part(keep_vo, far_vo)
    rest_qk, rest_vo = y_rest(keep_qk, far_qk), bit_rest(keep_vo, far_vo)
    got_qk, got_vo = across(sent_qk), flip(1)(sent_vo)
    mods_late = shaped((2 * slots, 2 * width), F32)
    operands = [at, after(d_proj, sent_qk, sent_vo), x_in, d_middle, member, mod_a, qkv_weight]
    made = call(
        input_back_body,
        [*operands, *qkv_pieces],
        [IN_SMEM] + [whole(a) for a in operands[1:]] + [ANYWHERE] * 2,
        [thin, mods_late],
        [whole(thin), whole(mods_late)],
        [pltpu.VMEM(qkv_weight.shape, BF16), semaphores((2,))],
        6 * rows * width * width,
        "input_back",
    )
    tokens_out, d_mods_a = beside(made, got_qk, got_vo, got, mixed)
    sent, rest = bit_part(rest, got), bit_rest(rest, got)
    token_gradient = turn(tokens_out)

    d_mix = d_mix.reshape(heads, -1)
    d_mix = jnp.concatenate(
        [
            jnp.where(mp_at == 0, d_mix[:half_heads], d_mix[half_heads:]),
            jnp.where(mp_at == 0, d_mix[half_heads:], d_mix[:half_heads]),
        ],
        axis=0,
    ).reshape(slots, -1)
    arch_low = (arches[:, None] == jnp.arange(128, dtype=jnp.int32)[None, :]).astype(BF16)
    modded = 6 * width
    mixed_to = modded + d_mix.shape[1]
    others = [cond_act, time_embed, cond_slope.astype(BF16), arch_low]
    filler = jnp.zeros((slots, -(mixed_to + 3 * cond_width + 128) % 256), BF16)
    held = core_half(
        jnp.concatenate(
            [d_mods_a[:slots], d_mods[:slots], d_mods_gate[:slots], d_mix], axis=1
        ),
        [*others, filler],
    )

    def together(*arrays):
        return lax.optimization_barrier(arrays)

    vo = plus(rest_vo, got_vo)
    qk = plus(rest_qk, got_qk)
    got_qk, got_vo = flip(1)(halves(qk, True)), across(vo[1])
    held = gather_step(near_bits, held)

    def finish(bit, kept, sent):
        while bit < bits:
            received = flip(bit)(sent)
            bit += 1
            if bit < bits:
                kept, sent = bit_rest(kept, received), bit_part(kept, received)
        return kept.astype(F32) + received.astype(F32)

    qkvo = jnp.concatenate(
        [plus(halves(qk, False), got_qk), plus(vo[0], got_vo)], axis=0
    )
    held, sent, qkvo, token_gradient = together(held, sent, qkvo, token_gradient)
    ffn_sum = finish(3, rest, sent)
    held = gather_step(far_bits, held)
    qkvo_sum = finish(2, halves(qkvo, False), halves(qkvo, True))

    held = whole_columns(held)
    mix_sum = jnp.sum(
        held[:, modded:mixed_to].astype(F32).reshape(dp_count, heads, -1), axis=0
    )
    mix_sum = jnp.where(mp_at == 0, mix_sum[:half_heads], mix_sum[half_heads:])
    taken = mix_sum.shape[1] // dp_count
    pair_sum = jnp.transpose(lax.dynamic_slice_in_dim(mix_sum, dp_at * taken, taken, 1))
    d_all = held[:, :modded]
    cond_all, time_all, slope_all, arch_all, _ = jnp.split(
        held[:, mixed_to:],
        [cond_width, 2 * cond_width, 3 * cond_width, 3 * cond_width + 128],
        axis=1,
    )
    mod_bias_sum = jnp.sum(d_all.astype(F32), axis=0)
    mod_weight_sum = dot_f32(jnp.transpose(cond_all), d_all)
    d_cond_pre = dot_nt(d_all, mod_weight) * slope_all.astype(F32)
    time_sum = highest_dot(jnp.transpose(time_all.astype(F32)), d_cond_pre)
    cath_sum = highest_dot(
        jnp.transpose(arch_all[:, : cath_table.shape[0]].astype(F32)), d_cond_pre
    )

    outs = [mixed, token_gradient, left_grad, right_grad]
    blocks = [pl.BlockSpec((rows // 4, a.shape[1]), lambda i: (i, 0)) for a in outs]
    mixed, token_gradient, left_grad, right_grad = call(
        deliver_body, outs, blocks, [shaped(a.shape) for a in outs], blocks, [], 0, "deliver", (4,)
    )
    return (
        mixed,
        token_gradient,
        left_grad,
        right_grad,
        cath_sum,
        time_sum,
        mod_weight_sum,
        mod_bias_sum,
        qkvo_sum[:3],
        pair_sum,
        jnp.transpose(qkvo_sum[3]),
        ffn_sum[:2],
        jnp.transpose(ffn_sum[2]),
    )


def solution(mesh):
    by_rows = P(AXES, None)
    placed = (
        by_rows,
        by_rows,
        by_rows,
        P("dp", None),
        P("dp", None),
        P("dp", None),
        P(),
        P(),
        P(),
        P(),
        P(None, None, "mp"),
        P(None, "mp"),
        P("mp", None),
        P(None, None, "mp"),
        P("mp", None),
        by_rows,
    )
    return jax.shard_map(
        shards,
        mesh=mesh,
        in_specs=placed,
        out_specs=(
            by_rows,
            by_rows,
            by_rows,
            by_rows,
            P(),
            P(),
            P(),
            P(),
            P(None, "dp", "mp"),
            P("dp", "mp"),
            P("mp", "dp"),
            P(None, "dp", "mp"),
            P("mp", "dp"),
        ),
        check_vma=False,
    )
```

```python
import functools
import math

import jax
import jax.numpy as jnp
from jax import lax
from jax.experimental import pallas as pl
from jax.experimental.pallas import tpu as pltpu
from jax.sharding import PartitionSpec as P

EPSILON = 1e-06
AXES = ("dp", "mp")
BF16 = jnp.bfloat16
F32 = jnp.float32
VMEM_LIMIT = 60 * 1024 * 1024
FFN_BLOCK = 512
GRAD_BLOCK = 768
BACK_PARTS = 1
COST_CUT = 20


def highest_dot(left_side, right_side):
    return jnp.dot(left_side, right_side, precision=lax.Precision.HIGHEST)


def silu_parts(values):
    sigma = jax.nn.sigmoid(values)
    return (values * sigma, sigma * (1.0 + values * (1.0 - sigma)))


def dot_f32(left_side, right_side):
    return jnp.dot(left_side, right_side, preferred_element_type=F32)


def dot_nt(left_side, right_side):
    return lax.dot_general(
        left_side, right_side, (((1,), (1,)), ((), ())), preferred_element_type=F32
    )

def lane_mix(first, second, odd):
    lane = lax.broadcasted_iota(jnp.int32, first.shape, 1)
    keep = (lane >= 64) if odd else (lane < 64)
    return jnp.where(keep, first, second)


def nt(left_side, right_side):
    return lax.dot_general(
        left_side, right_side, (((1,), (1,)), ((), ())), preferred_element_type=F32
    )


def attention_forward_body(
    pair_mix_ref, q_ref, left_ref, hot_ref, k_own_ref, k_near_ref, v_own_ref, v_near_ref,
    right_own_ref, right_near_ref, pen_own_ref, pen_near_ref,
    attended_ref, inverse_ref, probs_ref,
):
    rows = q_ref.shape[0]
    step = 256
    out_tiles = []
    left = left_ref[...].astype(F32)
    for odd in range(2):
        mix = pair_mix_ref[0, odd : odd + 1, :]
        left_mixed = (left * mix).astype(BF16)
        q_side = jnp.concatenate([left_mixed, lane_mix(q_ref[...], hot_ref[...], odd)], axis=1)
        k_own = jnp.concatenate(
            [right_own_ref[...], lane_mix(k_own_ref[...], pen_own_ref[...], odd)], axis=1
        )
        k_near = jnp.concatenate(
            [right_near_ref[...], lane_mix(k_near_ref[...], pen_near_ref[...], odd)], axis=1
        )
        v_own = lane_mix(v_own_ref[...], jnp.ones_like(v_own_ref[...]), odd)
        v_near = lane_mix(v_near_ref[...], jnp.ones_like(v_near_ref[...]), odd)
        tiles = []
        for start in range(0, rows, step):
            block = q_side[start : start + step]
            s_own = nt(block, k_own)
            s_near = nt(block, k_near)
            top = jnp.maximum(
                jnp.max(s_own, axis=1, keepdims=True), jnp.max(s_near, axis=1, keepdims=True)
            )
            e_own = jnp.exp(s_own - top).astype(BF16)
            e_near = jnp.exp(s_near - top).astype(BF16)
            probs_ref[odd, start : start + step, :rows] = e_own
            probs_ref[odd, start : start + step, rows:] = e_near
            tiles.append(
                jnp.dot(e_own, v_own, preferred_element_type=F32)
                + jnp.dot(e_near, v_near, preferred_element_type=F32)
            )
        out_tiles.append(jnp.concatenate(tiles, axis=0))
    sums = lane_mix(out_tiles[1], out_tiles[0], False)
    sums = pltpu.roll(sums, 64, 1)
    inverse = 1.0 / sums
    attended_ref[...] = (lane_mix(out_tiles[0], out_tiles[1], False) * inverse).astype(BF16)
    inverse_ref[...] = inverse


def attention_backward_body(
    pair_mix_ref, grad_ref, left_ref, right_own_ref, right_near_ref, pen_own_ref, pen_near_ref,
    *rest
):
    outs = rest[16:21]
    scores_ref, right_sum_ref, left_sum_ref, left_t_ref = rest[21:]
    pair = pl.program_id(0)
    pairs = pl.num_programs(0)

    @pl.when(pair == 0)
    def _():
        left_t_ref[...] = left_ref[...].T
        outs[4][...] = jnp.zeros_like(outs[4])
        right_sum_ref[...] = jnp.zeros_like(right_sum_ref)
        left_sum_ref[...] = jnp.zeros_like(left_sum_ref)

    common = (
        pair_mix_ref, grad_ref, left_ref, right_own_ref, right_near_ref, pen_own_ref, pen_near_ref,
        *outs, *rest[21:],
    )

    @pl.when(pair < pairs // 2)
    def _():
        attention_backward_pair(common, *rest[:8])

    @pl.when(pair >= pairs // 2)
    def _():
        attention_backward_pair(common, *rest[8:16])

    @pl.when(pair == pairs - 1)
    def _():
        rows = left_ref.shape[0]
        right = right_sum_ref[...].T.astype(BF16)
        outs[1][:, outs[1].shape[1] - right.shape[1] :] = right[:rows]
        outs[2][:, outs[1].shape[1] - right.shape[1] :] = right[rows:]
        outs[3][...] = left_sum_ref[...].astype(BF16)


def attention_backward_pair(
    common, attended_ref, inverse_ref, probs_ref, q_ref, k_own_ref, k_near_ref, v_own_ref,
    v_near_ref
):
    (
        pair_mix_ref, grad_ref, left_ref, right_own_ref, right_near_ref, pen_own_ref, pen_near_ref,
        d_q_ref, own_out, near_out, _, d_mix_ref,
        scores_ref, right_sum_ref, left_sum_ref, left_t_ref,
    ) = common
    pair = pl.program_id(0)
    rows = q_ref.shape[0]
    step = 256
    wide = grad_ref.shape[1] * pl.num_programs(0)
    scaled = (grad_ref[...].astype(F32) * inverse_ref[...]).astype(BF16)
    products = scaled.astype(F32) * attended_ref[...].astype(F32)
    scaled_t = scaled.T
    q_t = q_ref[...].T
    lane = lax.broadcasted_iota(jnp.int32, products.shape, 1)
    left = left_ref[...].astype(F32)
    left_t = left_t_ref[...].astype(F32)
    d_q, dk_t, dv_t = [], [], []
    for odd in range(2):
        mine = (lane >= 64) if odd else (lane < 64)
        delta = -jnp.sum(jnp.where(mine, products, 0.0), axis=1, keepdims=True)
        high = delta.astype(BF16).astype(F32)
        low = delta - high
        at = 0 if odd else 64
        extra = jnp.where(lane == at, high, jnp.where(lane == at + 1, low, 0.0)).astype(BF16)
        grad_side = jnp.where(mine, scaled, extra)
        mix = pair_mix_ref[0, odd : odd + 1, :]
        k_own = jnp.concatenate(
            [right_own_ref[...], lane_mix(k_own_ref[...], pen_own_ref[...], odd)], axis=1
        )
        k_near = jnp.concatenate(
            [right_near_ref[...], lane_mix(k_near_ref[...], pen_near_ref[...], odd)], axis=1
        )
        v_own = lane_mix(v_own_ref[...], jnp.ones_like(v_own_ref[...]), odd)
        v_near = lane_mix(v_near_ref[...], jnp.ones_like(v_near_ref[...]), odd)
        for start in range(0, rows, step):
            block = grad_side[start : start + step]
            own = nt(block, v_own).astype(BF16) * probs_ref[odd, start : start + step, :rows]
            near = nt(block, v_near).astype(BF16) * probs_ref[odd, start : start + step, rows:]
            scores_ref[start : start + step, :rows] = own
            scores_ref[start : start + step, rows:] = near
        d_query = jnp.dot(
            scores_ref[:, :rows], k_own, preferred_element_type=F32
        ) + jnp.dot(scores_ref[:, rows:], k_near, preferred_element_type=F32)
        width = left.shape[1]
        d_q.append(d_query[:, width:])
        d_pair = d_query[:, :width]
        left_sum_ref[...] += d_pair * mix
        d_mix_ref[pl.ds(pair, 1), odd * width : (odd + 1) * width] = jnp.sum(
            d_pair * left, axis=0, keepdims=True
        )
        mixed_t = (left_t * jnp.transpose(mix)).astype(BF16)
        low_row = 64 * odd
        q_side = jnp.concatenate([mixed_t, q_t[low_row : low_row + 64]], axis=0)
        d_key = jnp.dot(q_side, scores_ref[...], preferred_element_type=F32)
        right_sum_ref[...] += d_key[:width]
        dk_t.append(d_key[width:])
        dv_t.append(
            jnp.dot(
                scaled_t[low_row : low_row + 64], probs_ref[odd], preferred_element_type=F32
            )
        )
    d_q_ref[...] = (lane_mix(d_q[0], d_q[1], False) * 0.125).astype(BF16)
    for base, parts in ((0, dk_t), (wide, dv_t)):
        both = jnp.concatenate(parts, axis=0).T.astype(BF16)
        column = pl.multiple_of(base + pair * 128, 128)
        own_out[:, pl.ds(column, 128)] = both[:rows]
        near_out[:, pl.ds(column, 128)] = both[rows:]


def whole(array):
    zeros = (0,) * array.ndim
    return pl.BlockSpec(array.shape, lambda *_: zeros)


def attention_forward(
    part, pair_mix, queries, left, hot, kv_own, kv_near, right_own, right_near, pen_own, pen_near
):
    rows, width = queries.shape
    pairs = width // 128
    pair_width = left.shape[1]
    column = pl.BlockSpec((rows, 128), lambda p: (0, p))
    value_column = pl.BlockSpec((rows, 128), lambda p: (0, pairs + p))
    operands = [
        pair_mix, queries, left, hot, kv_own, kv_near, kv_own, kv_near, right_own, right_near,
        pen_own, pen_near,
    ]
    return call(
        attention_forward_body,
        operands,
        [
            pl.BlockSpec((1, 2, pair_width), lambda p: (part * pairs + p, 0, 0)), column,
            whole(left), whole(hot), column, column, value_column, value_column,
            whole(right_own), whole(right_near), whole(pen_own), whole(pen_near),
        ],
        [
            shaped((rows, width)), shaped((rows, width), F32),
            shaped((2 * pairs, rows, 2 * rows)),
        ],
        [column, column, pl.BlockSpec((2, rows, 2 * rows), lambda p: (p, 0, 0))],
        [],
        2 * 2 * pairs * rows * 2 * rows * 512,
        "attention_forward",
        (pairs,),
    )


def attention_backward(
    pair_mix, grad, halves, left, right_own, right_near, pen_own, pen_near
):
    rows, width = grad.shape
    pairs = width // 128
    here = pairs // 2
    pair_width = left.shape[1]
    column = pl.BlockSpec((rows, 128), lambda p: (0, p))
    mix = pl.BlockSpec((1, 2, pair_width), lambda p: (p, 0, 0))
    both = shaped((rows, 2 * width + pair_width))
    operands = [pair_mix, grad, left, right_own, right_near, pen_own, pen_near]
    specs = [mix, column] + [whole(a) for a in operands[2:]]
    for part, (attended, inverse, probs, queries, kv_own, kv_near) in enumerate(halves):
        at = lambda p, part=part: jnp.clip(p - part * here, 0, here - 1)
        own = pl.BlockSpec((rows, 128), lambda p, at=at: (0, at(p)))
        value = pl.BlockSpec((rows, 128), lambda p, at=at: (0, here + at(p)))
        operands += [attended, inverse, probs, queries, kv_own, kv_near, kv_own, kv_near]
        specs += [
            own, own, pl.BlockSpec((2, rows, 2 * rows), lambda p, at=at: (at(p), 0, 0)), own, own,
            own, value, value,
        ]
    outs = [
        shaped((rows, width)), both, both, shaped((rows, pair_width)),
        shaped((8, 2 * pair_width), F32),
    ]
    return call(
        attention_backward_body,
        operands,
        specs,
        outs,
        [column, whole(both), whole(both), whole(outs[3]), whole(outs[4])],
        [
            pltpu.VMEM((rows, 2 * rows), BF16),
            pltpu.VMEM((pair_width, 2 * rows), F32),
            pltpu.VMEM((rows, pair_width), F32),
            pltpu.VMEM((pair_width, rows), BF16),
        ],
        2 * 2 * pairs * rows * 2 * rows * 1000,
        "attention_backward",
        (pairs,),
    )


def norm_parts(values):
    centered = values - jnp.mean(values, axis=-1, keepdims=True)
    inverse = lax.rsqrt(jnp.mean(centered * centered, axis=-1, keepdims=True) + EPSILON)
    return centered * inverse, inverse


def tn(left_side, right_side):
    return lax.dot_general(
        left_side, right_side, (((0,), (0,)), ((), ())), preferred_element_type=F32
    )


def qkv_body(x_ref, member_ref, mod_ref, own_ref, q_ref, kv_ref, normed_ref):
    width = x_ref.shape[1]
    half = width // 2
    mods = jnp.dot(member_ref[...], mod_ref[...], preferred_element_type=F32)
    x_hat, _ = norm_parts(x_ref[...].astype(F32))
    normed = (x_hat * (1.0 + mods[:, width:]) + mods[:, :width]).astype(BF16)
    normed_ref[...] = normed
    q = jnp.dot(normed, own_ref[0], preferred_element_type=F32).astype(BF16)
    q_ref[...] = (q.astype(F32) * 0.125).astype(BF16)
    for k in (1, 2):
        kv_ref[:, (k - 1) * half : k * half] = jnp.dot(
            normed, own_ref[k], preferred_element_type=F32
        ).astype(BF16)


def columns_at(at_ref, r, size):
    return pl.ds(pl.multiple_of((at_ref[0] ^ r) * size, size), size)


def qkv_other_body(at_ref, normed_ref, piece_0, piece_1, q_ref, kv_ref):
    half = normed_ref.shape[1] // 2
    sides = [(normed_ref[:, columns_at(at_ref, r, half)], p) for r, p in enumerate((piece_0, piece_1))]

    def product(k):
        return sum(
            jnp.dot(side, piece[k], preferred_element_type=F32) for side, piece in sides
        ).astype(BF16)

    q_ref[...] = (product(0).astype(F32) * 0.125).astype(BF16)
    for k in (1, 2):
        kv_ref[:, (k - 1) * half : k * half] = product(k)


def branch_body(
    at_ref, attended_ref, attended_other_ref, own_ref, piece_0, piece_1, x_ref, member_ref, mod_ref,
    middle_ref, branch_ref, normed_ref
):
    width = x_ref.shape[1]
    half = width // 2
    member = member_ref[...]

    def mods(k):
        return jnp.dot(
            member, mod_ref[:, k * width : (k + 1) * width], preferred_element_type=F32
        )

    branch_ref[...] = jnp.dot(attended_ref[...], own_ref[...], preferred_element_type=F32)
    for r, piece in enumerate((piece_0, piece_1)):
        branch_ref[:, columns_at(at_ref, r, half)] += jnp.dot(
            attended_other_ref[...], piece[...], preferred_element_type=F32
        )
    branch = branch_ref[...]
    middle = x_ref[...].astype(F32) + mods(2) * branch
    middle_ref[...] = middle
    m_hat, _ = norm_parts(middle)
    normed_ref[...] = (m_hat * (1.0 + mods(4)) + mods(3)).astype(BF16)


def ffn_body(
    normed_ref, dout_ref, member_ref, mod_ref, moved_ref, gate_up_ref, down_ref,
    ffn_out_ref, d_normed_top_ref, d_normed_low_ref, normed_t_ref, d_ffn_t_ref, d_gate_ref,
    d_up_ref, hidden_ref, ffn_ref, d_normed_ref, d_ffn_ref,
):
    step = pl.program_id(0)
    last = pl.num_programs(0) - 1

    @pl.when(step == 0)
    def _():
        scale = jnp.dot(member_ref[...], mod_ref[...], preferred_element_type=F32)
        d_ffn_ref[...] = (scale * dout_ref[...].astype(F32)).astype(BF16)
        normed_t_ref[...] = nt(moved_ref[...], normed_ref[...]).astype(BF16)
        d_ffn_t_ref[...] = nt(moved_ref[...], d_ffn_ref[...]).astype(BF16)

    normed, d_ffn = normed_ref[...], d_ffn_ref[...]
    w_gate, w_up, w_down = gate_up_ref[0], gate_up_ref[1], down_ref[...]
    gate = jnp.dot(normed, w_gate, preferred_element_type=F32)
    up = jnp.dot(normed, w_up, preferred_element_type=F32)
    d_hidden = nt(d_ffn, w_down)
    sigma = jax.nn.sigmoid(gate)
    value = gate * sigma
    hid = (value * up).astype(BF16)
    d_up = (d_hidden * value).astype(BF16)
    d_gate = (d_hidden * up * (sigma + value * (1.0 - sigma))).astype(BF16)
    hidden_ref[...] = hid
    d_up_ref[...] = d_up
    d_gate_ref[...] = d_gate
    ffn = jnp.dot(hid, w_down, preferred_element_type=F32)
    d_normed = nt(d_gate, w_gate) + nt(d_up, w_up)

    @pl.when(step == 0)
    def _():
        ffn_ref[...] = ffn
        d_normed_ref[...] = d_normed

    @pl.when(jnp.logical_and(step > 0, step < last))
    def _():
        ffn_ref[...] += ffn
        d_normed_ref[...] += d_normed

    @pl.when(step == last)
    def _():
        ffn_out_ref[...] = (ffn_ref[...] + ffn).astype(ffn_out_ref.dtype)
        total = d_normed_ref[...] + d_normed
        cut = total.shape[0] // 2
        d_normed_top_ref[...] = total[:cut].astype(d_normed_top_ref.dtype)
        d_normed_low_ref[...] = total[cut:].astype(d_normed_low_ref.dtype)


def ffn_grad_body(
    normed_t_ref, normed_t_far_ref, d_ffn_t_ref, d_ffn_t_far_ref,
    d_gate_ref, d_gate_far_ref, d_up_ref, d_up_far_ref, hidden_ref, hidden_far_ref, out_ref,
):
    normed_t = (normed_t_ref, normed_t_far_ref)
    d_ffn_t = (d_ffn_t_ref, d_ffn_t_far_ref)
    for k, (left_t, near, far) in enumerate(
        (
            (normed_t, d_gate_ref, d_gate_far_ref),
            (normed_t, d_up_ref, d_up_far_ref),
            (d_ffn_t, hidden_ref, hidden_far_ref),
        )
    ):
        out_ref[k] = (
            jnp.dot(left_t[0][...], near[...], preferred_element_type=F32)
            + jnp.dot(left_t[1][...], far[...], preferred_element_type=F32)
        ).astype(BF16)


def mix_body(
    middle_ref, ffn_ref, ffn_far_ref, dout_ref, member_ref, mod_ref, d_mods_ref, d_mix_ref,
    info_ref, mixed_ref, known_ref, gate_sum
):
    member = member_ref[...]
    ffn = ffn_ref[...] + ffn_far_ref[...].astype(F32)
    scale = jnp.dot(member, mod_ref[...], preferred_element_type=F32)
    mixed_ref[...] = (middle_ref[...] + scale * ffn).astype(BF16)
    part = tn(member, (dout_ref[...].astype(F32) * ffn).astype(BF16))

    @pl.when(pl.program_id(0) == 0)
    def _():
        gate_sum[...] = part

    @pl.when(pl.program_id(0) == pl.num_programs(0) - 1)
    def _():
        slots = known_ref.shape[0]
        low = 0
        for values in (d_mods_ref[:slots], gate_sum[:slots] + part[:slots], d_mix_ref[...],
                       info_ref[...]):
            known_ref[:, low : low + values.shape[1]] = values.astype(BF16)
            low += values.shape[1]


def middle_back_body(
    at_ref, top_ref, low_ref, top_far_ref, low_far_ref, middle_ref, branch_ref, dout_ref, member_ref,
    mod_ref, own_ref, piece_0, piece_1, d_middle_ref, d_attended_ref, d_attn_ref, d_mods_ref
):
    step = pl.program_id(0)
    rows, width = top_ref.shape
    half = width // 2

    @pl.when(step == 0)
    def _():
        d_mods_ref[...] = jnp.zeros_like(d_mods_ref)

    member = member_ref[...]

    def mods(k):
        return jnp.dot(
            member, mod_ref[:, k * width : (k + 1) * width], preferred_element_type=F32
        )

    def add_mods(k, values):
        d_mods_ref[:, k * width : (k + 1) * width] += tn(member, values.astype(BF16))

    middle = middle_ref[...]
    m_hat, inverse = norm_parts(middle)
    d_normed = jnp.where(
        step == 0,
        top_ref[...] + top_far_ref[...].astype(F32),
        low_ref[...] + low_far_ref[...].astype(F32),
    )
    add_mods(1, d_normed)
    add_mods(2, d_normed * m_hat)
    d_hat = d_normed * (1.0 + mods(4))
    d_middle = dout_ref[...].astype(F32) + inverse * (
        d_hat
        - jnp.mean(d_hat, axis=-1, keepdims=True)
        - m_hat * jnp.mean(d_hat * m_hat, axis=-1, keepdims=True)
    )
    d_middle_ref[...] = d_middle
    add_mods(0, d_middle * branch_ref[...])
    d_attn = (mods(2) * d_middle).astype(BF16)
    d_attn_ref[...] = d_attn
    d_attended_ref[:, :half] = nt(d_attn, own_ref[...]).astype(BF16)

    d_attended_ref[:, half:] = sum(
        nt(d_attn_ref[:, columns_at(at_ref, r, half)], piece[...])
        for r, piece in enumerate((piece_0, piece_1))
    ).astype(BF16)


def attention_grad_body(
    q_ref, own_ref, far_ref, d_left_ref, normed_ref, d_attn_ref, attended_ref, attended_other_ref,
    moved_ref, d_proj_ref, back_ref, keep_ref, send_ref
):
    width = normed_ref.shape[1]
    half = width // 2
    d_proj_ref[:, :width] = q_ref[...]
    total = (own_ref[...].astype(F32) + far_ref[...].astype(F32)).astype(BF16)
    d_proj_ref[:, width:] = total[:, : 2 * width]
    pair_width = d_left_ref.shape[1]
    back_ref[:, :pair_width] = d_left_ref[...]
    back_ref[:, pair_width:] = total[:, 2 * width :]
    turned = nt(moved_ref[...], normed_ref[...]).astype(BF16)
    for j in range(4):
        if j == 3:
            turned = nt(moved_ref[...], d_attn_ref[...]).astype(BF16)
            right_side = jnp.concatenate([attended_ref[...], attended_other_ref[...]], axis=1)
        else:
            right_side = d_proj_ref[:, j * width : (j + 1) * width]
        total = jnp.dot(turned, right_side, preferred_element_type=F32).astype(BF16)
        for k in range(2):
            keep_ref[k, j] = total[:half, k * half : (k + 1) * half]
            send_ref[k, j] = total[half:, k * half : (k + 1) * half]


def chain_parts(early_ref):
    groups, _, doubled, columns = early_ref.shape
    count = groups * doubled
    return early_ref[:, 0].reshape(count, columns), early_ref[:, 1].reshape(count, columns)


def early_chain_body(here_ref, early_ref, mod_weight_ref, weight_out, bias_out, d_cond_out, mix_out):
    step = pl.program_id(0)
    width = mod_weight_ref.shape[1]
    wide = mod_weight_ref.shape[0]
    modded = 2 * width
    mixed = modded + mix_out.shape[1]
    first, second = chain_parts(early_ref)
    cond = first[:, mixed : mixed + wide]

    def block(low):
        summed = first[:, low : low + width].astype(F32) + second[:, low : low + width].astype(F32)
        early = summed.astype(BF16)
        weight_out[...] = tn(cond, early)
        bias_out[...] = jnp.sum(summed, axis=0, keepdims=True)
        return nt(early, mod_weight_ref[...])

    @pl.when(step == 0)
    def _():
        d_cond_out[...] = block(0)

    @pl.when(step == 1)
    def _():
        d_cond_out[...] += block(width)
        mix = first[:, modded:mixed].astype(F32) + second[:, modded:mixed].astype(F32)
        mix = jnp.sum(mix.reshape(-1, 2, early_ref.shape[2] // 2, mixed - modded), axis=0)
        own = mix_out.shape[0]
        own_half = mix[0, :own] + mix[1, own : 2 * own]
        other_half = mix[0, own : 2 * own] + mix[1, :own]
        mix_out[...] = jnp.where((here_ref[0] & 1) == 0, own_half, other_half)


def late_chain_body(
    far_count, pair_columns, here_ref, early_ref, held_ref, near_ref, mod_weight_ref, d_cond_ref,
    weight_in, weight_out, bias_out, time_out, cath_out
):
    count = held_ref.shape[0]
    slots = early_ref.shape[2] // 2
    wide = mod_weight_ref.shape[0]
    first, _ = chain_parts(early_ref)
    low = 2 * mod_weight_ref.shape[1] + pair_columns
    cond, times, slope = (first[:, low + k * wide : low + (k + 1) * wide] for k in range(3))
    arches = first[:, low + 3 * wide :]
    row = lax.broadcasted_iota(jnp.int32, (count, count), 0)
    column = lax.broadcasted_iota(jnp.int32, (count, count), 1)
    place = column // slots
    apart = (place % far_count) * 4 + place // far_count
    order = ((apart ^ here_ref[0]) * slots + column % slots == row).astype(BF16)
    late = (
        jnp.dot(order, held_ref[...], preferred_element_type=F32)
        + jnp.dot(order, near_ref[...], preferred_element_type=F32)
    ).astype(BF16)
    weight_out[...] = tn(cond, late)
    bias_out[...] = jnp.sum(late.astype(F32), axis=0, keepdims=True)
    d_cond = (nt(late, mod_weight_ref[...]) + d_cond_ref[...]) * slope.astype(F32)
    high = d_cond.astype(BF16)
    rest = (d_cond - high.astype(F32)).astype(BF16)
    time_out[...] = tn(times, high) + tn(times, rest)
    cath_out[...] = (tn(arches, high) + tn(arches, rest))[: cath_out.shape[0]]


def deliver_body(stays_ref, *refs):
    own_ref, came_ref, outs = refs[0], refs[1], refs[2:]

    def deliver(source):
        low = 0
        for ref in outs:
            ref[...] = source[:, low : low + ref.shape[1]]
            low += ref.shape[1]

    @pl.when(stays_ref[0] == 1)
    def _():
        deliver(own_ref)

    @pl.when(stays_ref[0] == 0)
    def _():
        deliver(came_ref)


def input_back_body(
    at_ref, d_proj_ref, x_ref, d_middle_ref, member_ref, mod_ref, own_ref, piece_0, piece_1,
    grad_ref, d_mods_ref, total_ref
):
    width = x_ref.shape[1]
    half = width // 2

    def product(weights, low):
        return sum(
            nt(d_proj_ref[:, j * width + low : j * width + low + half], weights[j])
            for j in range(3)
        )

    total_ref[...] = product(own_ref, 0)
    for r, piece in enumerate((piece_0, piece_1)):
        total_ref[:, columns_at(at_ref, r, half)] += product(piece, half)
    d_normed = total_ref[...]
    member = member_ref[...]
    scale = jnp.dot(member, mod_ref[:, width:], preferred_element_type=F32)
    x_hat, inverse = norm_parts(x_ref[...].astype(F32))
    slots = d_mods_ref.shape[0]
    d_mods_ref[:, :width] = tn(member, d_normed.astype(BF16))[:slots].astype(BF16)
    d_mods_ref[:, width:] = tn(member, (d_normed * x_hat).astype(BF16))[:slots].astype(BF16)
    d_hat = d_normed * (1.0 + scale)
    grad_ref[...] = (
        d_middle_ref[...]
        + inverse
        * (
            d_hat
            - jnp.mean(d_hat, axis=-1, keepdims=True)
            - x_hat * jnp.mean(d_hat * x_hat, axis=-1, keepdims=True)
        )
    ).astype(BF16)


ANYWHERE = pl.BlockSpec(memory_space=pl.ANY)
IN_SMEM = pl.BlockSpec(memory_space=pltpu.SMEM)


def call(body, operands, specs, outs, out_specs, scratch, flops, name, grid=(1,)):
    moved = sum(math.prod(a.shape) * a.dtype.itemsize for a in operands) + sum(
        math.prod(o.shape) * jnp.dtype(o.dtype).itemsize for o in outs
    )
    return pl.pallas_call(
        body,
        grid=grid,
        in_specs=specs,
        out_specs=out_specs,
        out_shape=outs,
        scratch_shapes=scratch,
        compiler_params=pltpu.CompilerParams(vmem_limit_bytes=VMEM_LIMIT),
        cost_estimate=pl.CostEstimate(
            flops=flops // COST_CUT, bytes_accessed=moved // COST_CUT, transcendentals=0
        ),
        name=name,
    )(*operands)


def added(first, second):
    return (first.astype(F32) + second.astype(F32)).astype(BF16)


def adder(cut, operands, shapes, name):
    def body(*refs):
        count = len(operands)
        for ref, value in zip(refs[count:], cut(*[ref[...] for ref in refs[:count]])):
            ref[...] = value

    outs = [shaped(shape) for shape in shapes]
    return call(
        body, operands, [whole(a) for a in operands], outs, [whole(a) for a in outs], [], 0, name
    )


def first_sum_body(keep_ref, far_ref, sent_a, rest_a, sent_b, rest_b):
    total = added(keep_ref[0], far_ref[0])
    rows, side = sent_a.shape[1:]
    rest_a[0], sent_a[0] = total[:rows, :side], total[rows:, :side]
    quarter = rows // 2
    for k in range(2):
        low = k * rows
        rest_b[0, k] = total[low : low + quarter, side:]
        sent_b[0, k] = total[low + quarter : low + rows, side:]


def shaped(shape, dtype=BF16):
    return jax.ShapeDtypeStruct(shape, dtype)


def make_moves(dp_count):
    def pairs(target):
        moved = []
        for d in range(dp_count):
            for m in range(2):
                to_d, to_m = target(d, m)
                if (to_d, to_m) != (d, m):
                    moved.append((d * 2 + m, to_d * 2 + to_m))
        return moved

    def mover(target):
        table = pairs(target)
        return lambda array: lax.ppermute(array, AXES, table)

    turn = mover(lambda d, m: ((d & ~1) | m, d & 1))
    turn_far = mover(lambda d, m: ((d & ~1) | m, 1 - (d & 1)))
    across = mover(lambda d, m: (d, 1 - m))

    def flip(bit):
        return mover(lambda d, m: (d ^ (1 << bit), m))

    def to(mask, over):
        return mover(lambda d, m: (d ^ mask, m ^ over))

    return turn, turn_far, across, flip, to


def shards(
    tokens,
    pair_left,
    pair_right,
    chain_len,
    chain_time,
    chain_arch,
    cath_table,
    time_weight,
    mod_weight,
    mod_bias,
    qkv_weight,
    pair_weight,
    out_weight,
    gate_up_weight,
    down_weight,
    cotangent,
):
    dp_count = lax.axis_size("dp")
    bits = dp_count.bit_length() - 1
    turn, turn_far, across, flip, to = make_moves(dp_count)
    core_swap = flip(0)
    dp_at = lax.axis_index("dp")
    mp_at = lax.axis_index("mp")
    core = dp_at & 1
    rows, width = tokens.shape
    slots = chain_len.shape[1]
    half_heads = pair_weight.shape[1]
    heads = 2 * half_heads
    pair_width = pair_left.shape[1]
    cond_width = time_weight.shape[0]
    half = width // 2
    hidden = down_weight.shape[0]

    def after(array, *earlier):
        return lax.optimization_barrier((array, *earlier))[0]

    def beside(made, *received):
        return lax.optimization_barrier((*made, *received))[: len(made)]

    held_chains = jnp.concatenate(
        [chain_len.astype(F32), chain_time, chain_arch.astype(F32)], axis=0
    )
    near_chains = core_swap(held_chains)

    cut = width // 2
    stays = core == mp_at

    def turned_in(array, *earlier):
        return jnp.where(stays, array, turn(after(array, *earlier)))

    pair_mix_other = across(pair_weight)
    x_in = turned_in(tokens)
    right_own = turned_in(pair_right, x_in)
    left_in = turned_in(pair_left, x_in)
    qkv_y = across(after(lax.dynamic_slice_in_dim(qkv_weight, core * cut, cut, 1), x_in))
    out_y = across(after(lax.dynamic_slice_in_dim(out_weight, core * cut, cut, 1), qkv_y))
    dout = turned_in(cotangent, out_y)
    dout_far = turn_far(after(cotangent, out_y))

    def ends_of(chains):
        return jnp.cumsum(chains[0].astype(jnp.int32))

    chains = jnp.where(core == mp_at, held_chains, near_chains)
    far_chains = jnp.where(core == mp_at, near_chains, held_chains)
    arches = chains[2].astype(jnp.int32)
    ends = ends_of(chains)
    times = jnp.concatenate([chains[1], far_chains[1]])

    def ids_of(part, ends=ends):
        positions = jnp.arange(rows, dtype=jnp.int32) + part * rows
        return jnp.sum((positions[:, None] >= ends[None, :]).astype(jnp.int32), axis=1)

    own_ids = ids_of(core)
    key_ids = jnp.concatenate([own_ids, ids_of(1 - core)])
    chain_numbers = jnp.arange(slots, dtype=jnp.int32)
    doubled = jnp.concatenate([chain_numbers, chain_numbers])[None, :]
    member = (own_ids[:, None] == doubled).astype(BF16)
    member_far = (ids_of(core, ends_of(far_chains))[:, None] == doubled).astype(BF16)
    lanes = jnp.arange(128, dtype=jnp.int32)[None, :] & 63
    hot = (own_ids[:, None] == lanes).astype(BF16)
    pens = jnp.where((key_ids[:, None] != lanes) & (lanes <= slots), -1e30, 0.0).astype(BF16)
    pen_own, pen_near = pens[:rows], pens[rows:]

    half_cond = cond_width // 2
    frequency = jnp.exp(jnp.arange(half_cond, dtype=F32) * (-math.log(10000.0) / half_cond))
    angles = times[:, None] * 1000.0 * frequency[None, :]
    time_embed = jnp.concatenate([jnp.sin(angles), jnp.cos(angles)], axis=1).astype(BF16)
    both_arches = jnp.concatenate([arches, far_chains[2].astype(jnp.int32)])
    arch_onehot = (
        both_arches[:, None] == jnp.arange(cath_table.shape[0], dtype=jnp.int32)[None, :]
    ).astype(F32)
    cond_pre = dot_f32(time_embed, time_weight) + highest_dot(arch_onehot, cath_table.astype(F32))
    cond_value, cond_slope = silu_parts(cond_pre)
    cond_act = cond_value.astype(BF16)
    chain_mod = dot_f32(cond_act, mod_weight) + mod_bias.astype(F32)[None, :]
    mod_high = lax.reduce_precision(chain_mod, 8, 7)
    mod_low = (chain_mod - mod_high).astype(BF16)
    mod_high = mod_high.astype(BF16)
    mods = jnp.concatenate([mod_high[:slots], mod_low[:slots]], axis=0)
    gate_far = jnp.concatenate([mod_high[slots:], mod_low[slots:]], axis=0)[:, 5 * width :]
    arch_low = (arches[:, None] == jnp.arange(128, dtype=jnp.int32)[None, :]).astype(BF16)
    info = jnp.concatenate(
        [cond_act[:slots], time_embed[:slots], cond_slope[:slots].astype(BF16), arch_low], axis=1
    )

    order = [int(format(p, "0%db" % bits)[::-1], 2) for p in range(dp_count)]
    block_at = jnp.array(order, jnp.int32) ^ dp_at
    block_rows = width // dp_count
    source = (block_at[:, None] * block_rows + jnp.arange(block_rows)[None, :]).reshape(-1)
    moved = (source[:, None] == jnp.arange(width)[None, :]).astype(BF16)
    at = core.reshape(1).astype(jnp.int32)
    semaphores = pltpu.SemaphoreType.DMA

    mod_a = mods[:, : 2 * width]
    pair_mix = jnp.concatenate([pair_weight, pair_mix_other], axis=1).astype(F32)
    mix_rows = jnp.transpose(pair_mix).reshape(half_heads, 2, -1)
    part_shape = shaped((rows, half))
    operands = [after(x_in, moved, mods, hot, pens, member_far, gate_far, mix_rows, info), member, mod_a,
                qkv_weight]
    made = call(
        qkv_body,
        operands,
        [whole(a) for a in operands],
        [part_shape, shaped((rows, width)), shaped((rows, width))],
        [whole(part_shape), whole(shaped((rows, width))), whole(shaped((rows, width)))],
        [],
        3 * rows * width * width,
        "project",
    )
    queries, kv_own, normed_a = beside(made, right_own, left_in)
    kv_near, right_near = core_swap(kv_own), core_swap(right_own)
    factors = (right_own, right_near, pen_own, pen_near)
    made = attention_forward(0, mix_rows, queries, left_in, hot, kv_own, kv_near, *factors)
    made = beside(made, qkv_y)
    qkv_y = after(qkv_y, made[0])
    qkv_pieces = [qkv_y, core_swap(qkv_y)]
    first_half = (*made, queries, kv_own, kv_near)
    made = call(
        qkv_other_body,
        [at, after(normed_a, made[0]), *qkv_pieces],
        [IN_SMEM, whole(normed_a), whole(qkv_y), whole(qkv_y)],
        [part_shape, shaped((rows, width))],
        [whole(part_shape), whole(shaped((rows, width)))],
        [],
        3 * rows * width * width,
        "project_other",
    )
    queries, kv_own = beside(made, out_y)
    out_pieces = [out_y, core_swap(out_y)]
    kv_near = core_swap(kv_own)
    made = attention_forward(1, mix_rows, queries, left_in, hot, kv_own, kv_near, *factors)
    made = beside(made, *out_pieces)
    second_half = (*made, queries, kv_own, kv_near)
    attended, attended_other = first_half[0], second_half[0]
    wide = shaped((rows, width), F32)
    thin = shaped((rows, width))
    middle, branch, normed_f = call(
        branch_body,
        [at, attended, attended_other, out_weight, *out_pieces, x_in, member, mods],
        [IN_SMEM]
        + [whole(a) for a in (attended, attended_other, out_weight, *out_pieces, x_in, member, mods)],
        [wide, wide, thin],
        [whole(thin)] * 3,
        [],
        2 * rows * width * width,
        "branch",
    )

    normed_far = across(normed_f)
    gate_mod = mods[:, 5 * width :]
    block = FFN_BLOCK
    active = shaped((rows, hidden))
    turned = shaped((width, rows))

    def feed_forward(normed, dout, member, gate, sum_type):
        column = pl.BlockSpec((rows, block), lambda i: (0, i))
        summed = shaped((rows, width), sum_type)
        part = shaped((rows // 2, width), sum_type)
        return call(
            ffn_body,
            [normed, dout, member, gate, moved, gate_up_weight, down_weight],
            [whole(a) for a in (normed, dout, member, gate, moved)]
            + [
                pl.BlockSpec((2, width, block), lambda i: (0, 0, i)),
                pl.BlockSpec((block, width), lambda i: (i, 0)),
            ],
            [summed, part, part, turned, turned, active, active, active],
            [whole(thin), whole(part), whole(part), whole(turned), whole(turned), column, column, column],
            [
                pltpu.VMEM((rows, width), F32), pltpu.VMEM((rows, width), F32),
                pltpu.VMEM((rows, width), BF16),
            ],
            12 * rows * width * hidden,
            "feed_forward",
            (hidden // block,),
        )

    made = feed_forward(normed_f, dout, member, gate_mod, F32)
    ffn, d_normed_top, d_normed_low, normed_t, d_ffn_t, d_gate, d_up, hid = made
    normed_far, dout_far = lax.optimization_barrier((normed_far, dout_far, *made))[:2]
    ffn_for, top_for, low_for, normed_t_far, d_ffn_t_far, d_gate_far, d_up_far, hid_far = feed_forward(
        normed_far, dout_far, member_far, gate_far, BF16
    )
    top_far, low_far = across(top_for), across(low_for)

    grad = shaped((3, half, hidden))
    grad_block = pl.BlockSpec((3, half, GRAD_BLOCK), lambda i: (0, 0, i))
    column = pl.BlockSpec((rows, GRAD_BLOCK), lambda i: (0, i))
    turned_half = [normed_t, normed_t_far, d_ffn_t, d_ffn_t_far]
    sides = [d_gate, d_gate_far, d_up, d_up_far, hid, hid_far]

    def ffn_grads(part, *earlier):
        row_half = pl.BlockSpec((half, rows), lambda i: (part, 0))
        return call(
            ffn_grad_body,
            [after(turned_half[0], *earlier), *turned_half[1:], *sides],
            [row_half] * 4 + [column] * 6,
            [grad],
            [grad_block],
            [],
            6 * rows * width * hidden,
            "feed_forward_grads",
            (hidden // GRAD_BLOCK,),
        )[0]

    (send,) = beside((ffn_grads(1),), top_far)
    far = core_swap(send)
    (keep,) = beside((ffn_grads(0, send),), far, low_far)
    ffn_far = across(after(ffn_for, keep))

    def plus(kept, received):
        return (kept.astype(F32) + received.astype(F32)).astype(BF16)

    def halves(array, upper):
        size = array.shape[-2] // 2
        return array[..., size:, :] if upper else array[..., :size, :]

    def y_part(kept, received):
        return plus(kept[1], received[1])

    def y_rest(kept, received):
        return plus(kept[0], received[0])

    def bit_part(kept, received):
        return plus(halves(kept, True), halves(received, True))

    def bit_rest(kept, received):
        return plus(halves(kept, False), halves(received, False))

    steps = 2
    row_block = pl.BlockSpec((rows // steps, width), lambda i: (i, 0))
    member_block = pl.BlockSpec((rows // steps, 2 * slots), lambda i: (i, 0))
    mods_early = shaped((2 * slots, 3 * width), F32)
    made = call(
        middle_back_body,
        [at, after(d_normed_top, keep), d_normed_low, top_far, low_far, middle, branch, dout,
         member, mods, out_weight, *out_pieces],
        [IN_SMEM] + [whole(d_normed_top)] * 4 + [row_block] * 3
        + [member_block, whole(mods), whole(out_weight), whole(out_y), whole(out_y)],
        [wide, thin, thin, mods_early],
        [row_block, row_block, row_block, whole(mods_early)],
        [],
        4 * rows * width * width,
        "middle_back",
        (steps,),
    )
    d_middle, d_attended, d_attn, d_mods = made
    side = hidden // 2
    shape_a, shape_b = (3, half // 2, side), (3, 2, half // 4, side)
    block_a = pl.BlockSpec((1, *shape_a[1:]), lambda i: (i, 0, 0))
    block_b = pl.BlockSpec((1, *shape_b[1:]), lambda i: (i, 0, 0, 0))
    sent, rest, sent_b, rest_b = call(
        first_sum_body,
        [keep, far],
        [pl.BlockSpec((1, half, hidden), lambda i: (i, 0, 0))] * 2,
        [shaped(shape_a), shaped(shape_a), shaped(shape_b), shaped(shape_b)],
        [block_a, block_a, block_b, block_b],
        [],
        0,
        "first_sum",
        (3,),
    )
    got, got_b = flip(1)(sent), flip(2)(sent_b)

    def finish(bit, kept, sent):
        while bit < bits:
            received = flip(bit)(sent)
            bit += 1
            if bit < bits:
                kept, sent = bit_rest(kept, received), bit_part(kept, received)
        return kept.astype(F32) + received.astype(F32)

    near_bits = [-1, 1] if bits > 1 else [-1]
    far_bits = list(range(2, bits))

    def several(group):
        moves = []
        for chosen in range(1, 1 << len(group)):
            mask, over = 0, 0
            for k, bit in enumerate(group):
                if chosen >> k & 1:
                    mask, over = (mask, 1) if bit < 0 else (mask | 1 << bit, over)
            moves.append((mask, over))
        return moves

    def gather_step(group, held):
        return jnp.concatenate(
            [held] + [to(mask, over)(held) for mask, over in several(group)], axis=0
        )

    made = attention_backward(
        mix_rows, after(d_attended, sent, sent_b), (first_half, second_half), left_in, *factors
    )
    d_query, d_own, d_far, d_left = beside(made[:4], ffn_far, got, got_b)

    def second_cut(rest, got, rest_b, got_b):
        total, total_b = added(rest, got), added(rest_b, got_b)
        rows = total.shape[1] // 2
        return total[:, rows:], total[:, :rows], total_b[:, 1], total_b[:, 0]

    shape = (3, half // 4, side)
    sent, rest, sent_b, rest_b = adder(
        second_cut, [rest, got, rest_b, got_b], [shape] * 4, "second_sum"
    )
    got, got_b = flip(2)(sent), flip(1)(sent_b)
    d_mix = made[4]
    far_kv = core_swap(d_far)

    known = shaped((slots, 4 * width + d_mix.shape[1] + info.shape[1]))
    mixed, known = call(
        mix_body,
        [after(middle, d_far, sent, sent_b), ffn, ffn_far, dout, member, gate_mod, d_mods, d_mix,
         info],
        [row_block] * 4 + [member_block] + [whole(a) for a in (gate_mod, d_mods, d_mix, info)],
        [thin, known],
        [row_block, whole(known)],
        [pltpu.VMEM((2 * slots, width), F32)],
        4 * rows * 16 * width,
        "mix",
        (steps,),
    )
    mixed, known = beside((mixed, known), far_kv)
    mixed_own, mixed = mixed, turn(mixed)
    early = lax.all_gather(known, AXES, axis=0, tiled=False)

    proj_grad = shaped((rows, 3 * width))
    back = shaped((rows, 2 * pair_width))
    grad = shaped((2, 4, half, half))
    operands = [d_query, d_own, far_kv, d_left, after(normed_a, known), d_attn, attended,
                attended_other, moved]
    outs = [proj_grad, back, grad, grad]
    made = call(
        attention_grad_body,
        operands,
        [whole(a) for a in operands],
        outs,
        [whole(a) for a in outs],
        [],
        12 * rows * width * width,
        "attention_grads",
    )
    d_proj, back, keep_qkvo, send_qkvo = beside(made, got, got_b, mixed)
    far_qkvo = core_swap(send_qkvo)
    back_own, back = back, turn(back)

    def third_cut(rest, got, rest_b, got_b):
        total = jnp.concatenate([added(rest, got), added(rest_b, got_b)], axis=2)
        rows = total.shape[1] // 2
        return total[:, rows:], total[:, :rows]

    shape = (3, half // 8, hidden)
    sent, rest = adder(third_cut, [rest, got, rest_b, got_b], [shape] * 2, "third_sum")

    def qkvo_cut(keep, far):
        total = added(keep, far)
        rows = half // 2
        return total[1, :2], total[0, :2], total[:, 2:, rows:], total[:, 2:, :rows]

    shape, shape_vo = (2, half, half), (2, 2, half // 2, half)
    sent_qk, rest_qk, sent_vo, rest_vo = adder(
        qkvo_cut, [keep_qkvo, far_qkvo], [shape, shape, shape_vo, shape_vo], "qkvo_sum"
    )
    got_qk, got_vo = across(sent_qk), flip(1)(sent_vo)
    mods_late = shaped((slots, 2 * width))
    operands = [at, after(d_proj, sent_qk, sent_vo, sent), x_in, d_middle, member, mod_a,
                qkv_weight, *qkv_pieces]
    made = call(
        input_back_body,
        operands,
        [IN_SMEM] + [whole(a) for a in operands[1:]],
        [thin, mods_late],
        [whole(thin), whole(mods_late)],
        [pltpu.VMEM((rows, width), F32)],
        6 * rows * width * width,
        "input_back",
    )
    tokens_out, held = beside(made, got_qk, got_vo, back)
    token_gradient = turn(tokens_out)
    got = flip(3)(sent)

    def together(*arrays):
        return lax.optimization_barrier(arrays)

    def qkvo_second(rest_qk, got_qk, rest_vo, got_vo):
        total, total_vo = added(rest_qk, got_qk), added(rest_vo, got_vo)
        rows = half // 2
        return total[:, rows:], total[:, :rows], total_vo[1], total_vo[0]

    shape = (2, half // 2, half)
    sent_qk, rest_qk, sent_vo, rest_vo = adder(
        qkvo_second, [after(rest_qk, tokens_out), got_qk, rest_vo, got_vo], [shape] * 4, "qkvo_second"
    )
    got_qk, got_vo = flip(1)(sent_qk), across(sent_vo)
    held = gather_step(far_bits, held)

    def qkvo_third(rest_qk, got_qk, rest_vo, got_vo):
        total = jnp.concatenate([added(rest_qk, got_qk), added(rest_vo, got_vo)], axis=0)
        rows = half // 4
        return total[:, rows:], total[:, :rows]

    shape = (4, half // 4, half)
    sent_qkvo, qkvo = adder(
        qkvo_third, [rest_qk, got_qk, rest_vo, got_vo], [shape] * 2, "qkvo_third"
    )
    held, qkvo, sent_qkvo = together(held, qkvo, sent_qkvo)
    held = gather_step(near_bits, held)
    got_qkvo = flip(2)(sent_qkvo)
    held, got_qkvo, token_gradient = together(held, got_qkvo, token_gradient)
    near = core_swap(held)
    sent_qkvo, qkvo = bit_part(qkvo, got_qkvo), bit_rest(qkvo, got_qkvo)
    got_qkvo = flip(3)(sent_qkvo)

    if bits > 4:
        ffn_sum = finish(4, bit_rest(rest, got), bit_part(rest, got))
    else:
        ffn_sum = rest.astype(F32) + got.astype(F32)
    down_sum = jnp.transpose(ffn_sum[2])
    ffn_sum = ffn_sum[:2]
    stay_flag = stays.reshape(1).astype(jnp.int32)

    def delivered(own, came, widths):
        blocks = [pl.BlockSpec((rows // 2, w), lambda i: (i, 0)) for w in [own.shape[1]] * 2 + widths]
        return call(
            deliver_body,
            [stay_flag, own, came],
            [IN_SMEM, *blocks[:2]],
            [shaped((rows, w)) for w in widths],
            blocks[2:],
            [],
            0,
            "deliver",
            (2,),
        )

    here = ((dp_at >> 1) * 2 + mp_at).reshape(1).astype(jnp.int32)
    early = early.reshape(dp_count // 2, 2, 2 * slots, -1)
    late_to = 2 * width
    weight_shape = shaped(mod_weight.shape, F32)
    bias_shape = shaped((1, 6 * width), F32)
    cond_shape = shaped((dp_count * slots, cond_width), F32)
    mix_shape = shaped((half_heads // 2, 2 * pair_width), F32)
    later = lambda i: (0, 1 + i)
    early = after(early, tokens_out)
    early_weight, early_bias, early_cond, mix_sum = call(
        early_chain_body,
        [here, early, mod_weight],
        [IN_SMEM, whole(early), pl.BlockSpec((cond_width, late_to), later)],
        [weight_shape, bias_shape, cond_shape, mix_shape],
        [
            pl.BlockSpec((cond_width, late_to), later), pl.BlockSpec((1, late_to), later),
            whole(cond_shape), whole(mix_shape),
        ],
        [],
        0,
        "early_chains",
        (2,),
    )
    (mixed,) = delivered(mixed_own, after(mixed, early_weight), [width])
    left_grad, right_grad = delivered(back_own, after(back, mixed), [pair_width, pair_width])
    mix_sum = mix_sum.reshape(half_heads, -1)
    taken = mix_sum.shape[1] // dp_count
    pair_sum = jnp.transpose(lax.dynamic_slice_in_dim(mix_sum, dp_at * taken, taken, 1))
    late_bias_shape = shaped((1, late_to), F32)
    token_gradient = delivered(
        tokens_out, after(token_gradient, near, ffn_sum, down_sum, pair_sum, right_grad), [width]
    )[0]
    operands = [here, early, after(held, token_gradient), near]
    time_shape, cath_shape = shaped((cond_width, cond_width), F32), shaped(cath_table.shape, F32)
    first_columns = pl.BlockSpec((cond_width, late_to), lambda i: (0, 0))
    mod_weight_sum, late_bias, time_sum, cath_sum = pl.pallas_call(
        functools.partial(late_chain_body, dp_count // 4, mix_shape.shape[1]),
        grid=(1,),
        in_specs=[IN_SMEM]
        + [whole(a) for a in operands[1:]]
        + [first_columns, whole(cond_shape), ANYWHERE],
        out_specs=[first_columns, whole(late_bias_shape), whole(time_shape), whole(cath_shape)],
        out_shape=[weight_shape, late_bias_shape, time_shape, cath_shape],
        input_output_aliases={6: 0},
        compiler_params=pltpu.CompilerParams(vmem_limit_bytes=VMEM_LIMIT),
        name="late_chains",
    )(*operands, mod_weight, early_cond, early_weight)
    mod_bias_sum = jnp.concatenate([late_bias[0], early_bias[0, late_to:]])

    got_qkvo, _ = together(got_qkvo, mod_weight_sum)
    if bits > 4:
        qkvo_sum = finish(4, bit_rest(qkvo, got_qkvo), bit_part(qkvo, got_qkvo))
    else:
        qkvo_sum = qkvo.astype(F32) + got_qkvo.astype(F32)

    return (
        mixed,
        token_gradient,
        left_grad,
        right_grad,
        cath_sum,
        time_sum,
        mod_weight_sum,
        mod_bias_sum,
        qkvo_sum[:3],
        pair_sum,
        jnp.transpose(qkvo_sum[3]),
        ffn_sum,
        down_sum,
    )


def solution(mesh):
    by_rows = P(AXES, None)
    placed = (
        by_rows,
        by_rows,
        by_rows,
        P("dp", None),
        P("dp", None),
        P("dp", None),
        P(),
        P(),
        P(),
        P(),
        P(None, None, "mp"),
        P(None, "mp"),
        P("mp", None),
        P(None, None, "mp"),
        P("mp", None),
        by_rows,
    )
    return jax.shard_map(
        shards,
        mesh=mesh,
        in_specs=placed,
        out_specs=(
            by_rows,
            by_rows,
            by_rows,
            by_rows,
            P(),
            P(),
            P(),
            P(),
            P(None, "dp", "mp"),
            P("dp", "mp"),
            P("mp", "dp"),
            P(None, "dp", "mp"),
            P("mp", "dp"),
        ),
        check_vma=False,
    )
```

```python
import functools
import math

import jax
import jax.numpy as jnp
from jax import lax
from jax.experimental import pallas as pl
from jax.experimental.pallas import tpu as pltpu
from jax.sharding import PartitionSpec as P

EPSILON = 1e-06
AXES = ("dp", "mp")
BF16 = jnp.bfloat16
F32 = jnp.float32
VMEM_LIMIT = 64 * 1024 * 1024
FFN_BLOCK = 512
GRAD_BLOCK = 768
BACK_PARTS = 1
COST_CUT = 20


def highest_dot(left_side, right_side):
    return jnp.dot(left_side, right_side, precision=lax.Precision.HIGHEST)


def silu_parts(values):
    sigma = jax.nn.sigmoid(values)
    return (values * sigma, sigma * (1.0 + values * (1.0 - sigma)))


def dot_f32(left_side, right_side):
    return jnp.dot(left_side, right_side, preferred_element_type=F32)


def dot_nt(left_side, right_side):
    return lax.dot_general(
        left_side, right_side, (((1,), (1,)), ((), ())), preferred_element_type=F32
    )

def lane_mix(first, second, odd):
    lane = lax.broadcasted_iota(jnp.int32, first.shape, 1)
    keep = (lane >= 64) if odd else (lane < 64)
    return jnp.where(keep, first, second)


def nt(left_side, right_side):
    return lax.dot_general(
        left_side, right_side, (((1,), (1,)), ((), ())), preferred_element_type=F32
    )


def attention_forward_body(
    pair_mix_ref, q_ref, left_ref, hot_ref, k_own_ref, k_near_ref, v_own_ref, v_near_ref,
    right_own_ref, right_near_ref, pen_own_ref, pen_near_ref,
    attended_ref, inverse_ref, probs_ref,
):
    rows = q_ref.shape[0]
    step = 256
    out_tiles = []
    left = left_ref[...].astype(F32)
    for odd in range(2):
        mix = pair_mix_ref[0, odd : odd + 1, :]
        left_mixed = (left * mix).astype(BF16)
        q_side = jnp.concatenate([left_mixed, lane_mix(q_ref[...], hot_ref[...], odd)], axis=1)
        k_own = jnp.concatenate(
            [right_own_ref[...], lane_mix(k_own_ref[...], pen_own_ref[...], odd)], axis=1
        )
        k_near = jnp.concatenate(
            [right_near_ref[...], lane_mix(k_near_ref[...], pen_near_ref[...], odd)], axis=1
        )
        v_own = lane_mix(v_own_ref[...], jnp.ones_like(v_own_ref[...]), odd)
        v_near = lane_mix(v_near_ref[...], jnp.ones_like(v_near_ref[...]), odd)
        tiles = []
        for start in range(0, rows, step):
            block = q_side[start : start + step]
            s_own = nt(block, k_own)
            s_near = nt(block, k_near)
            top = jnp.maximum(
                jnp.max(s_own, axis=1, keepdims=True), jnp.max(s_near, axis=1, keepdims=True)
            )
            e_own = jnp.exp(s_own - top).astype(BF16)
            e_near = jnp.exp(s_near - top).astype(BF16)
            probs_ref[odd, start : start + step, :rows] = e_own
            probs_ref[odd, start : start + step, rows:] = e_near
            tiles.append(
                jnp.dot(e_own, v_own, preferred_element_type=F32)
                + jnp.dot(e_near, v_near, preferred_element_type=F32)
            )
        out_tiles.append(jnp.concatenate(tiles, axis=0))
    sums = lane_mix(out_tiles[1], out_tiles[0], False)
    sums = pltpu.roll(sums, 64, 1)
    inverse = 1.0 / sums
    attended_ref[...] = (lane_mix(out_tiles[0], out_tiles[1], False) * inverse).astype(BF16)
    inverse_ref[...] = inverse


def attention_backward_body(
    pair_mix_ref, grad_ref, left_ref, right_own_ref, right_near_ref, pen_own_ref, pen_near_ref,
    *rest
):
    outs = rest[16:21]
    scores_ref, right_sum_ref, left_sum_ref, left_t_ref = rest[21:]
    pair = pl.program_id(0)
    pairs = pl.num_programs(0)

    @pl.when(pair == 0)
    def _():
        left_t_ref[...] = left_ref[...].T
        outs[4][...] = jnp.zeros_like(outs[4])
        right_sum_ref[...] = jnp.zeros_like(right_sum_ref)
        left_sum_ref[...] = jnp.zeros_like(left_sum_ref)

    common = (
        pair_mix_ref, grad_ref, left_ref, right_own_ref, right_near_ref, pen_own_ref, pen_near_ref,
        *outs, *rest[21:],
    )

    @pl.when(pair < pairs // 2)
    def _():
        attention_backward_pair(common, *rest[:8])

    @pl.when(pair >= pairs // 2)
    def _():
        attention_backward_pair(common, *rest[8:16])

    @pl.when(pair == pairs - 1)
    def _():
        rows = left_ref.shape[0]
        right = right_sum_ref[...].T.astype(BF16)
        outs[1][:, outs[1].shape[1] - right.shape[1] :] = right[:rows]
        outs[2][:, outs[1].shape[1] - right.shape[1] :] = right[rows:]
        outs[3][...] = left_sum_ref[...].astype(BF16)


def attention_backward_pair(
    common, attended_ref, inverse_ref, probs_ref, q_ref, k_own_ref, k_near_ref, v_own_ref,
    v_near_ref
):
    (
        pair_mix_ref, grad_ref, left_ref, right_own_ref, right_near_ref, pen_own_ref, pen_near_ref,
        d_q_ref, own_out, near_out, _, d_mix_ref,
        scores_ref, right_sum_ref, left_sum_ref, left_t_ref,
    ) = common
    pair = pl.program_id(0)
    rows = q_ref.shape[0]
    step = 256
    wide = grad_ref.shape[1] * pl.num_programs(0)
    scaled = (grad_ref[...].astype(F32) * inverse_ref[...]).astype(BF16)
    products = scaled.astype(F32) * attended_ref[...].astype(F32)
    scaled_t = scaled.T
    q_t = q_ref[...].T
    lane = lax.broadcasted_iota(jnp.int32, products.shape, 1)
    left = left_ref[...].astype(F32)
    left_t = left_t_ref[...].astype(F32)
    d_q, dk_t, dv_t = [], [], []
    for odd in range(2):
        mine = (lane >= 64) if odd else (lane < 64)
        delta = -jnp.sum(jnp.where(mine, products, 0.0), axis=1, keepdims=True)
        high = delta.astype(BF16).astype(F32)
        low = delta - high
        at = 0 if odd else 64
        extra = jnp.where(lane == at, high, jnp.where(lane == at + 1, low, 0.0)).astype(BF16)
        grad_side = jnp.where(mine, scaled, extra)
        mix = pair_mix_ref[0, odd : odd + 1, :]
        k_own = jnp.concatenate(
            [right_own_ref[...], lane_mix(k_own_ref[...], pen_own_ref[...], odd)], axis=1
        )
        k_near = jnp.concatenate(
            [right_near_ref[...], lane_mix(k_near_ref[...], pen_near_ref[...], odd)], axis=1
        )
        v_own = lane_mix(v_own_ref[...], jnp.ones_like(v_own_ref[...]), odd)
        v_near = lane_mix(v_near_ref[...], jnp.ones_like(v_near_ref[...]), odd)
        for start in range(0, rows, step):
            block = grad_side[start : start + step]
            own = nt(block, v_own).astype(BF16) * probs_ref[odd, start : start + step, :rows]
            near = nt(block, v_near).astype(BF16) * probs_ref[odd, start : start + step, rows:]
            scores_ref[start : start + step, :rows] = own
            scores_ref[start : start + step, rows:] = near
        d_query = jnp.dot(
            scores_ref[:, :rows], k_own, preferred_element_type=F32
        ) + jnp.dot(scores_ref[:, rows:], k_near, preferred_element_type=F32)
        width = left.shape[1]
        d_q.append(d_query[:, width:])
        d_pair = d_query[:, :width]
        left_sum_ref[...] += d_pair * mix
        d_mix_ref[pl.ds(pair, 1), odd * width : (odd + 1) * width] = jnp.sum(
            d_pair * left, axis=0, keepdims=True
        )
        mixed_t = (left_t * jnp.transpose(mix)).astype(BF16)
        low_row = 64 * odd
        q_side = jnp.concatenate([mixed_t, q_t[low_row : low_row + 64]], axis=0)
        d_key = jnp.dot(q_side, scores_ref[...], preferred_element_type=F32)
        right_sum_ref[...] += d_key[:width]
        dk_t.append(d_key[width:])
        dv_t.append(
            jnp.dot(
                scaled_t[low_row : low_row + 64], probs_ref[odd], preferred_element_type=F32
            )
        )
    d_q_ref[...] = (lane_mix(d_q[0], d_q[1], False) * 0.125).astype(BF16)
    for base, parts in ((0, dk_t), (wide, dv_t)):
        both = jnp.concatenate(parts, axis=0).T.astype(BF16)
        column = pl.multiple_of(base + pair * 128, 128)
        own_out[:, pl.ds(column, 128)] = both[:rows]
        near_out[:, pl.ds(column, 128)] = both[rows:]


def whole(array):
    zeros = (0,) * array.ndim
    return pl.BlockSpec(array.shape, lambda *_: zeros)


def attention_forward(
    part, pair_mix, queries, left, hot, kv_own, kv_near, right_own, right_near, pen_own, pen_near
):
    rows, width = queries.shape
    pairs = width // 128
    pair_width = left.shape[1]
    column = pl.BlockSpec((rows, 128), lambda p: (0, p))
    value_column = pl.BlockSpec((rows, 128), lambda p: (0, pairs + p))
    operands = [
        pair_mix, queries, left, hot, kv_own, kv_near, kv_own, kv_near, right_own, right_near,
        pen_own, pen_near,
    ]
    return call(
        attention_forward_body,
        operands,
        [
            pl.BlockSpec((1, 2, pair_width), lambda p: (part * pairs + p, 0, 0)), column,
            whole(left), whole(hot), column, column, value_column, value_column,
            whole(right_own), whole(right_near), whole(pen_own), whole(pen_near),
        ],
        [
            shaped((rows, width)), shaped((rows, width), F32),
            shaped((2 * pairs, rows, 2 * rows)),
        ],
        [column, column, pl.BlockSpec((2, rows, 2 * rows), lambda p: (p, 0, 0))],
        [],
        2 * 2 * pairs * rows * 2 * rows * 512,
        "attention_forward",
        (pairs,),
    )


def attention_backward(
    pair_mix, grad, halves, left, right_own, right_near, pen_own, pen_near
):
    rows, width = grad.shape
    pairs = width // 128
    here = pairs // 2
    pair_width = left.shape[1]
    column = pl.BlockSpec((rows, 128), lambda p: (0, p))
    mix = pl.BlockSpec((1, 2, pair_width), lambda p: (p, 0, 0))
    both = shaped((rows, 2 * width + pair_width))
    operands = [pair_mix, grad, left, right_own, right_near, pen_own, pen_near]
    specs = [mix, column] + [whole(a) for a in operands[2:]]
    for part, (attended, inverse, probs, queries, kv_own, kv_near) in enumerate(halves):
        at = lambda p, part=part: jnp.clip(p - part * here, 0, here - 1)
        own = pl.BlockSpec((rows, 128), lambda p, at=at: (0, at(p)))
        value = pl.BlockSpec((rows, 128), lambda p, at=at: (0, here + at(p)))
        operands += [attended, inverse, probs, queries, kv_own, kv_near, kv_own, kv_near]
        specs += [
            own, own, pl.BlockSpec((2, rows, 2 * rows), lambda p, at=at: (at(p), 0, 0)), own, own,
            own, value, value,
        ]
    outs = [
        shaped((rows, width)), both, both, shaped((rows, pair_width)),
        shaped((8, 2 * pair_width), F32),
    ]
    return call(
        attention_backward_body,
        operands,
        specs,
        outs,
        [column, whole(both), whole(both), whole(outs[3]), whole(outs[4])],
        [
            pltpu.VMEM((rows, 2 * rows), BF16),
            pltpu.VMEM((pair_width, 2 * rows), F32),
            pltpu.VMEM((rows, pair_width), F32),
            pltpu.VMEM((pair_width, rows), BF16),
        ],
        2 * 2 * pairs * rows * 2 * rows * 1000,
        "attention_backward",
        (pairs,),
    )


def norm_parts(values):
    centered = values - jnp.mean(values, axis=-1, keepdims=True)
    inverse = lax.rsqrt(jnp.mean(centered * centered, axis=-1, keepdims=True) + EPSILON)
    return centered * inverse, inverse


def tn(left_side, right_side):
    return lax.dot_general(
        left_side, right_side, (((0,), (0,)), ((), ())), preferred_element_type=F32
    )


def qkv_body(x_ref, member_ref, mod_ref, own_ref, q_ref, kv_ref, normed_ref):
    width = x_ref.shape[1]
    half = width // 2
    mods = jnp.dot(member_ref[...], mod_ref[...], preferred_element_type=F32)
    x_hat, _ = norm_parts(x_ref[...].astype(F32))
    normed = (x_hat * (1.0 + mods[:, width:]) + mods[:, :width]).astype(BF16)
    normed_ref[...] = normed
    q = jnp.dot(normed, own_ref[0], preferred_element_type=F32).astype(BF16)
    q_ref[...] = (q.astype(F32) * 0.125).astype(BF16)
    for k in (1, 2):
        kv_ref[:, (k - 1) * half : k * half] = jnp.dot(
            normed, own_ref[k], preferred_element_type=F32
        ).astype(BF16)


def columns_at(at_ref, r, size):
    return pl.ds(pl.multiple_of((at_ref[0] ^ r) * size, size), size)


def qkv_other_body(at_ref, normed_ref, piece_0, piece_1, q_ref, kv_ref):
    half = normed_ref.shape[1] // 2
    sides = [(normed_ref[:, columns_at(at_ref, r, half)], p) for r, p in enumerate((piece_0, piece_1))]

    def product(k):
        return sum(
            jnp.dot(side, piece[k], preferred_element_type=F32) for side, piece in sides
        ).astype(BF16)

    q_ref[...] = (product(0).astype(F32) * 0.125).astype(BF16)
    for k in (1, 2):
        kv_ref[:, (k - 1) * half : k * half] = product(k)


def branch_body(
    at_ref, attended_ref, attended_other_ref, own_ref, piece_0, piece_1, x_ref, member_ref, mod_ref,
    middle_ref, branch_ref, normed_ref
):
    width = x_ref.shape[1]
    half = width // 2
    member = member_ref[...]

    def mods(k):
        return jnp.dot(
            member, mod_ref[:, k * width : (k + 1) * width], preferred_element_type=F32
        )

    branch_ref[...] = jnp.dot(attended_ref[...], own_ref[...], preferred_element_type=F32)
    for r, piece in enumerate((piece_0, piece_1)):
        branch_ref[:, columns_at(at_ref, r, half)] += jnp.dot(
            attended_other_ref[...], piece[...], preferred_element_type=F32
        )
    branch = branch_ref[...]
    middle = x_ref[...].astype(F32) + mods(2) * branch
    middle_ref[...] = middle
    m_hat, _ = norm_parts(middle)
    normed_ref[...] = (m_hat * (1.0 + mods(4)) + mods(3)).astype(BF16)


def ffn_body(
    normed_ref, dout_ref, member_ref, mod_ref, moved_ref, gate_up_ref, down_ref,
    ffn_out_ref, d_normed_top_ref, d_normed_low_ref, normed_t_ref, d_ffn_t_ref, d_gate_ref,
    d_up_ref, hidden_ref, ffn_ref, d_normed_ref, d_ffn_ref,
):
    step = pl.program_id(0)
    last = pl.num_programs(0) - 1

    @pl.when(step == 0)
    def _():
        scale = jnp.dot(member_ref[...], mod_ref[...], preferred_element_type=F32)
        d_ffn_ref[...] = (scale * dout_ref[...].astype(F32)).astype(BF16)
        normed_t_ref[...] = nt(moved_ref[...], normed_ref[...]).astype(BF16)
        d_ffn_t_ref[...] = nt(moved_ref[...], d_ffn_ref[...]).astype(BF16)

    normed, d_ffn = normed_ref[...], d_ffn_ref[...]
    w_gate, w_up, w_down = gate_up_ref[0], gate_up_ref[1], down_ref[...]
    gate = jnp.dot(normed, w_gate, preferred_element_type=F32)
    up = jnp.dot(normed, w_up, preferred_element_type=F32)
    d_hidden = nt(d_ffn, w_down)
    sigma = jax.nn.sigmoid(gate)
    value = gate * sigma
    hid = (value * up).astype(BF16)
    d_up = (d_hidden * value).astype(BF16)
    d_gate = (d_hidden * up * (sigma + value * (1.0 - sigma))).astype(BF16)
    hidden_ref[...] = hid
    d_up_ref[...] = d_up
    d_gate_ref[...] = d_gate
    ffn = jnp.dot(hid, w_down, preferred_element_type=F32)
    d_normed = nt(d_gate, w_gate) + nt(d_up, w_up)

    @pl.when(step == 0)
    def _():
        ffn_ref[...] = ffn
        d_normed_ref[...] = d_normed

    @pl.when(jnp.logical_and(step > 0, step < last))
    def _():
        ffn_ref[...] += ffn
        d_normed_ref[...] += d_normed

    @pl.when(step == last)
    def _():
        ffn_out_ref[...] = (ffn_ref[...] + ffn).astype(ffn_out_ref.dtype)
        total = d_normed_ref[...] + d_normed
        cut = total.shape[0] // 2
        d_normed_top_ref[...] = total[:cut].astype(d_normed_top_ref.dtype)
        d_normed_low_ref[...] = total[cut:].astype(d_normed_low_ref.dtype)


def ffn_grad_body(
    normed_t_ref, normed_t_far_ref, d_ffn_t_ref, d_ffn_t_far_ref,
    d_gate_ref, d_gate_far_ref, d_up_ref, d_up_far_ref, hidden_ref, hidden_far_ref, out_ref,
):
    normed_t = (normed_t_ref, normed_t_far_ref)
    d_ffn_t = (d_ffn_t_ref, d_ffn_t_far_ref)
    for k, (left_t, near, far) in enumerate(
        (
            (normed_t, d_gate_ref, d_gate_far_ref),
            (normed_t, d_up_ref, d_up_far_ref),
            (d_ffn_t, hidden_ref, hidden_far_ref),
        )
    ):
        out_ref[k] = (
            jnp.dot(left_t[0][...], near[...], preferred_element_type=F32)
            + jnp.dot(left_t[1][...], far[...], preferred_element_type=F32)
        ).astype(BF16)


def mix_body(
    middle_ref, ffn_ref, ffn_far_ref, dout_ref, member_ref, mod_ref, d_mods_ref, d_mix_ref,
    info_ref, mixed_ref, known_ref, gate_sum
):
    member = member_ref[...]
    ffn = ffn_ref[...] + ffn_far_ref[...].astype(F32)
    scale = jnp.dot(member, mod_ref[...], preferred_element_type=F32)
    mixed_ref[...] = (middle_ref[...] + scale * ffn).astype(BF16)
    part = tn(member, (dout_ref[...].astype(F32) * ffn).astype(BF16))

    @pl.when(pl.program_id(0) == 0)
    def _():
        gate_sum[...] = part

    @pl.when(pl.program_id(0) == pl.num_programs(0) - 1)
    def _():
        slots = known_ref.shape[0]
        low = 0
        for values in (d_mods_ref[:slots], gate_sum[:slots] + part[:slots], d_mix_ref[...],
                       info_ref[...]):
            known_ref[:, low : low + values.shape[1]] = values.astype(BF16)
            low += values.shape[1]


def middle_back_body(
    at_ref, top_ref, low_ref, top_far_ref, low_far_ref, middle_ref, branch_ref, dout_ref, member_ref,
    mod_ref, own_ref, piece_0, piece_1, d_middle_ref, d_attended_ref, d_attn_ref, d_mods_ref
):
    step = pl.program_id(0)
    rows, width = top_ref.shape
    half = width // 2

    @pl.when(step == 0)
    def _():
        d_mods_ref[...] = jnp.zeros_like(d_mods_ref)

    member = member_ref[...]

    def mods(k):
        return jnp.dot(
            member, mod_ref[:, k * width : (k + 1) * width], preferred_element_type=F32
        )

    def add_mods(k, values):
        d_mods_ref[:, k * width : (k + 1) * width] += tn(member, values.astype(BF16))

    middle = middle_ref[...]
    m_hat, inverse = norm_parts(middle)
    d_normed = jnp.where(
        step == 0,
        top_ref[...] + top_far_ref[...].astype(F32),
        low_ref[...] + low_far_ref[...].astype(F32),
    )
    add_mods(1, d_normed)
    add_mods(2, d_normed * m_hat)
    d_hat = d_normed * (1.0 + mods(4))
    d_middle = dout_ref[...].astype(F32) + inverse * (
        d_hat
        - jnp.mean(d_hat, axis=-1, keepdims=True)
        - m_hat * jnp.mean(d_hat * m_hat, axis=-1, keepdims=True)
    )
    d_middle_ref[...] = d_middle
    add_mods(0, d_middle * branch_ref[...])
    d_attn = (mods(2) * d_middle).astype(BF16)
    d_attn_ref[...] = d_attn
    d_attended_ref[:, :half] = nt(d_attn, own_ref[...]).astype(BF16)

    d_attended_ref[:, half:] = sum(
        nt(d_attn_ref[:, columns_at(at_ref, r, half)], piece[...])
        for r, piece in enumerate((piece_0, piece_1))
    ).astype(BF16)


def attention_grad_body(
    q_ref, own_ref, far_ref, d_left_ref, normed_ref, d_attn_ref, attended_ref, attended_other_ref,
    moved_ref, d_proj_ref, back_ref, keep_ref, send_ref
):
    width = normed_ref.shape[1]
    half = width // 2
    d_proj_ref[:, :width] = q_ref[...]
    total = (own_ref[...].astype(F32) + far_ref[...].astype(F32)).astype(BF16)
    d_proj_ref[:, width:] = total[:, : 2 * width]
    pair_width = d_left_ref.shape[1]
    back_ref[:, :pair_width] = d_left_ref[...]
    back_ref[:, pair_width:] = total[:, 2 * width :]
    turned = nt(moved_ref[...], normed_ref[...]).astype(BF16)
    for j in range(4):
        if j == 3:
            turned = nt(moved_ref[...], d_attn_ref[...]).astype(BF16)
            right_side = jnp.concatenate([attended_ref[...], attended_other_ref[...]], axis=1)
        else:
            right_side = d_proj_ref[:, j * width : (j + 1) * width]
        total = jnp.dot(turned, right_side, preferred_element_type=F32).astype(BF16)
        for k in range(2):
            keep_ref[k, j] = total[:half, k * half : (k + 1) * half]
            send_ref[k, j] = total[half:, k * half : (k + 1) * half]


def chain_parts(early_ref):
    groups, _, doubled, columns = early_ref.shape
    count = groups * doubled
    return early_ref[:, 0].reshape(count, columns), early_ref[:, 1].reshape(count, columns)


def early_chain_body(here_ref, early_ref, mod_weight_ref, weight_out, bias_out, d_cond_out, mix_out):
    step = pl.program_id(0)
    width = mod_weight_ref.shape[1]
    wide = mod_weight_ref.shape[0]
    modded = 2 * width
    mixed = modded + mix_out.shape[1]
    first, second = chain_parts(early_ref)
    cond = first[:, mixed : mixed + wide]

    def block(low):
        summed = first[:, low : low + width].astype(F32) + second[:, low : low + width].astype(F32)
        early = summed.astype(BF16)
        weight_out[...] = tn(cond, early)
        bias_out[...] = jnp.sum(summed, axis=0, keepdims=True)
        return nt(early, mod_weight_ref[...])

    @pl.when(step == 0)
    def _():
        d_cond_out[...] = block(0)

    @pl.when(step == 1)
    def _():
        d_cond_out[...] += block(width)
        mix = first[:, modded:mixed].astype(F32) + second[:, modded:mixed].astype(F32)
        mix = jnp.sum(mix.reshape(-1, 2, early_ref.shape[2] // 2, mixed - modded), axis=0)
        own = mix_out.shape[0]
        own_half = mix[0, :own] + mix[1, own : 2 * own]
        other_half = mix[0, own : 2 * own] + mix[1, :own]
        mix_out[...] = jnp.where((here_ref[0] & 1) == 0, own_half, other_half)


def late_chain_body(
    far_count, pair_columns, here_ref, early_ref, held_ref, near_ref, mod_weight_ref, d_cond_ref,
    weight_in, weight_out, bias_out, time_out, cath_out
):
    count = held_ref.shape[0]
    slots = early_ref.shape[2] // 2
    wide = mod_weight_ref.shape[0]
    first, _ = chain_parts(early_ref)
    low = 2 * mod_weight_ref.shape[1] + pair_columns
    cond, times, slope = (first[:, low + k * wide : low + (k + 1) * wide] for k in range(3))
    arches = first[:, low + 3 * wide :]
    row = lax.broadcasted_iota(jnp.int32, (count, count), 0)
    column = lax.broadcasted_iota(jnp.int32, (count, count), 1)
    place = column // slots
    apart = (place % far_count) * 4 + place // far_count
    order = ((apart ^ here_ref[0]) * slots + column % slots == row).astype(BF16)
    late = (
        jnp.dot(order, held_ref[...], preferred_element_type=F32)
        + jnp.dot(order, near_ref[...], preferred_element_type=F32)
    ).astype(BF16)
    weight_out[...] = tn(cond, late)
    bias_out[...] = jnp.sum(late.astype(F32), axis=0, keepdims=True)
    d_cond = (nt(late, mod_weight_ref[...]) + d_cond_ref[...]) * slope.astype(F32)
    high = d_cond.astype(BF16)
    rest = (d_cond - high.astype(F32)).astype(BF16)
    time_out[...] = tn(times, high) + tn(times, rest)
    cath_out[...] = (tn(arches, high) + tn(arches, rest))[: cath_out.shape[0]]


def deliver_body(stays_ref, *refs):
    own_ref, came_ref, outs = refs[0], refs[1], refs[2:]

    def deliver(source):
        low = 0
        for ref in outs:
            ref[...] = source[:, low : low + ref.shape[1]]
            low += ref.shape[1]

    @pl.when(stays_ref[0] == 1)
    def _():
        deliver(own_ref)

    @pl.when(stays_ref[0] == 0)
    def _():
        deliver(came_ref)


def input_back_body(
    at_ref, d_proj_ref, x_ref, d_middle_ref, member_ref, mod_ref, own_ref, piece_0, piece_1,
    grad_ref, d_mods_ref, total_ref
):
    width = x_ref.shape[1]
    half = width // 2

    def product(weights, low):
        return sum(
            nt(d_proj_ref[:, j * width + low : j * width + low + half], weights[j])
            for j in range(3)
        )

    total_ref[...] = product(own_ref, 0)
    for r, piece in enumerate((piece_0, piece_1)):
        total_ref[:, columns_at(at_ref, r, half)] += product(piece, half)
    d_normed = total_ref[...]
    member = member_ref[...]
    scale = jnp.dot(member, mod_ref[:, width:], preferred_element_type=F32)
    x_hat, inverse = norm_parts(x_ref[...].astype(F32))
    slots = d_mods_ref.shape[0]
    d_mods_ref[:, :width] = tn(member, d_normed.astype(BF16))[:slots].astype(BF16)
    d_mods_ref[:, width:] = tn(member, (d_normed * x_hat).astype(BF16))[:slots].astype(BF16)
    d_hat = d_normed * (1.0 + scale)
    grad_ref[...] = (
        d_middle_ref[...]
        + inverse
        * (
            d_hat
            - jnp.mean(d_hat, axis=-1, keepdims=True)
            - x_hat * jnp.mean(d_hat * x_hat, axis=-1, keepdims=True)
        )
    ).astype(BF16)


ANYWHERE = pl.BlockSpec(memory_space=pl.ANY)
IN_SMEM = pl.BlockSpec(memory_space=pltpu.SMEM)


def call(body, operands, specs, outs, out_specs, scratch, flops, name, grid=(1,)):
    moved = sum(math.prod(a.shape) * a.dtype.itemsize for a in operands) + sum(
        math.prod(o.shape) * jnp.dtype(o.dtype).itemsize for o in outs
    )
    return pl.pallas_call(
        body,
        grid=grid,
        in_specs=specs,
        out_specs=out_specs,
        out_shape=outs,
        scratch_shapes=scratch,
        compiler_params=pltpu.CompilerParams(vmem_limit_bytes=VMEM_LIMIT),
        cost_estimate=pl.CostEstimate(
            flops=flops // COST_CUT, bytes_accessed=moved // COST_CUT, transcendentals=0
        ),
        name=name,
    )(*operands)


def added(first, second):
    return first + second


def adder(cut, operands, shapes, name):
    def body(*refs):
        count = len(operands)
        for ref, value in zip(refs[count:], cut(*[ref[...] for ref in refs[:count]])):
            ref[...] = value

    outs = [shaped(shape) for shape in shapes]
    return call(
        body, operands, [whole(a) for a in operands], outs, [whole(a) for a in outs], [], 0, name
    )


def first_sum_body(keep_ref, far_ref, sent_a, rest_a, sent_b, rest_b):
    total = added(keep_ref[0], far_ref[0])
    rows, side = sent_a.shape[1:]
    rest_a[0], sent_a[0] = total[:rows, :side], total[rows:, :side]
    quarter = rows // 2
    for k in range(2):
        low = k * rows
        rest_b[0, k] = total[low : low + quarter, side:]
        sent_b[0, k] = total[low + quarter : low + rows, side:]


def shaped(shape, dtype=BF16):
    return jax.ShapeDtypeStruct(shape, dtype)


def make_moves(dp_count):
    def pairs(target):
        moved = []
        for d in range(dp_count):
            for m in range(2):
                to_d, to_m = target(d, m)
                if (to_d, to_m) != (d, m):
                    moved.append((d * 2 + m, to_d * 2 + to_m))
        return moved

    def mover(target):
        table = pairs(target)
        return lambda array: lax.ppermute(array, AXES, table)

    turn = mover(lambda d, m: ((d & ~1) | m, d & 1))
    turn_far = mover(lambda d, m: ((d & ~1) | m, 1 - (d & 1)))
    across = mover(lambda d, m: (d, 1 - m))

    def flip(bit):
        return mover(lambda d, m: (d ^ (1 << bit), m))

    def to(mask, over):
        return mover(lambda d, m: (d ^ mask, m ^ over))

    return turn, turn_far, across, flip, to


def shards(
    tokens,
    pair_left,
    pair_right,
    chain_len,
    chain_time,
    chain_arch,
    cath_table,
    time_weight,
    mod_weight,
    mod_bias,
    qkv_weight,
    pair_weight,
    out_weight,
    gate_up_weight,
    down_weight,
    cotangent,
):
    dp_count = lax.axis_size("dp")
    bits = dp_count.bit_length() - 1
    turn, turn_far, across, flip, to = make_moves(dp_count)
    core_swap = flip(0)
    dp_at = lax.axis_index("dp")
    mp_at = lax.axis_index("mp")
    core = dp_at & 1
    rows, width = tokens.shape
    slots = chain_len.shape[1]
    half_heads = pair_weight.shape[1]
    heads = 2 * half_heads
    pair_width = pair_left.shape[1]
    cond_width = time_weight.shape[0]
    half = width // 2
    hidden = down_weight.shape[0]

    def after(array, *earlier):
        return lax.optimization_barrier((array, *earlier))[0]

    def beside(made, *received):
        return lax.optimization_barrier((*made, *received))[: len(made)]

    held_chains = jnp.concatenate(
        [chain_len.astype(F32), chain_time, chain_arch.astype(F32)], axis=0
    )
    near_chains = core_swap(held_chains)

    cut = width // 2
    stays = core == mp_at

    def turned_in(array, *earlier):
        return jnp.where(stays, array, turn(after(array, *earlier)))

    pair_mix_other = across(pair_weight)
    x_in = turned_in(tokens)
    right_own = turned_in(pair_right, x_in)
    left_in = turned_in(pair_left, x_in)
    qkv_y = across(after(lax.dynamic_slice_in_dim(qkv_weight, core * cut, cut, 1), x_in))
    out_y = across(after(lax.dynamic_slice_in_dim(out_weight, core * cut, cut, 1), qkv_y))
    dout = turned_in(cotangent, out_y)
    dout_far = turn_far(after(cotangent, out_y))

    def ends_of(chains):
        return jnp.cumsum(chains[0].astype(jnp.int32))

    chains = jnp.where(core == mp_at, held_chains, near_chains)
    far_chains = jnp.where(core == mp_at, near_chains, held_chains)
    arches = chains[2].astype(jnp.int32)
    ends = ends_of(chains)
    times = jnp.concatenate([chains[1], far_chains[1]])

    def ids_of(part, ends=ends):
        positions = jnp.arange(rows, dtype=jnp.int32) + part * rows
        return jnp.sum((positions[:, None] >= ends[None, :]).astype(jnp.int32), axis=1)

    own_ids = ids_of(core)
    key_ids = jnp.concatenate([own_ids, ids_of(1 - core)])
    chain_numbers = jnp.arange(slots, dtype=jnp.int32)
    doubled = jnp.concatenate([chain_numbers, chain_numbers])[None, :]
    member = (own_ids[:, None] == doubled).astype(BF16)
    member_far = (ids_of(core, ends_of(far_chains))[:, None] == doubled).astype(BF16)
    lanes = jnp.arange(128, dtype=jnp.int32)[None, :] & 63
    hot = (own_ids[:, None] == lanes).astype(BF16)
    pens = jnp.where((key_ids[:, None] != lanes) & (lanes <= slots), -1e30, 0.0).astype(BF16)
    pen_own, pen_near = pens[:rows], pens[rows:]

    half_cond = cond_width // 2
    frequency = jnp.exp(jnp.arange(half_cond, dtype=F32) * (-math.log(10000.0) / half_cond))
    angles = times[:, None] * 1000.0 * frequency[None, :]
    time_embed = jnp.concatenate([jnp.sin(angles), jnp.cos(angles)], axis=1).astype(BF16)
    both_arches = jnp.concatenate([arches, far_chains[2].astype(jnp.int32)])
    arch_onehot = (
        both_arches[:, None] == jnp.arange(cath_table.shape[0], dtype=jnp.int32)[None, :]
    ).astype(F32)
    cond_pre = dot_f32(time_embed, time_weight) + highest_dot(arch_onehot, cath_table.astype(F32))
    cond_value, cond_slope = silu_parts(cond_pre)
    cond_act = cond_value.astype(BF16)
    chain_mod = dot_f32(cond_act, mod_weight) + mod_bias.astype(F32)[None, :]
    mod_high = lax.reduce_precision(chain_mod, 8, 7)
    mod_low = (chain_mod - mod_high).astype(BF16)
    mod_high = mod_high.astype(BF16)
    mods = jnp.concatenate([mod_high[:slots], mod_low[:slots]], axis=0)
    gate_far = jnp.concatenate([mod_high[slots:], mod_low[slots:]], axis=0)[:, 5 * width :]
    arch_low = (arches[:, None] == jnp.arange(128, dtype=jnp.int32)[None, :]).astype(BF16)
    info = jnp.concatenate(
        [cond_act[:slots], time_embed[:slots], cond_slope[:slots].astype(BF16), arch_low], axis=1
    )

    order = [int(format(p, "0%db" % bits)[::-1], 2) for p in range(dp_count)]
    block_at = jnp.array(order, jnp.int32) ^ dp_at
    block_rows = width // dp_count
    source = (block_at[:, None] * block_rows + jnp.arange(block_rows)[None, :]).reshape(-1)
    moved = (source[:, None] == jnp.arange(width)[None, :]).astype(BF16)
    at = core.reshape(1).astype(jnp.int32)
    semaphores = pltpu.SemaphoreType.DMA

    mod_a = mods[:, : 2 * width]
    pair_mix = jnp.concatenate([pair_weight, pair_mix_other], axis=1).astype(F32)
    mix_rows = jnp.transpose(pair_mix).reshape(half_heads, 2, -1)
    part_shape = shaped((rows, half))
    operands = [after(x_in, moved, mods, hot, pens, member_far, gate_far, mix_rows, info), member, mod_a,
                qkv_weight]
    made = call(
        qkv_body,
        operands,
        [whole(a) for a in operands],
        [part_shape, shaped((rows, width)), shaped((rows, width))],
        [whole(part_shape), whole(shaped((rows, width))), whole(shaped((rows, width)))],
        [],
        3 * rows * width * width,
        "project",
    )
    queries, kv_own, normed_a = beside(made, right_own, left_in)
    kv_near, right_near = core_swap(kv_own), core_swap(right_own)
    factors = (right_own, right_near, pen_own, pen_near)
    made = attention_forward(0, mix_rows, queries, left_in, hot, kv_own, kv_near, *factors)
    made = beside(made, qkv_y)
    qkv_y = after(qkv_y, made[0])
    qkv_pieces = [qkv_y, core_swap(qkv_y)]
    first_half = (*made, queries, kv_own, kv_near)
    made = call(
        qkv_other_body,
        [at, after(normed_a, made[0]), *qkv_pieces],
        [IN_SMEM, whole(normed_a), whole(qkv_y), whole(qkv_y)],
        [part_shape, shaped((rows, width))],
        [whole(part_shape), whole(shaped((rows, width)))],
        [],
        3 * rows * width * width,
        "project_other",
    )
    queries, kv_own = beside(made, out_y)
    out_pieces = [out_y, core_swap(out_y)]
    kv_near = core_swap(kv_own)
    made = attention_forward(1, mix_rows, queries, left_in, hot, kv_own, kv_near, *factors)
    made = beside(made, *out_pieces)
    second_half = (*made, queries, kv_own, kv_near)
    attended, attended_other = first_half[0], second_half[0]
    wide = shaped((rows, width), F32)
    thin = shaped((rows, width))
    middle, branch, normed_f = call(
        branch_body,
        [at, attended, attended_other, out_weight, *out_pieces, x_in, member, mods],
        [IN_SMEM]
        + [whole(a) for a in (attended, attended_other, out_weight, *out_pieces, x_in, member, mods)],
        [wide, wide, thin],
        [whole(thin)] * 3,
        [],
        2 * rows * width * width,
        "branch",
    )

    normed_far = across(normed_f)
    gate_mod = mods[:, 5 * width :]
    block = FFN_BLOCK
    active = shaped((rows, hidden))
    turned = shaped((width, rows))

    def feed_forward(normed, dout, member, gate, sum_type):
        column = pl.BlockSpec((rows, block), lambda i: (0, i))
        summed = shaped((rows, width), sum_type)
        part = shaped((rows // 2, width), sum_type)
        return call(
            ffn_body,
            [normed, dout, member, gate, moved, gate_up_weight, down_weight],
            [whole(a) for a in (normed, dout, member, gate, moved)]
            + [
                pl.BlockSpec((2, width, block), lambda i: (0, 0, i)),
                pl.BlockSpec((block, width), lambda i: (i, 0)),
            ],
            [summed, part, part, turned, turned, active, active, active],
            [whole(thin), whole(part), whole(part), whole(turned), whole(turned), column, column, column],
            [
                pltpu.VMEM((rows, width), F32), pltpu.VMEM((rows, width), F32),
                pltpu.VMEM((rows, width), BF16),
            ],
            12 * rows * width * hidden,
            "feed_forward",
            (hidden // block,),
        )

    made = feed_forward(normed_f, dout, member, gate_mod, F32)
    ffn, d_normed_top, d_normed_low, normed_t, d_ffn_t, d_gate, d_up, hid = made
    normed_far, dout_far = lax.optimization_barrier((normed_far, dout_far, *made))[:2]
    ffn_for, top_for, low_for, normed_t_far, d_ffn_t_far, d_gate_far, d_up_far, hid_far = feed_forward(
        normed_far, dout_far, member_far, gate_far, BF16
    )
    top_far, low_far = across(top_for), across(low_for)

    grad = shaped((3, half, hidden))
    grad_block = pl.BlockSpec((3, half, GRAD_BLOCK), lambda i: (0, 0, i))
    column = pl.BlockSpec((rows, GRAD_BLOCK), lambda i: (0, i))
    turned_half = [normed_t, normed_t_far, d_ffn_t, d_ffn_t_far]
    sides = [d_gate, d_gate_far, d_up, d_up_far, hid, hid_far]

    def ffn_grads(part, *earlier):
        row_half = pl.BlockSpec((half, rows), lambda i: (part, 0))
        return call(
            ffn_grad_body,
            [after(turned_half[0], *earlier), *turned_half[1:], *sides],
            [row_half] * 4 + [column] * 6,
            [grad],
            [grad_block],
            [],
            6 * rows * width * hidden,
            "feed_forward_grads",
            (hidden // GRAD_BLOCK,),
        )[0]

    (send,) = beside((ffn_grads(1),), top_far)
    far = core_swap(send)
    (keep,) = beside((ffn_grads(0, send),), far, low_far)
    ffn_far = across(after(ffn_for, keep))

    def plus(kept, received):
        return (kept.astype(F32) + received.astype(F32)).astype(BF16)

    def halves(array, upper):
        size = array.shape[-2] // 2
        return array[..., size:, :] if upper else array[..., :size, :]

    def y_part(kept, received):
        return plus(kept[1], received[1])

    def y_rest(kept, received):
        return plus(kept[0], received[0])

    def bit_part(kept, received):
        return plus(halves(kept, True), halves(received, True))

    def bit_rest(kept, received):
        return plus(halves(kept, False), halves(received, False))

    steps = 2
    row_block = pl.BlockSpec((rows // steps, width), lambda i: (i, 0))
    member_block = pl.BlockSpec((rows // steps, 2 * slots), lambda i: (i, 0))
    mods_early = shaped((2 * slots, 3 * width), F32)
    made = call(
        middle_back_body,
        [at, after(d_normed_top, keep), d_normed_low, top_far, low_far, middle, branch, dout,
         member, mods, out_weight, *out_pieces],
        [IN_SMEM] + [whole(d_normed_top)] * 4 + [row_block] * 3
        + [member_block, whole(mods), whole(out_weight), whole(out_y), whole(out_y)],
        [wide, thin, thin, mods_early],
        [row_block, row_block, row_block, whole(mods_early)],
        [],
        4 * rows * width * width,
        "middle_back",
        (steps,),
    )
    d_middle, d_attended, d_attn, d_mods = made
    side = hidden // 2
    shape_a, shape_b = (3, half // 2, side), (3, 2, half // 4, side)
    block_a = pl.BlockSpec((1, *shape_a[1:]), lambda i: (i, 0, 0))
    block_b = pl.BlockSpec((1, *shape_b[1:]), lambda i: (i, 0, 0, 0))
    sent, rest, sent_b, rest_b = call(
        first_sum_body,
        [keep, far],
        [pl.BlockSpec((1, half, hidden), lambda i: (i, 0, 0))] * 2,
        [shaped(shape_a), shaped(shape_a), shaped(shape_b), shaped(shape_b)],
        [block_a, block_a, block_b, block_b],
        [],
        0,
        "first_sum",
        (3,),
    )
    got, got_b = flip(1)(sent), flip(2)(sent_b)

    def finish(bit, kept, sent):
        while bit < bits:
            received = flip(bit)(sent)
            bit += 1
            if bit < bits:
                kept, sent = bit_rest(kept, received), bit_part(kept, received)
        return kept.astype(F32) + received.astype(F32)

    near_bits = [-1, 1] if bits > 1 else [-1]
    far_bits = list(range(2, bits))

    def several(group):
        moves = []
        for chosen in range(1, 1 << len(group)):
            mask, over = 0, 0
            for k, bit in enumerate(group):
                if chosen >> k & 1:
                    mask, over = (mask, 1) if bit < 0 else (mask | 1 << bit, over)
            moves.append((mask, over))
        return moves

    def gather_step(group, held):
        return jnp.concatenate(
            [held] + [to(mask, over)(held) for mask, over in several(group)], axis=0
        )

    made = attention_backward(
        mix_rows, after(d_attended, sent, sent_b), (first_half, second_half), left_in, *factors
    )
    d_query, d_own, d_far, d_left = beside(made[:4], ffn_far, got, got_b)

    def second_cut(rest, got, rest_b, got_b):
        total, total_b = added(rest, got), added(rest_b, got_b)
        rows = total.shape[1] // 2
        return total[:, rows:], total[:, :rows], total_b[:, 1], total_b[:, 0]

    shape = (3, half // 4, side)
    sent, rest, sent_b, rest_b = adder(
        second_cut, [rest, got, rest_b, got_b], [shape] * 4, "second_sum"
    )
    got, got_b = flip(2)(sent), flip(1)(sent_b)
    d_mix = made[4]
    far_kv = core_swap(d_far)

    known = shaped((slots, 4 * width + d_mix.shape[1] + info.shape[1]))
    mixed, known = call(
        mix_body,
        [after(middle, d_far, sent, sent_b), ffn, ffn_far, dout, member, gate_mod, d_mods, d_mix,
         info],
        [row_block] * 4 + [member_block] + [whole(a) for a in (gate_mod, d_mods, d_mix, info)],
        [thin, known],
        [row_block, whole(known)],
        [pltpu.VMEM((2 * slots, width), F32)],
        4 * rows * 16 * width,
        "mix",
        (steps,),
    )
    mixed, known = beside((mixed, known), far_kv)
    mixed_own, mixed = mixed, turn(mixed)
    early = lax.all_gather(known, AXES, axis=0, tiled=False)

    proj_grad = shaped((rows, 3 * width))
    back = shaped((rows, 2 * pair_width))
    grad = shaped((2, 4, half, half))
    operands = [d_query, d_own, far_kv, d_left, after(normed_a, known), d_attn, attended,
                attended_other, moved]
    outs = [proj_grad, back, grad, grad]
    made = call(
        attention_grad_body,
        operands,
        [whole(a) for a in operands],
        outs,
        [whole(a) for a in outs],
        [],
        12 * rows * width * width,
        "attention_grads",
    )
    d_proj, back, keep_qkvo, send_qkvo = beside(made, got, got_b, mixed)
    far_qkvo = core_swap(send_qkvo)
    back_own, back = back, turn(back)

    def third_cut(rest, got, rest_b, got_b):
        total = jnp.concatenate([added(rest, got), added(rest_b, got_b)], axis=2)
        rows = total.shape[1] // 2
        return total[:, rows:], total[:, :rows]

    shape = (3, half // 8, hidden)
    sent, rest = adder(third_cut, [rest, got, rest_b, got_b], [shape] * 2, "third_sum")

    def qkvo_cut(keep, far):
        total = added(keep, far)
        rows = half // 2
        return total[1, :2], total[0, :2], total[:, 2:, rows:], total[:, 2:, :rows]

    shape, shape_vo = (2, half, half), (2, 2, half // 2, half)
    sent_qk, rest_qk, sent_vo, rest_vo = adder(
        qkvo_cut, [keep_qkvo, far_qkvo], [shape, shape, shape_vo, shape_vo], "qkvo_sum"
    )
    got_qk, got_vo = across(sent_qk), flip(1)(sent_vo)
    mods_late = shaped((slots, 2 * width))
    operands = [at, after(d_proj, sent_qk, sent_vo, sent), x_in, d_middle, member, mod_a,
                qkv_weight, *qkv_pieces]
    made = call(
        input_back_body,
        operands,
        [IN_SMEM] + [whole(a) for a in operands[1:]],
        [thin, mods_late],
        [whole(thin), whole(mods_late)],
        [pltpu.VMEM((rows, width), F32)],
        6 * rows * width * width,
        "input_back",
    )
    tokens_out, held = beside(made, got_qk, got_vo)
    token_gradient = turn(tokens_out)
    got = flip(3)(sent)

    def together(*arrays):
        return lax.optimization_barrier(arrays)

    def qkvo_second(rest_qk, got_qk, rest_vo, got_vo):
        total, total_vo = added(rest_qk, got_qk), added(rest_vo, got_vo)
        rows = half // 2
        return total[:, rows:], total[:, :rows], total_vo[1], total_vo[0]

    shape = (2, half // 2, half)
    sent_qk, rest_qk, sent_vo, rest_vo = adder(
        qkvo_second, [after(rest_qk, tokens_out), got_qk, rest_vo, got_vo], [shape] * 4, "qkvo_second"
    )
    got_qk, got_vo = flip(1)(sent_qk), across(sent_vo)
    held = gather_step(far_bits, held)

    def qkvo_third(rest_qk, got_qk, rest_vo, got_vo):
        total = jnp.concatenate([added(rest_qk, got_qk), added(rest_vo, got_vo)], axis=0)
        rows = half // 4
        return total[:, rows:], total[:, :rows]

    shape = (4, half // 4, half)
    sent_qkvo, qkvo = adder(
        qkvo_third, [rest_qk, got_qk, rest_vo, got_vo], [shape] * 2, "qkvo_third"
    )
    stay_flag = stays.reshape(1).astype(jnp.int32)

    def delivered(own, came, widths):
        blocks = [pl.BlockSpec((rows // 2, w), lambda i: (i, 0)) for w in [own.shape[1]] * 2 + widths]
        return call(
            deliver_body,
            [stay_flag, own, came],
            [IN_SMEM, *blocks[:2]],
            [shaped((rows, w)) for w in widths],
            blocks[2:],
            [],
            0,
            "deliver",
            (2,),
        )

    (mixed,) = delivered(mixed_own, after(mixed, tokens_out), [width])
    left_grad, right_grad = delivered(back_own, after(back, mixed), [pair_width, pair_width])
    held, qkvo, sent_qkvo, token_gradient = together(
        held, qkvo, sent_qkvo, token_gradient, left_grad, right_grad, mixed
    )[:4]
    held = gather_step(near_bits, held)
    got_qkvo = flip(2)(sent_qkvo)
    here = ((dp_at >> 1) * 2 + mp_at).reshape(1).astype(jnp.int32)
    early = early.reshape(dp_count // 2, 2, 2 * slots, -1)
    late_to = 2 * width
    weight_shape = shaped(mod_weight.shape, F32)
    bias_shape = shaped((1, 6 * width), F32)
    cond_shape = shaped((dp_count * slots, cond_width), F32)
    mix_shape = shaped((half_heads // 2, 2 * pair_width), F32)
    later = lambda i: (0, 1 + i)
    early = after(early, tokens_out, sent_qkvo)
    early_weight, early_bias, early_cond, mix_sum = call(
        early_chain_body,
        [here, early, mod_weight],
        [IN_SMEM, whole(early), pl.BlockSpec((cond_width, late_to), later)],
        [weight_shape, bias_shape, cond_shape, mix_shape],
        [
            pl.BlockSpec((cond_width, late_to), later), pl.BlockSpec((1, late_to), later),
            whole(cond_shape), whole(mix_shape),
        ],
        [],
        0,
        "early_chains",
        (2,),
    )
    mix_sum = mix_sum.reshape(half_heads, -1)
    taken = mix_sum.shape[1] // dp_count
    pair_sum = jnp.transpose(lax.dynamic_slice_in_dim(mix_sum, dp_at * taken, taken, 1))
    if bits > 4:
        ffn_sum = finish(4, bit_rest(rest, got), bit_part(rest, got))
    else:
        ffn_sum = rest.astype(F32) + got.astype(F32)
    down_sum = jnp.transpose(ffn_sum[2])
    ffn_sum = ffn_sum[:2]
    (token_gradient,) = delivered(tokens_out, token_gradient, [width])
    held, got_qkvo = together(
        held, got_qkvo, early_weight, pair_sum, ffn_sum, down_sum, token_gradient
    )[:2]
    near = core_swap(held)
    sent_qkvo, qkvo = bit_part(qkvo, got_qkvo), bit_rest(qkvo, got_qkvo)
    got_qkvo = flip(3)(sent_qkvo)

    late_bias_shape = shaped((1, late_to), F32)
    operands = [here, early, held, near]
    time_shape, cath_shape = shaped((cond_width, cond_width), F32), shaped(cath_table.shape, F32)
    first_columns = pl.BlockSpec((cond_width, late_to), lambda i: (0, 0))
    mod_weight_sum, late_bias, time_sum, cath_sum = pl.pallas_call(
        functools.partial(late_chain_body, dp_count // 4, mix_shape.shape[1]),
        grid=(1,),
        in_specs=[IN_SMEM]
        + [whole(a) for a in operands[1:]]
        + [first_columns, whole(cond_shape), ANYWHERE],
        out_specs=[first_columns, whole(late_bias_shape), whole(time_shape), whole(cath_shape)],
        out_shape=[weight_shape, late_bias_shape, time_shape, cath_shape],
        input_output_aliases={6: 0},
        compiler_params=pltpu.CompilerParams(vmem_limit_bytes=VMEM_LIMIT),
        name="late_chains",
    )(*operands, mod_weight, early_cond, early_weight)
    mod_bias_sum = jnp.concatenate([late_bias[0], early_bias[0, late_to:]])

    got_qkvo, _ = together(got_qkvo, mod_weight_sum)
    if bits > 4:
        qkvo_sum = finish(4, bit_rest(qkvo, got_qkvo), bit_part(qkvo, got_qkvo))
    else:
        qkvo_sum = qkvo.astype(F32) + got_qkvo.astype(F32)

    return (
        mixed,
        token_gradient,
        left_grad,
        right_grad,
        cath_sum,
        time_sum,
        mod_weight_sum,
        mod_bias_sum,
        qkvo_sum[:3],
        pair_sum,
        jnp.transpose(qkvo_sum[3]),
        ffn_sum,
        down_sum,
    )


def solution(mesh):
    by_rows = P(AXES, None)
    placed = (
        by_rows,
        by_rows,
        by_rows,
        P("dp", None),
        P("dp", None),
        P("dp", None),
        P(),
        P(),
        P(),
        P(),
        P(None, None, "mp"),
        P(None, "mp"),
        P("mp", None),
        P(None, None, "mp"),
        P("mp", None),
        by_rows,
    )
    return jax.shard_map(
        shards,
        mesh=mesh,
        in_specs=placed,
        out_specs=(
            by_rows,
            by_rows,
            by_rows,
            by_rows,
            P(),
            P(),
            P(),
            P(),
            P(None, "dp", "mp"),
            P("dp", "mp"),
            P("mp", "dp"),
            P(None, "dp", "mp"),
            P("mp", "dp"),
        ),
        check_vma=False,
    )
```

```python
import functools
import math

import jax
import jax.numpy as jnp
from jax import lax
from jax.experimental import pallas as pl
from jax.experimental.pallas import tpu as pltpu
from jax.sharding import PartitionSpec as P

EPSILON = 1e-06
AXES = ("dp", "mp")
BF16 = jnp.bfloat16
F32 = jnp.float32
VMEM_LIMIT = 64 * 1024 * 1024
FFN_BLOCK = 512
GRAD_BLOCK = 768
BACK_PARTS = 1
COST_CUT = 20


def highest_dot(left_side, right_side):
    return jnp.dot(left_side, right_side, precision=lax.Precision.HIGHEST)


def silu_parts(values):
    sigma = jax.nn.sigmoid(values)
    return (values * sigma, sigma * (1.0 + values * (1.0 - sigma)))


def dot_f32(left_side, right_side):
    return jnp.dot(left_side, right_side, preferred_element_type=F32)


def dot_nt(left_side, right_side):
    return lax.dot_general(
        left_side, right_side, (((1,), (1,)), ((), ())), preferred_element_type=F32
    )

def lane_mix(first, second, odd):
    lane = lax.broadcasted_iota(jnp.int32, first.shape, 1)
    keep = (lane >= 64) if odd else (lane < 64)
    return jnp.where(keep, first, second)


def nt(left_side, right_side):
    return lax.dot_general(
        left_side, right_side, (((1,), (1,)), ((), ())), preferred_element_type=F32
    )


def attention_forward_body(
    pair_mix_ref, q_ref, left_ref, hot_ref, k_own_ref, k_near_ref, v_own_ref, v_near_ref,
    right_own_ref, right_near_ref, pen_own_ref, pen_near_ref,
    attended_ref, inverse_ref, probs_ref,
):
    rows = q_ref.shape[0]
    step = 512
    out_tiles = []
    left = left_ref[...].astype(F32)
    for odd in range(2):
        mix = pair_mix_ref[0, odd : odd + 1, :]
        left_mixed = (left * mix).astype(BF16)
        q_side = jnp.concatenate([left_mixed, lane_mix(q_ref[...], hot_ref[...], odd)], axis=1)
        k_own = jnp.concatenate(
            [right_own_ref[...], lane_mix(k_own_ref[...], pen_own_ref[...], odd)], axis=1
        )
        k_near = jnp.concatenate(
            [right_near_ref[...], lane_mix(k_near_ref[...], pen_near_ref[...], odd)], axis=1
        )
        v_own = lane_mix(v_own_ref[...], jnp.ones_like(v_own_ref[...]), odd)
        v_near = lane_mix(v_near_ref[...], jnp.ones_like(v_near_ref[...]), odd)
        tiles = []
        for start in range(0, rows, step):
            block = q_side[start : start + step]
            s_own = nt(block, k_own)
            s_near = nt(block, k_near)
            top = jnp.maximum(
                jnp.max(s_own, axis=1, keepdims=True), jnp.max(s_near, axis=1, keepdims=True)
            )
            e_own = jnp.exp(s_own - top).astype(BF16)
            e_near = jnp.exp(s_near - top).astype(BF16)
            probs_ref[odd, start : start + step, :rows] = e_own
            probs_ref[odd, start : start + step, rows:] = e_near
            tiles.append(
                jnp.dot(e_own, v_own, preferred_element_type=F32)
                + jnp.dot(e_near, v_near, preferred_element_type=F32)
            )
        out_tiles.append(jnp.concatenate(tiles, axis=0))
    sums = lane_mix(out_tiles[1], out_tiles[0], False)
    sums = pltpu.roll(sums, 64, 1)
    inverse = 1.0 / sums
    attended_ref[...] = (lane_mix(out_tiles[0], out_tiles[1], False) * inverse).astype(BF16)
    inverse_ref[...] = inverse


def attention_backward_body(
    pair_mix_ref, grad_ref, left_ref, right_own_ref, right_near_ref, pen_own_ref, pen_near_ref,
    *rest
):
    outs = rest[16:21]
    scores_ref, right_sum_ref, left_sum_ref, left_t_ref = rest[21:]
    pair = pl.program_id(0)
    pairs = pl.num_programs(0)

    @pl.when(pair == 0)
    def _():
        left_t_ref[...] = left_ref[...].T
        outs[4][...] = jnp.zeros_like(outs[4])
        right_sum_ref[...] = jnp.zeros_like(right_sum_ref)
        left_sum_ref[...] = jnp.zeros_like(left_sum_ref)

    common = (
        pair_mix_ref, grad_ref, left_ref, right_own_ref, right_near_ref, pen_own_ref, pen_near_ref,
        *outs, *rest[21:],
    )

    @pl.when(pair < pairs // 2)
    def _():
        attention_backward_pair(common, *rest[:8])

    @pl.when(pair >= pairs // 2)
    def _():
        attention_backward_pair(common, *rest[8:16])

    @pl.when(pair == pairs - 1)
    def _():
        rows = left_ref.shape[0]
        right = right_sum_ref[...].T.astype(BF16)
        outs[1][:, outs[1].shape[1] - right.shape[1] :] = right[:rows]
        outs[2][:, outs[1].shape[1] - right.shape[1] :] = right[rows:]
        outs[3][...] = left_sum_ref[...].astype(BF16)


def attention_backward_pair(
    common, attended_ref, inverse_ref, probs_ref, q_ref, k_own_ref, k_near_ref, v_own_ref,
    v_near_ref
):
    (
        pair_mix_ref, grad_ref, left_ref, right_own_ref, right_near_ref, pen_own_ref, pen_near_ref,
        d_q_ref, own_out, near_out, _, d_mix_ref,
        scores_ref, right_sum_ref, left_sum_ref, left_t_ref,
    ) = common
    pair = pl.program_id(0)
    rows = q_ref.shape[0]
    step = 256
    wide = grad_ref.shape[1] * pl.num_programs(0)
    scaled = (grad_ref[...].astype(F32) * inverse_ref[...]).astype(BF16)
    products = scaled.astype(F32) * attended_ref[...].astype(F32)
    scaled_t = scaled.T
    q_t = q_ref[...].T
    lane = lax.broadcasted_iota(jnp.int32, products.shape, 1)
    left = left_ref[...].astype(F32)
    left_t = left_t_ref[...].astype(F32)
    d_q, dk_t, dv_t = [], [], []
    for odd in range(2):
        mine = (lane >= 64) if odd else (lane < 64)
        delta = -jnp.sum(jnp.where(mine, products, 0.0), axis=1, keepdims=True)
        high = delta.astype(BF16).astype(F32)
        low = delta - high
        at = 0 if odd else 64
        extra = jnp.where(lane == at, high, jnp.where(lane == at + 1, low, 0.0)).astype(BF16)
        grad_side = jnp.where(mine, scaled, extra)
        mix = pair_mix_ref[0, odd : odd + 1, :]
        k_own = jnp.concatenate(
            [right_own_ref[...], lane_mix(k_own_ref[...], pen_own_ref[...], odd)], axis=1
        )
        k_near = jnp.concatenate(
            [right_near_ref[...], lane_mix(k_near_ref[...], pen_near_ref[...], odd)], axis=1
        )
        v_own = lane_mix(v_own_ref[...], jnp.ones_like(v_own_ref[...]), odd)
        v_near = lane_mix(v_near_ref[...], jnp.ones_like(v_near_ref[...]), odd)
        for start in range(0, rows, step):
            block = grad_side[start : start + step]
            own = nt(block, v_own).astype(BF16) * probs_ref[odd, start : start + step, :rows]
            near = nt(block, v_near).astype(BF16) * probs_ref[odd, start : start + step, rows:]
            scores_ref[start : start + step, :rows] = own
            scores_ref[start : start + step, rows:] = near
        d_query = jnp.dot(
            scores_ref[:, :rows], k_own, preferred_element_type=F32
        ) + jnp.dot(scores_ref[:, rows:], k_near, preferred_element_type=F32)
        width = left.shape[1]
        d_q.append(d_query[:, width:])
        d_pair = d_query[:, :width]
        left_sum_ref[...] += d_pair * mix
        d_mix_ref[pl.ds(pair, 1), odd * width : (odd + 1) * width] = jnp.sum(
            d_pair * left, axis=0, keepdims=True
        )
        mixed_t = (left_t * jnp.transpose(mix)).astype(BF16)
        low_row = 64 * odd
        q_side = jnp.concatenate([mixed_t, q_t[low_row : low_row + 64]], axis=0)
        d_key = jnp.dot(q_side, scores_ref[...], preferred_element_type=F32)
        right_sum_ref[...] += d_key[:width]
        dk_t.append(d_key[width:])
        dv_t.append(
            jnp.dot(
                scaled_t[low_row : low_row + 64], probs_ref[odd], preferred_element_type=F32
            )
        )
    d_q_ref[...] = (lane_mix(d_q[0], d_q[1], False) * 0.125).astype(BF16)
    for base, parts in ((0, dk_t), (wide, dv_t)):
        both = jnp.concatenate(parts, axis=0).T.astype(BF16)
        column = pl.multiple_of(base + pair * 128, 128)
        own_out[:, pl.ds(column, 128)] = both[:rows]
        near_out[:, pl.ds(column, 128)] = both[rows:]


def whole(array):
    zeros = (0,) * array.ndim
    return pl.BlockSpec(array.shape, lambda *_: zeros)


def attention_forward(
    part, pair_mix, queries, left, hot, kv_own, kv_near, right_own, right_near, pen_own, pen_near
):
    rows, width = queries.shape
    pairs = width // 128
    pair_width = left.shape[1]
    column = pl.BlockSpec((rows, 128), lambda p: (0, p))
    value_column = pl.BlockSpec((rows, 128), lambda p: (0, pairs + p))
    operands = [
        pair_mix, queries, left, hot, kv_own, kv_near, kv_own, kv_near, right_own, right_near,
        pen_own, pen_near,
    ]
    return call(
        attention_forward_body,
        operands,
        [
            pl.BlockSpec((1, 2, pair_width), lambda p: (part * pairs + p, 0, 0)), column,
            whole(left), whole(hot), column, column, value_column, value_column,
            whole(right_own), whole(right_near), whole(pen_own), whole(pen_near),
        ],
        [
            shaped((rows, width)), shaped((rows, width), F32),
            shaped((2 * pairs, rows, 2 * rows)),
        ],
        [column, column, pl.BlockSpec((2, rows, 2 * rows), lambda p: (p, 0, 0))],
        [],
        2 * 2 * pairs * rows * 2 * rows * 512,
        "attention_forward",
        (pairs,),
    )


def attention_backward(
    pair_mix, grad, halves, left, right_own, right_near, pen_own, pen_near
):
    rows, width = grad.shape
    pairs = width // 128
    here = pairs // 2
    pair_width = left.shape[1]
    column = pl.BlockSpec((rows, 128), lambda p: (0, p))
    mix = pl.BlockSpec((1, 2, pair_width), lambda p: (p, 0, 0))
    both = shaped((rows, 2 * width + pair_width))
    operands = [pair_mix, grad, left, right_own, right_near, pen_own, pen_near]
    specs = [mix, column] + [whole(a) for a in operands[2:]]
    for part, (attended, inverse, probs, queries, kv_own, kv_near) in enumerate(halves):
        at = lambda p, part=part: jnp.clip(p - part * here, 0, here - 1)
        own = pl.BlockSpec((rows, 128), lambda p, at=at: (0, at(p)))
        value = pl.BlockSpec((rows, 128), lambda p, at=at: (0, here + at(p)))
        operands += [attended, inverse, probs, queries, kv_own, kv_near, kv_own, kv_near]
        specs += [
            own, own, pl.BlockSpec((2, rows, 2 * rows), lambda p, at=at: (at(p), 0, 0)), own, own,
            own, value, value,
        ]
    outs = [
        shaped((rows, width)), both, both, shaped((rows, pair_width)),
        shaped((8, 2 * pair_width), F32),
    ]
    return call(
        attention_backward_body,
        operands,
        specs,
        outs,
        [column, whole(both), whole(both), whole(outs[3]), whole(outs[4])],
        [
            pltpu.VMEM((rows, 2 * rows), BF16),
            pltpu.VMEM((pair_width, 2 * rows), F32),
            pltpu.VMEM((rows, pair_width), F32),
            pltpu.VMEM((pair_width, rows), BF16),
        ],
        2 * 2 * pairs * rows * 2 * rows * 1000,
        "attention_backward",
        (pairs,),
    )


def norm_parts(values):
    centered = values - jnp.mean(values, axis=-1, keepdims=True)
    inverse = lax.rsqrt(jnp.mean(centered * centered, axis=-1, keepdims=True) + EPSILON)
    return centered * inverse, inverse


def tn(left_side, right_side):
    return lax.dot_general(
        left_side, right_side, (((0,), (0,)), ((), ())), preferred_element_type=F32
    )


def qkv_body(x_ref, member_ref, mod_ref, own_ref, q_ref, kv_ref, normed_ref):
    width = x_ref.shape[1]
    half = width // 2
    mods = jnp.dot(member_ref[...], mod_ref[...], preferred_element_type=F32)
    x_hat, _ = norm_parts(x_ref[...].astype(F32))
    normed = (x_hat * (1.0 + mods[:, width:]) + mods[:, :width]).astype(BF16)
    normed_ref[...] = normed
    q = jnp.dot(normed, own_ref[0], preferred_element_type=F32).astype(BF16)
    q_ref[...] = (q.astype(F32) * 0.125).astype(BF16)
    for k in (1, 2):
        kv_ref[:, (k - 1) * half : k * half] = jnp.dot(
            normed, own_ref[k], preferred_element_type=F32
        ).astype(BF16)


def columns_at(at_ref, r, size):
    return pl.ds(pl.multiple_of((at_ref[0] ^ r) * size, size), size)


def qkv_other_body(at_ref, normed_ref, piece_0, piece_1, q_ref, kv_ref):
    half = normed_ref.shape[1] // 2
    sides = [(normed_ref[:, columns_at(at_ref, r, half)], p) for r, p in enumerate((piece_0, piece_1))]

    def product(k):
        return sum(
            jnp.dot(side, piece[k], preferred_element_type=F32) for side, piece in sides
        ).astype(BF16)

    q_ref[...] = (product(0).astype(F32) * 0.125).astype(BF16)
    for k in (1, 2):
        kv_ref[:, (k - 1) * half : k * half] = product(k)


def branch_body(
    at_ref, attended_ref, attended_other_ref, own_ref, piece_0, piece_1, x_ref, member_ref, mod_ref,
    middle_ref, branch_ref, normed_ref
):
    width = x_ref.shape[1]
    half = width // 2
    member = member_ref[...]

    def mods(k):
        return jnp.dot(
            member, mod_ref[:, k * width : (k + 1) * width], preferred_element_type=F32
        )

    branch_ref[...] = jnp.dot(attended_ref[...], own_ref[...], preferred_element_type=F32)
    for r, piece in enumerate((piece_0, piece_1)):
        branch_ref[:, columns_at(at_ref, r, half)] += jnp.dot(
            attended_other_ref[...], piece[...], preferred_element_type=F32
        )
    branch = branch_ref[...]
    middle = x_ref[...].astype(F32) + mods(2) * branch
    middle_ref[...] = middle
    m_hat, _ = norm_parts(middle)
    normed_ref[...] = (m_hat * (1.0 + mods(4)) + mods(3)).astype(BF16)


def ffn_body(
    normed_ref, dout_ref, member_ref, mod_ref, moved_ref, gate_up_ref, down_ref,
    ffn_out_ref, d_normed_top_ref, d_normed_low_ref, normed_t_ref, d_ffn_t_ref, d_gate_ref,
    d_up_ref, hidden_ref, ffn_ref, d_normed_ref, d_ffn_ref,
):
    step = pl.program_id(0)
    last = pl.num_programs(0) - 1

    @pl.when(step == 0)
    def _():
        scale = jnp.dot(member_ref[...], mod_ref[...], preferred_element_type=F32)
        d_ffn_ref[...] = (scale * dout_ref[...].astype(F32)).astype(BF16)
        normed_t_ref[...] = nt(moved_ref[...], normed_ref[...]).astype(BF16)
        d_ffn_t_ref[...] = nt(moved_ref[...], d_ffn_ref[...]).astype(BF16)

    normed, d_ffn = normed_ref[...], d_ffn_ref[...]
    w_gate, w_up, w_down = gate_up_ref[0], gate_up_ref[1], down_ref[...]
    gate = jnp.dot(normed, w_gate, preferred_element_type=F32)
    up = jnp.dot(normed, w_up, preferred_element_type=F32)
    d_hidden = nt(d_ffn, w_down)
    sigma = jax.nn.sigmoid(gate)
    value = gate * sigma
    hid = (value * up).astype(BF16)
    d_up = (d_hidden * value).astype(BF16)
    d_gate = (d_hidden * up * (sigma + value * (1.0 - sigma))).astype(BF16)
    hidden_ref[...] = hid
    d_up_ref[...] = d_up
    d_gate_ref[...] = d_gate
    ffn = jnp.dot(hid, w_down, preferred_element_type=F32)
    d_normed = nt(d_gate, w_gate) + nt(d_up, w_up)

    @pl.when(step == 0)
    def _():
        ffn_ref[...] = ffn
        d_normed_ref[...] = d_normed

    @pl.when(jnp.logical_and(step > 0, step < last))
    def _():
        ffn_ref[...] += ffn
        d_normed_ref[...] += d_normed

    @pl.when(step == last)
    def _():
        ffn_out_ref[...] = (ffn_ref[...] + ffn).astype(ffn_out_ref.dtype)
        total = d_normed_ref[...] + d_normed
        cut = total.shape[0] // 2
        d_normed_top_ref[...] = total[:cut].astype(d_normed_top_ref.dtype)
        d_normed_low_ref[...] = total[cut:].astype(d_normed_low_ref.dtype)


def ffn_grad_body(
    normed_t_ref, normed_t_far_ref, d_ffn_t_ref, d_ffn_t_far_ref,
    d_gate_ref, d_gate_far_ref, d_up_ref, d_up_far_ref, hidden_ref, hidden_far_ref, out_ref,
):
    normed_t = (normed_t_ref, normed_t_far_ref)
    d_ffn_t = (d_ffn_t_ref, d_ffn_t_far_ref)
    for k, (left_t, near, far) in enumerate(
        (
            (normed_t, d_gate_ref, d_gate_far_ref),
            (normed_t, d_up_ref, d_up_far_ref),
            (d_ffn_t, hidden_ref, hidden_far_ref),
        )
    ):
        out_ref[k] = (
            jnp.dot(left_t[0][...], near[...], preferred_element_type=F32)
            + jnp.dot(left_t[1][...], far[...], preferred_element_type=F32)
        ).astype(BF16)


def mix_body(
    middle_ref, ffn_ref, ffn_far_ref, dout_ref, member_ref, mod_ref, d_mods_ref, d_mix_ref,
    info_ref, mixed_ref, known_ref, gate_sum
):
    member = member_ref[...]
    ffn = ffn_ref[...] + ffn_far_ref[...].astype(F32)
    scale = jnp.dot(member, mod_ref[...], preferred_element_type=F32)
    mixed_ref[...] = (middle_ref[...] + scale * ffn).astype(BF16)
    part = tn(member, (dout_ref[...].astype(F32) * ffn).astype(BF16))

    @pl.when(pl.program_id(0) == 0)
    def _():
        gate_sum[...] = part

    @pl.when(pl.program_id(0) == pl.num_programs(0) - 1)
    def _():
        slots = known_ref.shape[0]
        low = 0
        for values in (d_mods_ref[:slots], gate_sum[:slots] + part[:slots], d_mix_ref[...],
                       info_ref[...]):
            known_ref[:, low : low + values.shape[1]] = values.astype(BF16)
            low += values.shape[1]


def middle_back_body(
    at_ref, top_ref, low_ref, top_far_ref, low_far_ref, middle_ref, branch_ref, dout_ref, member_ref,
    mod_ref, own_ref, piece_0, piece_1, d_middle_ref, d_attended_ref, d_attn_ref, d_mods_ref
):
    step = pl.program_id(0)
    rows, width = top_ref.shape
    half = width // 2

    @pl.when(step == 0)
    def _():
        d_mods_ref[...] = jnp.zeros_like(d_mods_ref)

    member = member_ref[...]

    def mods(k):
        return jnp.dot(
            member, mod_ref[:, k * width : (k + 1) * width], preferred_element_type=F32
        )

    def add_mods(k, values):
        d_mods_ref[:, k * width : (k + 1) * width] += tn(member, values.astype(BF16))

    middle = middle_ref[...]
    m_hat, inverse = norm_parts(middle)
    d_normed = jnp.where(
        step == 0,
        top_ref[...] + top_far_ref[...].astype(F32),
        low_ref[...] + low_far_ref[...].astype(F32),
    )
    add_mods(1, d_normed)
    add_mods(2, d_normed * m_hat)
    d_hat = d_normed * (1.0 + mods(4))
    d_middle = dout_ref[...].astype(F32) + inverse * (
        d_hat
        - jnp.mean(d_hat, axis=-1, keepdims=True)
        - m_hat * jnp.mean(d_hat * m_hat, axis=-1, keepdims=True)
    )
    d_middle_ref[...] = d_middle
    add_mods(0, d_middle * branch_ref[...])
    d_attn = (mods(2) * d_middle).astype(BF16)
    d_attn_ref[...] = d_attn
    d_attended_ref[:, :half] = nt(d_attn, own_ref[...]).astype(BF16)

    d_attended_ref[:, half:] = sum(
        nt(d_attn_ref[:, columns_at(at_ref, r, half)], piece[...])
        for r, piece in enumerate((piece_0, piece_1))
    ).astype(BF16)


def attention_grad_body(
    q_ref, own_ref, far_ref, d_left_ref, normed_ref, d_attn_ref, attended_ref, attended_other_ref,
    moved_ref, d_proj_ref, back_ref, keep_ref, send_ref
):
    width = normed_ref.shape[1]
    half = width // 2
    d_proj_ref[:, :width] = q_ref[...]
    total = (own_ref[...].astype(F32) + far_ref[...].astype(F32)).astype(BF16)
    d_proj_ref[:, width:] = total[:, : 2 * width]
    pair_width = d_left_ref.shape[1]
    back_ref[:, :pair_width] = d_left_ref[...]
    back_ref[:, pair_width:] = total[:, 2 * width :]
    turned = nt(moved_ref[...], normed_ref[...]).astype(BF16)
    for j in range(4):
        if j == 3:
            turned = nt(moved_ref[...], d_attn_ref[...]).astype(BF16)
            right_side = jnp.concatenate([attended_ref[...], attended_other_ref[...]], axis=1)
        else:
            right_side = d_proj_ref[:, j * width : (j + 1) * width]
        total = jnp.dot(turned, right_side, preferred_element_type=F32).astype(BF16)
        for k in range(2):
            keep_ref[k, j] = total[:half, k * half : (k + 1) * half]
            send_ref[k, j] = total[half:, k * half : (k + 1) * half]


def chain_parts(early_ref):
    groups, _, doubled, columns = early_ref.shape
    count = groups * doubled
    return early_ref[:, 0].reshape(count, columns), early_ref[:, 1].reshape(count, columns)


def early_chain_body(here_ref, early_ref, mod_weight_ref, weight_out, bias_out, d_cond_out, mix_out):
    step = pl.program_id(0)
    width = mod_weight_ref.shape[1]
    wide = mod_weight_ref.shape[0]
    modded = 2 * width
    mixed = modded + mix_out.shape[1]
    first, second = chain_parts(early_ref)
    cond = first[:, mixed : mixed + wide]

    def block(low):
        summed = first[:, low : low + width].astype(F32) + second[:, low : low + width].astype(F32)
        early = summed.astype(BF16)
        weight_out[...] = tn(cond, early)
        bias_out[...] = jnp.sum(summed, axis=0, keepdims=True)
        return nt(early, mod_weight_ref[...])

    @pl.when(step == 0)
    def _():
        d_cond_out[...] = block(0)

    @pl.when(step == 1)
    def _():
        d_cond_out[...] += block(width)
        mix = first[:, modded:mixed].astype(F32) + second[:, modded:mixed].astype(F32)
        mix = jnp.sum(mix.reshape(-1, 2, early_ref.shape[2] // 2, mixed - modded), axis=0)
        own = mix_out.shape[0]
        own_half = mix[0, :own] + mix[1, own : 2 * own]
        other_half = mix[0, own : 2 * own] + mix[1, :own]
        mix_out[...] = jnp.where((here_ref[0] & 1) == 0, own_half, other_half)


def late_chain_body(
    far_count, pair_columns, here_ref, early_ref, held_ref, near_ref, mod_weight_ref, d_cond_ref,
    weight_in, weight_out, bias_out, time_out, cath_out
):
    count = held_ref.shape[0]
    slots = early_ref.shape[2] // 2
    wide = mod_weight_ref.shape[0]
    first, _ = chain_parts(early_ref)
    low = 2 * mod_weight_ref.shape[1] + pair_columns
    cond, times, slope = (first[:, low + k * wide : low + (k + 1) * wide] for k in range(3))
    arches = first[:, low + 3 * wide :]
    row = lax.broadcasted_iota(jnp.int32, (count, count), 0)
    column = lax.broadcasted_iota(jnp.int32, (count, count), 1)
    place = column // slots
    apart = (place % far_count) * 4 + place // far_count
    order = ((apart ^ here_ref[0]) * slots + column % slots == row).astype(BF16)
    late = (
        jnp.dot(order, held_ref[...], preferred_element_type=F32)
        + jnp.dot(order, near_ref[...], preferred_element_type=F32)
    ).astype(BF16)
    weight_out[...] = tn(cond, late)
    bias_out[...] = jnp.sum(late.astype(F32), axis=0, keepdims=True)
    d_cond = (nt(late, mod_weight_ref[...]) + d_cond_ref[...]) * slope.astype(F32)
    high = d_cond.astype(BF16)
    rest = (d_cond - high.astype(F32)).astype(BF16)
    time_out[...] = tn(times, high) + tn(times, rest)
    cath_out[...] = (tn(arches, high) + tn(arches, rest))[: cath_out.shape[0]]


def deliver_body(stays_ref, *refs):
    own_ref, came_ref, outs = refs[0], refs[1], refs[2:]

    def deliver(source):
        low = 0
        for ref in outs:
            ref[...] = source[:, low : low + ref.shape[1]]
            low += ref.shape[1]

    @pl.when(stays_ref[0] == 1)
    def _():
        deliver(own_ref)

    @pl.when(stays_ref[0] == 0)
    def _():
        deliver(came_ref)


def input_back_body(
    at_ref, d_proj_ref, x_ref, d_middle_ref, member_ref, mod_ref, own_ref, piece_0, piece_1,
    grad_ref, d_mods_ref, total_ref
):
    width = x_ref.shape[1]
    half = width // 2

    def product(weights, low):
        return sum(
            nt(d_proj_ref[:, j * width + low : j * width + low + half], weights[j])
            for j in range(3)
        )

    total_ref[...] = product(own_ref, 0)
    for r, piece in enumerate((piece_0, piece_1)):
        total_ref[:, columns_at(at_ref, r, half)] += product(piece, half)
    d_normed = total_ref[...]
    member = member_ref[...]
    scale = jnp.dot(member, mod_ref[:, width:], preferred_element_type=F32)
    x_hat, inverse = norm_parts(x_ref[...].astype(F32))
    slots = d_mods_ref.shape[0]
    d_mods_ref[:, :width] = tn(member, d_normed.astype(BF16))[:slots].astype(BF16)
    d_mods_ref[:, width:] = tn(member, (d_normed * x_hat).astype(BF16))[:slots].astype(BF16)
    d_hat = d_normed * (1.0 + scale)
    grad_ref[...] = (
        d_middle_ref[...]
        + inverse
        * (
            d_hat
            - jnp.mean(d_hat, axis=-1, keepdims=True)
            - x_hat * jnp.mean(d_hat * x_hat, axis=-1, keepdims=True)
        )
    ).astype(BF16)


ANYWHERE = pl.BlockSpec(memory_space=pl.ANY)
IN_SMEM = pl.BlockSpec(memory_space=pltpu.SMEM)


def call(body, operands, specs, outs, out_specs, scratch, flops, name, grid=(1,)):
    moved = sum(math.prod(a.shape) * a.dtype.itemsize for a in operands) + sum(
        math.prod(o.shape) * jnp.dtype(o.dtype).itemsize for o in outs
    )
    return pl.pallas_call(
        body,
        grid=grid,
        in_specs=specs,
        out_specs=out_specs,
        out_shape=outs,
        scratch_shapes=scratch,
        compiler_params=pltpu.CompilerParams(vmem_limit_bytes=VMEM_LIMIT),
        cost_estimate=pl.CostEstimate(
            flops=flops // COST_CUT, bytes_accessed=moved // COST_CUT, transcendentals=0
        ),
        name=name,
    )(*operands)


def added(first, second):
    return first + second


def adder(cut, operands, shapes, name):
    def body(*refs):
        count = len(operands)
        for ref, value in zip(refs[count:], cut(*[ref[...] for ref in refs[:count]])):
            ref[...] = value

    outs = [shaped(shape) for shape in shapes]
    return call(
        body, operands, [whole(a) for a in operands], outs, [whole(a) for a in outs], [], 0, name
    )


def first_sum_body(keep_ref, far_ref, sent_a, rest_a, sent_b, rest_b):
    total = added(keep_ref[0], far_ref[0])
    rows, side = sent_a.shape[1:]
    rest_a[0], sent_a[0] = total[:rows, :side], total[rows:, :side]
    quarter = rows // 2
    for k in range(2):
        low = k * rows
        rest_b[0, k] = total[low : low + quarter, side:]
        sent_b[0, k] = total[low + quarter : low + rows, side:]


def shaped(shape, dtype=BF16):
    return jax.ShapeDtypeStruct(shape, dtype)


def make_moves(dp_count):
    def pairs(target):
        moved = []
        for d in range(dp_count):
            for m in range(2):
                to_d, to_m = target(d, m)
                if (to_d, to_m) != (d, m):
                    moved.append((d * 2 + m, to_d * 2 + to_m))
        return moved

    def mover(target):
        table = pairs(target)
        return lambda array: lax.ppermute(array, AXES, table)

    turn = mover(lambda d, m: ((d & ~1) | m, d & 1))
    turn_far = mover(lambda d, m: ((d & ~1) | m, 1 - (d & 1)))
    across = mover(lambda d, m: (d, 1 - m))

    def flip(bit):
        return mover(lambda d, m: (d ^ (1 << bit), m))

    def to(mask, over):
        return mover(lambda d, m: (d ^ mask, m ^ over))

    return turn, turn_far, across, flip, to


def shards(
    tokens,
    pair_left,
    pair_right,
    chain_len,
    chain_time,
    chain_arch,
    cath_table,
    time_weight,
    mod_weight,
    mod_bias,
    qkv_weight,
    pair_weight,
    out_weight,
    gate_up_weight,
    down_weight,
    cotangent,
):
    dp_count = lax.axis_size("dp")
    bits = dp_count.bit_length() - 1
    turn, turn_far, across, flip, to = make_moves(dp_count)
    core_swap = flip(0)
    dp_at = lax.axis_index("dp")
    mp_at = lax.axis_index("mp")
    core = dp_at & 1
    rows, width = tokens.shape
    slots = chain_len.shape[1]
    half_heads = pair_weight.shape[1]
    heads = 2 * half_heads
    pair_width = pair_left.shape[1]
    cond_width = time_weight.shape[0]
    half = width // 2
    hidden = down_weight.shape[0]

    def after(array, *earlier):
        return lax.optimization_barrier((array, *earlier))[0]

    def beside(made, *received):
        return lax.optimization_barrier((*made, *received))[: len(made)]

    held_chains = jnp.concatenate(
        [chain_len.astype(F32), chain_time, chain_arch.astype(F32)], axis=0
    )
    near_chains = core_swap(held_chains)

    cut = width // 2
    stays = core == mp_at

    def turned_in(array, *earlier):
        return jnp.where(stays, array, turn(after(array, *earlier)))

    pair_mix_other = across(pair_weight)
    x_in = turned_in(tokens)
    right_own = turned_in(pair_right, x_in)
    left_in = turned_in(pair_left, x_in)
    qkv_y = across(after(lax.dynamic_slice_in_dim(qkv_weight, core * cut, cut, 1), x_in))
    out_y = across(after(lax.dynamic_slice_in_dim(out_weight, core * cut, cut, 1), qkv_y))
    dout = turned_in(cotangent, out_y)
    dout_far = turn_far(after(cotangent, out_y))

    def ends_of(chains):
        return jnp.cumsum(chains[0].astype(jnp.int32))

    chains = jnp.where(core == mp_at, held_chains, near_chains)
    far_chains = jnp.where(core == mp_at, near_chains, held_chains)
    arches = chains[2].astype(jnp.int32)
    ends = ends_of(chains)
    times = jnp.concatenate([chains[1], far_chains[1]])

    def ids_of(part, ends=ends):
        positions = jnp.arange(rows, dtype=jnp.int32) + part * rows
        return jnp.sum((positions[:, None] >= ends[None, :]).astype(jnp.int32), axis=1)

    own_ids = ids_of(core)
    key_ids = jnp.concatenate([own_ids, ids_of(1 - core)])
    chain_numbers = jnp.arange(slots, dtype=jnp.int32)
    doubled = jnp.concatenate([chain_numbers, chain_numbers])[None, :]
    member = (own_ids[:, None] == doubled).astype(BF16)
    member_far = (ids_of(core, ends_of(far_chains))[:, None] == doubled).astype(BF16)
    lanes = jnp.arange(128, dtype=jnp.int32)[None, :] & 63
    hot = (own_ids[:, None] == lanes).astype(BF16)
    pens = jnp.where((key_ids[:, None] != lanes) & (lanes <= slots), -1e30, 0.0).astype(BF16)
    pen_own, pen_near = pens[:rows], pens[rows:]

    half_cond = cond_width // 2
    frequency = jnp.exp(jnp.arange(half_cond, dtype=F32) * (-math.log(10000.0) / half_cond))
    angles = times[:, None] * 1000.0 * frequency[None, :]
    time_embed = jnp.concatenate([jnp.sin(angles), jnp.cos(angles)], axis=1).astype(BF16)
    both_arches = jnp.concatenate([arches, far_chains[2].astype(jnp.int32)])
    arch_onehot = (
        both_arches[:, None] == jnp.arange(cath_table.shape[0], dtype=jnp.int32)[None, :]
    ).astype(F32)
    cond_pre = dot_f32(time_embed, time_weight) + highest_dot(arch_onehot, cath_table.astype(F32))
    cond_value, cond_slope = silu_parts(cond_pre)
    cond_act = cond_value.astype(BF16)
    chain_mod = dot_f32(cond_act, mod_weight) + mod_bias.astype(F32)[None, :]
    mod_high = lax.reduce_precision(chain_mod, 8, 7)
    mod_low = (chain_mod - mod_high).astype(BF16)
    mod_high = mod_high.astype(BF16)
    mods = jnp.concatenate([mod_high[:slots], mod_low[:slots]], axis=0)
    gate_far = jnp.concatenate([mod_high[slots:], mod_low[slots:]], axis=0)[:, 5 * width :]
    arch_low = (arches[:, None] == jnp.arange(128, dtype=jnp.int32)[None, :]).astype(BF16)
    info = jnp.concatenate(
        [cond_act[:slots], time_embed[:slots], cond_slope[:slots].astype(BF16), arch_low], axis=1
    )

    order = [int(format(p, "0%db" % bits)[::-1], 2) for p in range(dp_count)]
    block_at = jnp.array(order, jnp.int32) ^ dp_at
    block_rows = width // dp_count
    source = (block_at[:, None] * block_rows + jnp.arange(block_rows)[None, :]).reshape(-1)
    moved = (source[:, None] == jnp.arange(width)[None, :]).astype(BF16)
    at = core.reshape(1).astype(jnp.int32)
    semaphores = pltpu.SemaphoreType.DMA

    mod_a = mods[:, : 2 * width]
    pair_mix = jnp.concatenate([pair_weight, pair_mix_other], axis=1).astype(F32)
    mix_rows = jnp.transpose(pair_mix).reshape(half_heads, 2, -1)
    part_shape = shaped((rows, half))
    operands = [after(x_in, moved, mods, hot, pens, member_far, gate_far, mix_rows, info), member, mod_a,
                qkv_weight]
    made = call(
        qkv_body,
        operands,
        [whole(a) for a in operands],
        [part_shape, shaped((rows, width)), shaped((rows, width))],
        [whole(part_shape), whole(shaped((rows, width))), whole(shaped((rows, width)))],
        [],
        3 * rows * width * width,
        "project",
    )
    queries, kv_own, normed_a = beside(made, right_own, left_in)
    kv_near, right_near = core_swap(kv_own), core_swap(right_own)
    factors = (right_own, right_near, pen_own, pen_near)
    made = attention_forward(0, mix_rows, queries, left_in, hot, kv_own, kv_near, *factors)
    made = beside(made, qkv_y)
    qkv_y = after(qkv_y, made[0])
    qkv_pieces = [qkv_y, core_swap(qkv_y)]
    first_half = (*made, queries, kv_own, kv_near)
    made = call(
        qkv_other_body,
        [at, after(normed_a, made[0]), *qkv_pieces],
        [IN_SMEM, whole(normed_a), whole(qkv_y), whole(qkv_y)],
        [part_shape, shaped((rows, width))],
        [whole(part_shape), whole(shaped((rows, width)))],
        [],
        3 * rows * width * width,
        "project_other",
    )
    queries, kv_own = beside(made, out_y)
    out_pieces = [out_y, core_swap(out_y)]
    kv_near = core_swap(kv_own)
    made = attention_forward(1, mix_rows, queries, left_in, hot, kv_own, kv_near, *factors)
    made = beside(made, *out_pieces)
    second_half = (*made, queries, kv_own, kv_near)
    attended, attended_other = first_half[0], second_half[0]
    wide = shaped((rows, width), F32)
    thin = shaped((rows, width))
    middle, branch, normed_f = call(
        branch_body,
        [at, attended, attended_other, out_weight, *out_pieces, x_in, member, mods],
        [IN_SMEM]
        + [whole(a) for a in (attended, attended_other, out_weight, *out_pieces, x_in, member, mods)],
        [wide, wide, thin],
        [whole(thin)] * 3,
        [],
        2 * rows * width * width,
        "branch",
    )

    normed_far = across(normed_f)
    gate_mod = mods[:, 5 * width :]
    block = FFN_BLOCK
    active = shaped((rows, hidden))
    turned = shaped((width, rows))

    def feed_forward(normed, dout, member, gate, sum_type):
        column = pl.BlockSpec((rows, block), lambda i: (0, i))
        summed = shaped((rows, width), sum_type)
        part = shaped((rows // 2, width), sum_type)
        return call(
            ffn_body,
            [normed, dout, member, gate, moved, gate_up_weight, down_weight],
            [whole(a) for a in (normed, dout, member, gate, moved)]
            + [
                pl.BlockSpec((2, width, block), lambda i: (0, 0, i)),
                pl.BlockSpec((block, width), lambda i: (i, 0)),
            ],
            [summed, part, part, turned, turned, active, active, active],
            [whole(thin), whole(part), whole(part), whole(turned), whole(turned), column, column, column],
            [
                pltpu.VMEM((rows, width), F32), pltpu.VMEM((rows, width), F32),
                pltpu.VMEM((rows, width), BF16),
            ],
            12 * rows * width * hidden,
            "feed_forward",
            (hidden // block,),
        )

    made = feed_forward(normed_f, dout, member, gate_mod, F32)
    ffn, d_normed_top, d_normed_low, normed_t, d_ffn_t, d_gate, d_up, hid = made
    normed_far, dout_far = lax.optimization_barrier((normed_far, dout_far, *made))[:2]
    ffn_for, top_for, low_for, normed_t_far, d_ffn_t_far, d_gate_far, d_up_far, hid_far = feed_forward(
        normed_far, dout_far, member_far, gate_far, BF16
    )
    top_far, low_far = across(top_for), across(low_for)

    grad = shaped((3, half, hidden))
    grad_block = pl.BlockSpec((3, half, GRAD_BLOCK), lambda i: (0, 0, i))
    column = pl.BlockSpec((rows, GRAD_BLOCK), lambda i: (0, i))
    turned_half = [normed_t, normed_t_far, d_ffn_t, d_ffn_t_far]
    sides = [d_gate, d_gate_far, d_up, d_up_far, hid, hid_far]

    def ffn_grads(part, *earlier):
        row_half = pl.BlockSpec((half, rows), lambda i: (part, 0))
        return call(
            ffn_grad_body,
            [after(turned_half[0], *earlier), *turned_half[1:], *sides],
            [row_half] * 4 + [column] * 6,
            [grad],
            [grad_block],
            [],
            6 * rows * width * hidden,
            "feed_forward_grads",
            (hidden // GRAD_BLOCK,),
        )[0]

    (send,) = beside((ffn_grads(1),), top_far)
    far = core_swap(send)
    (keep,) = beside((ffn_grads(0, send),), far, low_far)
    ffn_far = across(after(ffn_for, keep))

    def plus(kept, received):
        return (kept.astype(F32) + received.astype(F32)).astype(BF16)

    def halves(array, upper):
        size = array.shape[-2] // 2
        return array[..., size:, :] if upper else array[..., :size, :]

    def y_part(kept, received):
        return plus(kept[1], received[1])

    def y_rest(kept, received):
        return plus(kept[0], received[0])

    def bit_part(kept, received):
        return plus(halves(kept, True), halves(received, True))

    def bit_rest(kept, received):
        return plus(halves(kept, False), halves(received, False))

    steps = 2
    row_block = pl.BlockSpec((rows // steps, width), lambda i: (i, 0))
    member_block = pl.BlockSpec((rows // steps, 2 * slots), lambda i: (i, 0))
    mods_early = shaped((2 * slots, 3 * width), F32)
    made = call(
        middle_back_body,
        [at, after(d_normed_top, keep), d_normed_low, top_far, low_far, middle, branch, dout,
         member, mods, out_weight, *out_pieces],
        [IN_SMEM] + [whole(d_normed_top)] * 4 + [row_block] * 3
        + [member_block, whole(mods), whole(out_weight), whole(out_y), whole(out_y)],
        [wide, thin, thin, mods_early],
        [row_block, row_block, row_block, whole(mods_early)],
        [],
        4 * rows * width * width,
        "middle_back",
        (steps,),
    )
    d_middle, d_attended, d_attn, d_mods = made
    side = hidden // 2
    shape_a, shape_b = (3, half // 2, side), (3, 2, half // 4, side)
    block_a = pl.BlockSpec((1, *shape_a[1:]), lambda i: (i, 0, 0))
    block_b = pl.BlockSpec((1, *shape_b[1:]), lambda i: (i, 0, 0, 0))
    sent, rest, sent_b, rest_b = call(
        first_sum_body,
        [keep, far],
        [pl.BlockSpec((1, half, hidden), lambda i: (i, 0, 0))] * 2,
        [shaped(shape_a), shaped(shape_a), shaped(shape_b), shaped(shape_b)],
        [block_a, block_a, block_b, block_b],
        [],
        0,
        "first_sum",
        (3,),
    )
    got, got_b = flip(1)(sent), flip(2)(sent_b)

    def finish(bit, kept, sent):
        while bit < bits:
            received = flip(bit)(sent)
            bit += 1
            if bit < bits:
                kept, sent = bit_rest(kept, received), bit_part(kept, received)
        return kept.astype(F32) + received.astype(F32)

    near_bits = [-1, 1] if bits > 1 else [-1]
    far_bits = list(range(2, bits))

    def several(group):
        moves = []
        for chosen in range(1, 1 << len(group)):
            mask, over = 0, 0
            for k, bit in enumerate(group):
                if chosen >> k & 1:
                    mask, over = (mask, 1) if bit < 0 else (mask | 1 << bit, over)
            moves.append((mask, over))
        return moves

    def gather_step(group, held):
        return jnp.concatenate(
            [held] + [to(mask, over)(held) for mask, over in several(group)], axis=0
        )

    made = attention_backward(
        mix_rows, after(d_attended, sent, sent_b), (first_half, second_half), left_in, *factors
    )
    d_query, d_own, d_far, d_left = beside(made[:4], ffn_far, got, got_b)

    def second_cut(rest, got, rest_b, got_b):
        total, total_b = added(rest, got), added(rest_b, got_b)
        rows = total.shape[1] // 2
        return total[:, rows:], total[:, :rows], total_b[:, 1], total_b[:, 0]

    shape = (3, half // 4, side)
    sent, rest, sent_b, rest_b = adder(
        second_cut, [rest, got, rest_b, got_b], [shape] * 4, "second_sum"
    )
    got, got_b = flip(2)(sent), flip(1)(sent_b)
    d_mix = made[4]
    far_kv = core_swap(d_far)

    known = shaped((slots, 4 * width + d_mix.shape[1] + info.shape[1]))
    mixed, known = call(
        mix_body,
        [after(middle, d_far, sent, sent_b), ffn, ffn_far, dout, member, gate_mod, d_mods, d_mix,
         info],
        [row_block] * 4 + [member_block] + [whole(a) for a in (gate_mod, d_mods, d_mix, info)],
        [thin, known],
        [row_block, whole(known)],
        [pltpu.VMEM((2 * slots, width), F32)],
        4 * rows * 16 * width,
        "mix",
        (steps,),
    )
    mixed, known = beside((mixed, known), far_kv)
    mixed_own, mixed = mixed, turn(mixed)
    early = lax.all_gather(known, AXES, axis=0, tiled=False)

    proj_grad = shaped((rows, 3 * width))
    back = shaped((rows, 2 * pair_width))
    grad = shaped((2, 4, half, half))
    operands = [d_query, d_own, far_kv, d_left, after(normed_a, known), d_attn, attended,
                attended_other, moved]
    outs = [proj_grad, back, grad, grad]
    made = call(
        attention_grad_body,
        operands,
        [whole(a) for a in operands],
        outs,
        [whole(a) for a in outs],
        [],
        12 * rows * width * width,
        "attention_grads",
    )
    d_proj, back, keep_qkvo, send_qkvo = beside(made, got, got_b, mixed)
    far_qkvo = core_swap(send_qkvo)
    stay_flag = stays.reshape(1).astype(jnp.int32)

    def delivered(own, came, widths):
        blocks = [pl.BlockSpec((rows // 2, w), lambda i: (i, 0)) for w in [own.shape[1]] * 2 + widths]
        return call(
            deliver_body,
            [stay_flag, own, came],
            [IN_SMEM, *blocks[:2]],
            [shaped((rows, w)) for w in widths],
            blocks[2:],
            [],
            0,
            "deliver",
            (2,),
        )

    (mixed,) = delivered(mixed_own, after(mixed, d_proj), [width])
    keep_qkvo = after(keep_qkvo, mixed)
    back_own, back = back, turn(back)

    def third_cut(rest, got, rest_b, got_b):
        total = jnp.concatenate([added(rest, got), added(rest_b, got_b)], axis=2)
        rows = total.shape[1] // 2
        return total[:, rows:], total[:, :rows]

    shape = (3, half // 8, hidden)
    sent, rest = adder(third_cut, [rest, got, rest_b, got_b], [shape] * 2, "third_sum")

    def qkvo_cut(keep, far):
        total = added(keep, far)
        rows = half // 2
        return total[1, :2], total[0, :2], total[:, 2:, rows:], total[:, 2:, :rows]

    shape, shape_vo = (2, half, half), (2, 2, half // 2, half)
    sent_qk, rest_qk, sent_vo, rest_vo = adder(
        qkvo_cut, [keep_qkvo, far_qkvo], [shape, shape, shape_vo, shape_vo], "qkvo_sum"
    )
    got_qk, got_vo = across(sent_qk), flip(1)(sent_vo)
    mods_late = shaped((slots, 2 * width))
    operands = [at, after(d_proj, sent_qk, sent_vo, sent), x_in, d_middle, member, mod_a,
                qkv_weight, *qkv_pieces]
    made = call(
        input_back_body,
        operands,
        [IN_SMEM] + [whole(a) for a in operands[1:]],
        [thin, mods_late],
        [whole(thin), whole(mods_late)],
        [pltpu.VMEM((rows, width), F32)],
        6 * rows * width * width,
        "input_back",
    )
    tokens_out, held = beside(made, got_qk, got_vo)
    got = flip(3)(sent)

    def together(*arrays):
        return lax.optimization_barrier(arrays)

    def qkvo_second(rest_qk, got_qk, rest_vo, got_vo):
        total, total_vo = added(rest_qk, got_qk), added(rest_vo, got_vo)
        rows = half // 2
        return total[:, rows:], total[:, :rows], total_vo[1], total_vo[0]

    shape = (2, half // 2, half)
    sent_qk, rest_qk, sent_vo, rest_vo = adder(
        qkvo_second, [after(rest_qk, tokens_out), got_qk, rest_vo, got_vo], [shape] * 4, "qkvo_second"
    )
    got_qk, got_vo = flip(1)(sent_qk), across(sent_vo)
    token_gradient = turn(after(tokens_out, sent_vo))
    held = gather_step(far_bits, held)

    def qkvo_third(rest_qk, got_qk, rest_vo, got_vo):
        total = jnp.concatenate([added(rest_qk, got_qk), added(rest_vo, got_vo)], axis=0)
        rows = half // 4
        return total[:, rows:], total[:, :rows]

    shape = (4, half // 4, half)
    sent_qkvo, qkvo = adder(
        qkvo_third, [rest_qk, got_qk, rest_vo, got_vo], [shape] * 2, "qkvo_third"
    )
    left_grad, right_grad = delivered(back_own, after(back, tokens_out), [pair_width, pair_width])
    held, qkvo, sent_qkvo, token_gradient = together(
        held, qkvo, sent_qkvo, token_gradient, left_grad, right_grad
    )[:4]
    held = gather_step(near_bits, held)
    got_qkvo = flip(2)(sent_qkvo)
    here = ((dp_at >> 1) * 2 + mp_at).reshape(1).astype(jnp.int32)
    early = early.reshape(dp_count // 2, 2, 2 * slots, -1)
    late_to = 2 * width
    weight_shape = shaped(mod_weight.shape, F32)
    bias_shape = shaped((1, 6 * width), F32)
    cond_shape = shaped((dp_count * slots, cond_width), F32)
    mix_shape = shaped((half_heads // 2, 2 * pair_width), F32)
    later = lambda i: (0, 1 + i)
    early = after(early, tokens_out, sent_qkvo)
    early_weight, early_bias, early_cond, mix_sum = call(
        early_chain_body,
        [here, early, mod_weight],
        [IN_SMEM, whole(early), pl.BlockSpec((cond_width, late_to), later)],
        [weight_shape, bias_shape, cond_shape, mix_shape],
        [
            pl.BlockSpec((cond_width, late_to), later), pl.BlockSpec((1, late_to), later),
            whole(cond_shape), whole(mix_shape),
        ],
        [],
        0,
        "early_chains",
        (2,),
    )
    mix_sum = mix_sum.reshape(half_heads, -1)
    taken = mix_sum.shape[1] // dp_count
    pair_sum = jnp.transpose(lax.dynamic_slice_in_dim(mix_sum, dp_at * taken, taken, 1))
    def last_sums(kept, got):
        for bit in range(4, bits):
            kept, got = bit_rest(kept, got), flip(bit)(bit_part(kept, got))
        total = kept[:-1].astype(F32) + got[:-1].astype(F32)
        return total, jnp.transpose(kept[-1].astype(F32) + got[-1].astype(F32))

    ffn_sum, down_sum = last_sums(after(rest, sent_vo), got)
    (token_gradient,) = delivered(tokens_out, token_gradient, [width])
    held, got_qkvo = together(
        held, got_qkvo, early_weight, pair_sum, ffn_sum, down_sum, token_gradient
    )[:2]
    near = core_swap(held)
    sent_qkvo, qkvo = bit_part(qkvo, got_qkvo), bit_rest(qkvo, got_qkvo)
    got_qkvo = flip(3)(sent_qkvo)

    late_bias_shape = shaped((1, late_to), F32)
    operands = [here, early, held, near]
    time_shape, cath_shape = shaped((cond_width, cond_width), F32), shaped(cath_table.shape, F32)
    first_columns = pl.BlockSpec((cond_width, late_to), lambda i: (0, 0))
    mod_weight_sum, late_bias, time_sum, cath_sum = pl.pallas_call(
        functools.partial(late_chain_body, dp_count // 4, mix_shape.shape[1]),
        grid=(1,),
        in_specs=[IN_SMEM]
        + [whole(a) for a in operands[1:]]
        + [first_columns, whole(cond_shape), ANYWHERE],
        out_specs=[first_columns, whole(late_bias_shape), whole(time_shape), whole(cath_shape)],
        out_shape=[weight_shape, late_bias_shape, time_shape, cath_shape],
        input_output_aliases={6: 0},
        compiler_params=pltpu.CompilerParams(vmem_limit_bytes=VMEM_LIMIT),
        name="late_chains",
    )(*operands, mod_weight, early_cond, early_weight)
    mod_bias_sum = jnp.concatenate([late_bias, early_bias[:, late_to:]], axis=1).reshape(-1)

    got_qkvo, _ = together(got_qkvo, mod_weight_sum)
    qkv_sum, out_sum = last_sums(qkvo, got_qkvo)

    return (
        mixed,
        token_gradient,
        left_grad,
        right_grad,
        cath_sum,
        time_sum,
        mod_weight_sum,
        mod_bias_sum,
        qkv_sum,
        pair_sum,
        out_sum,
        ffn_sum,
        down_sum,
    )


def solution(mesh):
    by_rows = P(AXES, None)
    placed = (
        by_rows,
        by_rows,
        by_rows,
        P("dp", None),
        P("dp", None),
        P("dp", None),
        P(),
        P(),
        P(),
        P(),
        P(None, None, "mp"),
        P(None, "mp"),
        P("mp", None),
        P(None, None, "mp"),
        P("mp", None),
        by_rows,
    )
    return jax.shard_map(
        shards,
        mesh=mesh,
        in_specs=placed,
        out_specs=(
            by_rows,
            by_rows,
            by_rows,
            by_rows,
            P(),
            P(),
            P(),
            P(),
            P(None, "dp", "mp"),
            P("dp", "mp"),
            P("mp", "dp"),
            P(None, "dp", "mp"),
            P("mp", "dp"),
        ),
        check_vma=False,
    )
```

```python
import functools
import math

import jax
import jax.numpy as jnp
from jax import lax
from jax.experimental import pallas as pl
from jax.experimental.pallas import tpu as pltpu
from jax.sharding import PartitionSpec as P

EPSILON = 1e-06
AXES = ("dp", "mp")
BF16 = jnp.bfloat16
F32 = jnp.float32
VMEM_LIMIT = 64 * 1024 * 1024
FFN_BLOCK = 512
GRAD_BLOCK = 768
BACK_PARTS = 1
COST_CUT = 20


def highest_dot(left_side, right_side):
    return jnp.dot(left_side, right_side, precision=lax.Precision.HIGHEST)


def silu_parts(values):
    sigma = jax.nn.sigmoid(values)
    return (values * sigma, sigma * (1.0 + values * (1.0 - sigma)))


def dot_f32(left_side, right_side):
    return jnp.dot(left_side, right_side, preferred_element_type=F32)


def dot_nt(left_side, right_side):
    return lax.dot_general(
        left_side, right_side, (((1,), (1,)), ((), ())), preferred_element_type=F32
    )

def lane_mix(first, second, odd):
    lane = lax.broadcasted_iota(jnp.int32, first.shape, 1)
    keep = (lane >= 64) if odd else (lane < 64)
    return jnp.where(keep, first, second)


def nt(left_side, right_side):
    return lax.dot_general(
        left_side, right_side, (((1,), (1,)), ((), ())), preferred_element_type=F32
    )


def attention_forward_body(
    pair_mix_ref, q_ref, left_ref, hot_ref, k_own_ref, k_near_ref, v_own_ref, v_near_ref,
    right_own_ref, right_near_ref, pen_own_ref, pen_near_ref,
    attended_ref, inverse_ref, probs_ref,
):
    rows = q_ref.shape[0]
    step = 512
    out_tiles = []
    left = left_ref[...].astype(F32)
    for odd in range(2):
        mix = pair_mix_ref[0, odd : odd + 1, :]
        left_mixed = (left * mix).astype(BF16)
        q_side = jnp.concatenate([left_mixed, lane_mix(q_ref[...], hot_ref[...], odd)], axis=1)
        k_own = jnp.concatenate(
            [right_own_ref[...], lane_mix(k_own_ref[...], pen_own_ref[...], odd)], axis=1
        )
        k_near = jnp.concatenate(
            [right_near_ref[...], lane_mix(k_near_ref[...], pen_near_ref[...], odd)], axis=1
        )
        v_own = lane_mix(v_own_ref[...], jnp.ones_like(v_own_ref[...]), odd)
        v_near = lane_mix(v_near_ref[...], jnp.ones_like(v_near_ref[...]), odd)
        tiles = []
        for start in range(0, rows, step):
            block = q_side[start : start + step]
            s_own = nt(block, k_own)
            s_near = nt(block, k_near)
            top = jnp.maximum(
                jnp.max(s_own, axis=1, keepdims=True), jnp.max(s_near, axis=1, keepdims=True)
            )
            e_own = jnp.exp(s_own - top).astype(BF16)
            e_near = jnp.exp(s_near - top).astype(BF16)
            probs_ref[odd, start : start + step, :rows] = e_own
            probs_ref[odd, start : start + step, rows:] = e_near
            tiles.append(
                jnp.dot(e_own, v_own, preferred_element_type=F32)
                + jnp.dot(e_near, v_near, preferred_element_type=F32)
            )
        out_tiles.append(jnp.concatenate(tiles, axis=0))
    sums = lane_mix(out_tiles[1], out_tiles[0], False)
    sums = pltpu.roll(sums, 64, 1)
    inverse = 1.0 / sums
    attended_ref[...] = (lane_mix(out_tiles[0], out_tiles[1], False) * inverse).astype(BF16)
    inverse_ref[...] = inverse


def attention_backward_body(
    pair_mix_ref, grad_ref, left_ref, right_own_ref, right_near_ref, pen_own_ref, pen_near_ref,
    *rest
):
    outs = rest[16:21]
    scores_ref, right_sum_ref, left_sum_ref, left_t_ref = rest[21:]
    pair = pl.program_id(0)
    pairs = pl.num_programs(0)

    @pl.when(pair == 0)
    def _():
        left_t_ref[...] = left_ref[...].T
        outs[4][...] = jnp.zeros_like(outs[4])
        right_sum_ref[...] = jnp.zeros_like(right_sum_ref)
        left_sum_ref[...] = jnp.zeros_like(left_sum_ref)

    common = (
        pair_mix_ref, grad_ref, left_ref, right_own_ref, right_near_ref, pen_own_ref, pen_near_ref,
        *outs, *rest[21:],
    )

    @pl.when(pair < pairs // 2)
    def _():
        attention_backward_pair(common, *rest[:8])

    @pl.when(pair >= pairs // 2)
    def _():
        attention_backward_pair(common, *rest[8:16])

    @pl.when(pair == pairs - 1)
    def _():
        rows = left_ref.shape[0]
        right = right_sum_ref[...].T.astype(BF16)
        outs[1][:, outs[1].shape[1] - right.shape[1] :] = right[:rows]
        outs[2][:, outs[1].shape[1] - right.shape[1] :] = right[rows:]
        outs[3][...] = left_sum_ref[...].astype(BF16)


def attention_backward_pair(
    common, attended_ref, inverse_ref, probs_ref, q_ref, k_own_ref, k_near_ref, v_own_ref,
    v_near_ref
):
    (
        pair_mix_ref, grad_ref, left_ref, right_own_ref, right_near_ref, pen_own_ref, pen_near_ref,
        d_q_ref, own_out, near_out, _, d_mix_ref,
        scores_ref, right_sum_ref, left_sum_ref, left_t_ref,
    ) = common
    pair = pl.program_id(0)
    rows = q_ref.shape[0]
    step = 256
    wide = grad_ref.shape[1] * pl.num_programs(0)
    scaled = (grad_ref[...].astype(F32) * inverse_ref[...]).astype(BF16)
    products = scaled.astype(F32) * attended_ref[...].astype(F32)
    scaled_t = scaled.T
    q_t = q_ref[...].T
    lane = lax.broadcasted_iota(jnp.int32, products.shape, 1)
    left = left_ref[...].astype(F32)
    left_t = left_t_ref[...].astype(F32)
    d_q, dk_t, dv_t = [], [], []
    for odd in range(2):
        mine = (lane >= 64) if odd else (lane < 64)
        delta = -jnp.sum(jnp.where(mine, products, 0.0), axis=1, keepdims=True)
        high = delta.astype(BF16).astype(F32)
        low = delta - high
        at = 0 if odd else 64
        extra = jnp.where(lane == at, high, jnp.where(lane == at + 1, low, 0.0)).astype(BF16)
        grad_side = jnp.where(mine, scaled, extra)
        mix = pair_mix_ref[0, odd : odd + 1, :]
        k_own = jnp.concatenate(
            [right_own_ref[...], lane_mix(k_own_ref[...], pen_own_ref[...], odd)], axis=1
        )
        k_near = jnp.concatenate(
            [right_near_ref[...], lane_mix(k_near_ref[...], pen_near_ref[...], odd)], axis=1
        )
        v_own = lane_mix(v_own_ref[...], jnp.ones_like(v_own_ref[...]), odd)
        v_near = lane_mix(v_near_ref[...], jnp.ones_like(v_near_ref[...]), odd)
        for start in range(0, rows, step):
            block = grad_side[start : start + step]
            own = nt(block, v_own).astype(BF16) * probs_ref[odd, start : start + step, :rows]
            near = nt(block, v_near).astype(BF16) * probs_ref[odd, start : start + step, rows:]
            scores_ref[start : start + step, :rows] = own
            scores_ref[start : start + step, rows:] = near
        d_query = jnp.dot(
            scores_ref[:, :rows], k_own, preferred_element_type=F32
        ) + jnp.dot(scores_ref[:, rows:], k_near, preferred_element_type=F32)
        width = left.shape[1]
        d_q.append(d_query[:, width:])
        d_pair = d_query[:, :width]
        left_sum_ref[...] += d_pair * mix
        d_mix_ref[pl.ds(pair, 1), odd * width : (odd + 1) * width] = jnp.sum(
            d_pair * left, axis=0, keepdims=True
        )
        mixed_t = (left_t * jnp.transpose(mix)).astype(BF16)
        low_row = 64 * odd
        q_side = jnp.concatenate([mixed_t, q_t[low_row : low_row + 64]], axis=0)
        d_key = jnp.dot(q_side, scores_ref[...], preferred_element_type=F32)
        right_sum_ref[...] += d_key[:width]
        dk_t.append(d_key[width:])
        dv_t.append(
            jnp.dot(
                scaled_t[low_row : low_row + 64], probs_ref[odd], preferred_element_type=F32
            )
        )
    d_q_ref[...] = (lane_mix(d_q[0], d_q[1], False) * 0.125).astype(BF16)
    for base, parts in ((0, dk_t), (wide, dv_t)):
        both = jnp.concatenate(parts, axis=0).T.astype(BF16)
        column = pl.multiple_of(base + pair * 128, 128)
        own_out[:, pl.ds(column, 128)] = both[:rows]
        near_out[:, pl.ds(column, 128)] = both[rows:]


def whole(array):
    zeros = (0,) * array.ndim
    return pl.BlockSpec(array.shape, lambda *_: zeros)


def attention_forward(
    part, pair_mix, queries, left, hot, kv_own, kv_near, right_own, right_near, pen_own, pen_near
):
    rows, width = queries.shape
    pairs = width // 128
    pair_width = left.shape[1]
    column = pl.BlockSpec((rows, 128), lambda p: (0, p))
    value_column = pl.BlockSpec((rows, 128), lambda p: (0, pairs + p))
    operands = [
        pair_mix, queries, left, hot, kv_own, kv_near, kv_own, kv_near, right_own, right_near,
        pen_own, pen_near,
    ]
    return call(
        attention_forward_body,
        operands,
        [
            pl.BlockSpec((1, 2, pair_width), lambda p: (part * pairs + p, 0, 0)), column,
            whole(left), whole(hot), column, column, value_column, value_column,
            whole(right_own), whole(right_near), whole(pen_own), whole(pen_near),
        ],
        [
            shaped((rows, width)), shaped((rows, width), F32),
            shaped((2 * pairs, rows, 2 * rows)),
        ],
        [column, column, pl.BlockSpec((2, rows, 2 * rows), lambda p: (p, 0, 0))],
        [],
        2 * 2 * pairs * rows * 2 * rows * 512,
        "attention_forward",
        (pairs,),
    )


def attention_backward(
    pair_mix, grad, halves, left, right_own, right_near, pen_own, pen_near
):
    rows, width = grad.shape
    pairs = width // 128
    here = pairs // 2
    pair_width = left.shape[1]
    column = pl.BlockSpec((rows, 128), lambda p: (0, p))
    mix = pl.BlockSpec((1, 2, pair_width), lambda p: (p, 0, 0))
    both = shaped((rows, 2 * width + pair_width))
    operands = [pair_mix, grad, left, right_own, right_near, pen_own, pen_near]
    specs = [mix, column] + [whole(a) for a in operands[2:]]
    for part, (attended, inverse, probs, queries, kv_own, kv_near) in enumerate(halves):
        at = lambda p, part=part: jnp.clip(p - part * here, 0, here - 1)
        own = pl.BlockSpec((rows, 128), lambda p, at=at: (0, at(p)))
        value = pl.BlockSpec((rows, 128), lambda p, at=at: (0, here + at(p)))
        operands += [attended, inverse, probs, queries, kv_own, kv_near, kv_own, kv_near]
        specs += [
            own, own, pl.BlockSpec((2, rows, 2 * rows), lambda p, at=at: (at(p), 0, 0)), own, own,
            own, value, value,
        ]
    outs = [
        shaped((rows, width)), both, both, shaped((rows, pair_width)),
        shaped((8, 2 * pair_width), F32),
    ]
    return call(
        attention_backward_body,
        operands,
        specs,
        outs,
        [column, whole(both), whole(both), whole(outs[3]), whole(outs[4])],
        [
            pltpu.VMEM((rows, 2 * rows), BF16),
            pltpu.VMEM((pair_width, 2 * rows), F32),
            pltpu.VMEM((rows, pair_width), F32),
            pltpu.VMEM((pair_width, rows), BF16),
        ],
        2 * 2 * pairs * rows * 2 * rows * 1000,
        "attention_backward",
        (pairs,),
    )


def norm_parts(values):
    centered = values - jnp.mean(values, axis=-1, keepdims=True)
    inverse = lax.rsqrt(jnp.mean(centered * centered, axis=-1, keepdims=True) + EPSILON)
    return centered * inverse, inverse


def tn(left_side, right_side):
    return lax.dot_general(
        left_side, right_side, (((0,), (0,)), ((), ())), preferred_element_type=F32
    )


def qkv_body(x_ref, member_ref, mod_ref, own_ref, q_ref, kv_ref, normed_ref):
    width = x_ref.shape[1]
    half = width // 2
    mods = jnp.dot(member_ref[...], mod_ref[...], preferred_element_type=F32)
    x_hat, _ = norm_parts(x_ref[...].astype(F32))
    normed = (x_hat * (1.0 + mods[:, width:]) + mods[:, :width]).astype(BF16)
    normed_ref[...] = normed
    q = jnp.dot(normed, own_ref[0], preferred_element_type=F32).astype(BF16)
    q_ref[...] = (q.astype(F32) * 0.125).astype(BF16)
    for k in (1, 2):
        kv_ref[:, (k - 1) * half : k * half] = jnp.dot(
            normed, own_ref[k], preferred_element_type=F32
        ).astype(BF16)


def columns_at(at_ref, r, size):
    return pl.ds(pl.multiple_of((at_ref[0] ^ r) * size, size), size)


def qkv_other_body(at_ref, normed_ref, piece_0, piece_1, q_ref, kv_ref):
    half = normed_ref.shape[1] // 2
    sides = [(normed_ref[:, columns_at(at_ref, r, half)], p) for r, p in enumerate((piece_0, piece_1))]

    def product(k):
        return sum(
            jnp.dot(side, piece[k], preferred_element_type=F32) for side, piece in sides
        ).astype(BF16)

    q_ref[...] = (product(0).astype(F32) * 0.125).astype(BF16)
    for k in (1, 2):
        kv_ref[:, (k - 1) * half : k * half] = product(k)


def branch_body(
    at_ref, attended_ref, attended_other_ref, own_ref, piece_0, piece_1, x_ref, member_ref, mod_ref,
    middle_ref, branch_ref, normed_ref
):
    width = x_ref.shape[1]
    half = width // 2
    member = member_ref[...]

    def mods(k):
        return jnp.dot(
            member, mod_ref[:, k * width : (k + 1) * width], preferred_element_type=F32
        )

    branch_ref[...] = jnp.dot(attended_ref[...], own_ref[...], preferred_element_type=F32)
    for r, piece in enumerate((piece_0, piece_1)):
        branch_ref[:, columns_at(at_ref, r, half)] += jnp.dot(
            attended_other_ref[...], piece[...], preferred_element_type=F32
        )
    branch = branch_ref[...]
    middle = x_ref[...].astype(F32) + mods(2) * branch
    middle_ref[...] = middle
    m_hat, _ = norm_parts(middle)
    normed_ref[...] = (m_hat * (1.0 + mods(4)) + mods(3)).astype(BF16)


def ffn_body(
    normed_ref, dout_ref, member_ref, mod_ref, moved_ref, gate_up_ref, down_ref,
    ffn_out_ref, d_normed_top_ref, d_normed_low_ref, normed_t_ref, d_ffn_t_ref, d_gate_ref,
    d_up_ref, hidden_ref, ffn_ref, d_normed_ref, d_ffn_ref,
):
    step = pl.program_id(0)
    last = pl.num_programs(0) - 1

    @pl.when(step == 0)
    def _():
        scale = jnp.dot(member_ref[...], mod_ref[...], preferred_element_type=F32)
        d_ffn_ref[...] = (scale * dout_ref[...].astype(F32)).astype(BF16)
        normed_t_ref[...] = nt(moved_ref[...], normed_ref[...]).astype(BF16)
        d_ffn_t_ref[...] = nt(moved_ref[...], d_ffn_ref[...]).astype(BF16)

    normed, d_ffn = normed_ref[...], d_ffn_ref[...]
    w_gate, w_up, w_down = gate_up_ref[0], gate_up_ref[1], down_ref[...]
    gate = jnp.dot(normed, w_gate, preferred_element_type=F32)
    up = jnp.dot(normed, w_up, preferred_element_type=F32)
    d_hidden = nt(d_ffn, w_down)
    sigma = jax.nn.sigmoid(gate)
    value = gate * sigma
    hid = (value * up).astype(BF16)
    d_up = (d_hidden * value).astype(BF16)
    d_gate = (d_hidden * up * (sigma + value * (1.0 - sigma))).astype(BF16)
    hidden_ref[...] = hid
    d_up_ref[...] = d_up
    d_gate_ref[...] = d_gate
    ffn = jnp.dot(hid, w_down, preferred_element_type=F32)
    d_normed = nt(d_gate, w_gate) + nt(d_up, w_up)

    @pl.when(step == 0)
    def _():
        ffn_ref[...] = ffn
        d_normed_ref[...] = d_normed

    @pl.when(jnp.logical_and(step > 0, step < last))
    def _():
        ffn_ref[...] += ffn
        d_normed_ref[...] += d_normed

    @pl.when(step == last)
    def _():
        ffn_out_ref[...] = (ffn_ref[...] + ffn).astype(ffn_out_ref.dtype)
        total = d_normed_ref[...] + d_normed
        cut = total.shape[0] // 2
        d_normed_top_ref[...] = total[:cut].astype(d_normed_top_ref.dtype)
        d_normed_low_ref[...] = total[cut:].astype(d_normed_low_ref.dtype)


def ffn_grad_body(
    normed_t_ref, normed_t_far_ref, d_ffn_t_ref, d_ffn_t_far_ref,
    d_gate_ref, d_gate_far_ref, d_up_ref, d_up_far_ref, hidden_ref, hidden_far_ref, out_ref,
):
    normed_t = (normed_t_ref, normed_t_far_ref)
    d_ffn_t = (d_ffn_t_ref, d_ffn_t_far_ref)
    for k, (left_t, near, far) in enumerate(
        (
            (normed_t, d_gate_ref, d_gate_far_ref),
            (normed_t, d_up_ref, d_up_far_ref),
            (d_ffn_t, hidden_ref, hidden_far_ref),
        )
    ):
        out_ref[k] = (
            jnp.dot(left_t[0][...], near[...], preferred_element_type=F32)
            + jnp.dot(left_t[1][...], far[...], preferred_element_type=F32)
        ).astype(BF16)


def mix_body(
    middle_ref, ffn_ref, ffn_far_ref, dout_ref, member_ref, mod_ref, d_mods_ref, d_mix_ref,
    info_ref, mixed_ref, known_ref, gate_sum
):
    member = member_ref[...]
    ffn = ffn_ref[...] + ffn_far_ref[...].astype(F32)
    scale = jnp.dot(member, mod_ref[...], preferred_element_type=F32)
    mixed_ref[...] = (middle_ref[...] + scale * ffn).astype(BF16)
    part = tn(member, (dout_ref[...].astype(F32) * ffn).astype(BF16))

    @pl.when(pl.program_id(0) == 0)
    def _():
        gate_sum[...] = part

    @pl.when(pl.program_id(0) == pl.num_programs(0) - 1)
    def _():
        slots = known_ref.shape[0]
        low = 0
        for values in (d_mods_ref[:slots], gate_sum[:slots] + part[:slots], d_mix_ref[...],
                       info_ref[...]):
            known_ref[:, low : low + values.shape[1]] = values.astype(BF16)
            low += values.shape[1]


def middle_back_body(
    at_ref, top_ref, low_ref, top_far_ref, low_far_ref, middle_ref, branch_ref, dout_ref, member_ref,
    mod_ref, own_ref, piece_0, piece_1, d_middle_ref, d_attended_ref, d_attn_ref, d_mods_ref
):
    step = pl.program_id(0)
    rows, width = top_ref.shape
    half = width // 2

    @pl.when(step == 0)
    def _():
        d_mods_ref[...] = jnp.zeros_like(d_mods_ref)

    member = member_ref[...]

    def mods(k):
        return jnp.dot(
            member, mod_ref[:, k * width : (k + 1) * width], preferred_element_type=F32
        )

    def add_mods(k, values):
        d_mods_ref[:, k * width : (k + 1) * width] += tn(member, values.astype(BF16))

    middle = middle_ref[...]
    m_hat, inverse = norm_parts(middle)
    d_normed = jnp.where(
        step == 0,
        top_ref[...] + top_far_ref[...].astype(F32),
        low_ref[...] + low_far_ref[...].astype(F32),
    )
    add_mods(1, d_normed)
    add_mods(2, d_normed * m_hat)
    d_hat = d_normed * (1.0 + mods(4))
    d_middle = dout_ref[...].astype(F32) + inverse * (
        d_hat
        - jnp.mean(d_hat, axis=-1, keepdims=True)
        - m_hat * jnp.mean(d_hat * m_hat, axis=-1, keepdims=True)
    )
    d_middle_ref[...] = d_middle
    add_mods(0, d_middle * branch_ref[...])
    d_attn = (mods(2) * d_middle).astype(BF16)
    d_attn_ref[...] = d_attn
    d_attended_ref[:, :half] = nt(d_attn, own_ref[...]).astype(BF16)

    d_attended_ref[:, half:] = sum(
        nt(d_attn_ref[:, columns_at(at_ref, r, half)], piece[...])
        for r, piece in enumerate((piece_0, piece_1))
    ).astype(BF16)


def attention_grad_body(
    q_ref, own_ref, far_ref, d_left_ref, normed_ref, d_attn_ref, attended_ref, attended_other_ref,
    moved_ref, d_proj_ref, back_ref, keep_ref, send_ref
):
    width = normed_ref.shape[1]
    half = width // 2
    d_proj_ref[:, :width] = q_ref[...]
    total = (own_ref[...].astype(F32) + far_ref[...].astype(F32)).astype(BF16)
    d_proj_ref[:, width:] = total[:, : 2 * width]
    pair_width = d_left_ref.shape[1]
    back_ref[:, :pair_width] = d_left_ref[...]
    back_ref[:, pair_width:] = total[:, 2 * width :]
    turned = nt(moved_ref[...], normed_ref[...]).astype(BF16)
    for j in range(4):
        if j == 3:
            turned = nt(moved_ref[...], d_attn_ref[...]).astype(BF16)
            right_side = jnp.concatenate([attended_ref[...], attended_other_ref[...]], axis=1)
        else:
            right_side = d_proj_ref[:, j * width : (j + 1) * width]
        total = jnp.dot(turned, right_side, preferred_element_type=F32).astype(BF16)
        for k in range(2):
            keep_ref[k, j] = total[:half, k * half : (k + 1) * half]
            send_ref[k, j] = total[half:, k * half : (k + 1) * half]


def chain_parts(early_ref):
    groups, _, doubled, columns = early_ref.shape
    count = groups * doubled
    return early_ref[:, 0].reshape(count, columns), early_ref[:, 1].reshape(count, columns)


def early_chain_body(here_ref, early_ref, mod_weight_ref, weight_out, bias_out, d_cond_out, mix_out):
    step = pl.program_id(0)
    width = mod_weight_ref.shape[1]
    wide = mod_weight_ref.shape[0]
    modded = 2 * width
    mixed = modded + mix_out.shape[1]
    first, second = chain_parts(early_ref)
    cond = first[:, mixed : mixed + wide]

    def block(low):
        summed = first[:, low : low + width].astype(F32) + second[:, low : low + width].astype(F32)
        early = summed.astype(BF16)
        weight_out[...] = tn(cond, early)
        bias_out[...] = jnp.sum(summed, axis=0, keepdims=True)
        return nt(early, mod_weight_ref[...])

    @pl.when(step == 0)
    def _():
        d_cond_out[...] = block(0)

    @pl.when(step == 1)
    def _():
        d_cond_out[...] += block(width)
        mix = first[:, modded:mixed].astype(F32) + second[:, modded:mixed].astype(F32)
        mix = jnp.sum(mix.reshape(-1, 2, early_ref.shape[2] // 2, mixed - modded), axis=0)
        own = mix_out.shape[0]
        own_half = mix[0, :own] + mix[1, own : 2 * own]
        other_half = mix[0, own : 2 * own] + mix[1, :own]
        mix_out[...] = jnp.where((here_ref[0] & 1) == 0, own_half, other_half)


def late_chain_body(
    far_count, pair_columns, here_ref, early_ref, held_ref, near_ref, mod_weight_ref, d_cond_ref,
    weight_in, weight_out, bias_out, time_out, cath_out
):
    count = held_ref.shape[0]
    slots = early_ref.shape[2] // 2
    wide = mod_weight_ref.shape[0]
    first, _ = chain_parts(early_ref)
    low = 2 * mod_weight_ref.shape[1] + pair_columns
    cond, times, slope = (first[:, low + k * wide : low + (k + 1) * wide] for k in range(3))
    arches = first[:, low + 3 * wide :]
    row = lax.broadcasted_iota(jnp.int32, (count, count), 0)
    column = lax.broadcasted_iota(jnp.int32, (count, count), 1)
    place = column // slots
    apart = (place % far_count) * 4 + place // far_count
    order = ((apart ^ here_ref[0]) * slots + column % slots == row).astype(BF16)
    late = (
        jnp.dot(order, held_ref[...], preferred_element_type=F32)
        + jnp.dot(order, near_ref[...], preferred_element_type=F32)
    ).astype(BF16)
    weight_out[...] = tn(cond, late)
    bias_out[...] = jnp.sum(late.astype(F32), axis=0, keepdims=True)
    d_cond = (nt(late, mod_weight_ref[...]) + d_cond_ref[...]) * slope.astype(F32)
    high = d_cond.astype(BF16)
    rest = (d_cond - high.astype(F32)).astype(BF16)
    time_out[...] = tn(times, high) + tn(times, rest)
    cath_out[...] = (tn(arches, high) + tn(arches, rest))[: cath_out.shape[0]]


def deliver_body(stays_ref, *refs):
    own_ref, came_ref, outs = refs[0], refs[1], refs[2:]

    def deliver(source):
        low = 0
        for ref in outs:
            ref[...] = source[:, low : low + ref.shape[1]]
            low += ref.shape[1]

    @pl.when(stays_ref[0] == 1)
    def _():
        deliver(own_ref)

    @pl.when(stays_ref[0] == 0)
    def _():
        deliver(came_ref)


def input_back_body(
    at_ref, d_proj_ref, x_ref, d_middle_ref, member_ref, mod_ref, own_ref, piece_0, piece_1,
    grad_ref, d_mods_ref, total_ref
):
    width = x_ref.shape[1]
    half = width // 2

    def product(weights, low):
        return sum(
            nt(d_proj_ref[:, j * width + low : j * width + low + half], weights[j])
            for j in range(3)
        )

    total_ref[...] = product(own_ref, 0)
    for r, piece in enumerate((piece_0, piece_1)):
        total_ref[:, columns_at(at_ref, r, half)] += product(piece, half)
    d_normed = total_ref[...]
    member = member_ref[...]
    scale = jnp.dot(member, mod_ref[:, width:], preferred_element_type=F32)
    x_hat, inverse = norm_parts(x_ref[...].astype(F32))
    slots = d_mods_ref.shape[0]
    d_mods_ref[:, :width] = tn(member, d_normed.astype(BF16))[:slots].astype(BF16)
    d_mods_ref[:, width:] = tn(member, (d_normed * x_hat).astype(BF16))[:slots].astype(BF16)
    d_hat = d_normed * (1.0 + scale)
    grad_ref[...] = (
        d_middle_ref[...]
        + inverse
        * (
            d_hat
            - jnp.mean(d_hat, axis=-1, keepdims=True)
            - x_hat * jnp.mean(d_hat * x_hat, axis=-1, keepdims=True)
        )
    ).astype(BF16)


ANYWHERE = pl.BlockSpec(memory_space=pl.ANY)
IN_SMEM = pl.BlockSpec(memory_space=pltpu.SMEM)


def call(body, operands, specs, outs, out_specs, scratch, flops, name, grid=(1,)):
    moved = sum(math.prod(a.shape) * a.dtype.itemsize for a in operands) + sum(
        math.prod(o.shape) * jnp.dtype(o.dtype).itemsize for o in outs
    )
    return pl.pallas_call(
        body,
        grid=grid,
        in_specs=specs,
        out_specs=out_specs,
        out_shape=outs,
        scratch_shapes=scratch,
        compiler_params=pltpu.CompilerParams(vmem_limit_bytes=VMEM_LIMIT),
        cost_estimate=pl.CostEstimate(
            flops=flops // COST_CUT, bytes_accessed=moved // COST_CUT, transcendentals=0
        ),
        name=name,
    )(*operands)


def added(first, second):
    return first + second


def adder(cut, operands, shapes, name):
    def body(*refs):
        count = len(operands)
        for ref, value in zip(refs[count:], cut(*[ref[...] for ref in refs[:count]])):
            ref[...] = value

    outs = [shaped(shape) for shape in shapes]
    return call(
        body, operands, [whole(a) for a in operands], outs, [whole(a) for a in outs], [], 0, name
    )


def first_sum_body(keep_ref, far_ref, sent_a, rest_a, sent_b, rest_b):
    total = added(keep_ref[0], far_ref[0])
    rows, side = sent_a.shape[1:]
    rest_a[0], sent_a[0] = total[:rows, :side], total[rows:, :side]
    quarter = rows // 2
    for k in range(2):
        low = k * rows
        rest_b[0, k] = total[low : low + quarter, side:]
        sent_b[0, k] = total[low + quarter : low + rows, side:]


def shaped(shape, dtype=BF16):
    return jax.ShapeDtypeStruct(shape, dtype)


def make_moves(dp_count):
    def pairs(target):
        moved = []
        for d in range(dp_count):
            for m in range(2):
                to_d, to_m = target(d, m)
                if (to_d, to_m) != (d, m):
                    moved.append((d * 2 + m, to_d * 2 + to_m))
        return moved

    def mover(target):
        table = pairs(target)
        return lambda array: lax.ppermute(array, AXES, table)

    turn = mover(lambda d, m: ((d & ~1) | m, d & 1))
    turn_far = mover(lambda d, m: ((d & ~1) | m, 1 - (d & 1)))
    across = mover(lambda d, m: (d, 1 - m))

    def flip(bit):
        return mover(lambda d, m: (d ^ (1 << bit), m))

    def to(mask, over):
        return mover(lambda d, m: (d ^ mask, m ^ over))

    return turn, turn_far, across, flip, to


def shards(
    tokens,
    pair_left,
    pair_right,
    chain_len,
    chain_time,
    chain_arch,
    cath_table,
    time_weight,
    mod_weight,
    mod_bias,
    qkv_weight,
    pair_weight,
    out_weight,
    gate_up_weight,
    down_weight,
    cotangent,
):
    dp_count = lax.axis_size("dp")
    bits = dp_count.bit_length() - 1
    turn, turn_far, across, flip, to = make_moves(dp_count)
    core_swap = flip(0)
    dp_at = lax.axis_index("dp")
    mp_at = lax.axis_index("mp")
    core = dp_at & 1
    rows, width = tokens.shape
    slots = chain_len.shape[1]
    half_heads = pair_weight.shape[1]
    heads = 2 * half_heads
    pair_width = pair_left.shape[1]
    cond_width = time_weight.shape[0]
    half = width // 2
    hidden = down_weight.shape[0]

    def after(array, *earlier):
        return lax.optimization_barrier((array, *earlier))[0]

    def beside(made, *received):
        return lax.optimization_barrier((*made, *received))[: len(made)]

    held_chains = jnp.concatenate(
        [chain_len.astype(F32), chain_time, chain_arch.astype(F32)], axis=0
    )
    near_chains = core_swap(held_chains)

    cut = width // 2
    stays = core == mp_at

    def turned_in(array, *earlier):
        return jnp.where(stays, array, turn(after(array, *earlier)))

    pair_mix_other = across(pair_weight)
    x_in = turned_in(tokens)
    right_own = turned_in(pair_right, x_in)
    left_in = turned_in(pair_left, x_in)
    qkv_y = across(after(lax.dynamic_slice_in_dim(qkv_weight, core * cut, cut, 1), x_in))
    out_y = across(after(lax.dynamic_slice_in_dim(out_weight, core * cut, cut, 1), qkv_y))
    dout = turned_in(cotangent, out_y)
    dout_far = turn_far(after(cotangent, out_y))

    def ends_of(chains):
        return jnp.cumsum(chains[0].astype(jnp.int32))

    chains = jnp.where(core == mp_at, held_chains, near_chains)
    far_chains = jnp.where(core == mp_at, near_chains, held_chains)
    arches = chains[2].astype(jnp.int32)
    ends = ends_of(chains)
    times = jnp.concatenate([chains[1], far_chains[1]])

    def ids_of(part, ends=ends):
        positions = jnp.arange(rows, dtype=jnp.int32) + part * rows
        return jnp.sum((positions[:, None] >= ends[None, :]).astype(jnp.int32), axis=1)

    own_ids = ids_of(core)
    key_ids = jnp.concatenate([own_ids, ids_of(1 - core)])
    chain_numbers = jnp.arange(slots, dtype=jnp.int32)
    doubled = jnp.concatenate([chain_numbers, chain_numbers])[None, :]
    member = (own_ids[:, None] == doubled).astype(BF16)
    member_far = (ids_of(core, ends_of(far_chains))[:, None] == doubled).astype(BF16)
    lanes = jnp.arange(128, dtype=jnp.int32)[None, :] & 63
    hot = (own_ids[:, None] == lanes).astype(BF16)
    pens = jnp.where((key_ids[:, None] != lanes) & (lanes <= slots), -1e30, 0.0).astype(BF16)
    pen_own, pen_near = pens[:rows], pens[rows:]

    half_cond = cond_width // 2
    frequency = jnp.exp(jnp.arange(half_cond, dtype=F32) * (-math.log(10000.0) / half_cond))
    angles = times[:, None] * 1000.0 * frequency[None, :]
    time_embed = jnp.concatenate([jnp.sin(angles), jnp.cos(angles)], axis=1).astype(BF16)
    both_arches = jnp.concatenate([arches, far_chains[2].astype(jnp.int32)])
    arch_onehot = (
        both_arches[:, None] == jnp.arange(cath_table.shape[0], dtype=jnp.int32)[None, :]
    ).astype(F32)
    cond_pre = dot_f32(time_embed, time_weight) + highest_dot(arch_onehot, cath_table.astype(F32))
    cond_value, cond_slope = silu_parts(cond_pre)
    cond_act = cond_value.astype(BF16)
    chain_mod = dot_f32(cond_act, mod_weight) + mod_bias.astype(F32)[None, :]
    mod_high = lax.reduce_precision(chain_mod, 8, 7)
    mod_low = (chain_mod - mod_high).astype(BF16)
    mod_high = mod_high.astype(BF16)
    mods = jnp.concatenate([mod_high[:slots], mod_low[:slots]], axis=0)
    gate_far = jnp.concatenate([mod_high[slots:], mod_low[slots:]], axis=0)[:, 5 * width :]
    arch_low = (arches[:, None] == jnp.arange(128, dtype=jnp.int32)[None, :]).astype(BF16)
    info = jnp.concatenate(
        [cond_act[:slots], time_embed[:slots], cond_slope[:slots].astype(BF16), arch_low], axis=1
    )

    order = [int(format(p, "0%db" % bits)[::-1], 2) for p in range(dp_count)]
    block_at = jnp.array(order, jnp.int32) ^ dp_at
    block_rows = width // dp_count
    source = (block_at[:, None] * block_rows + jnp.arange(block_rows)[None, :]).reshape(-1)
    moved = (source[:, None] == jnp.arange(width)[None, :]).astype(BF16)
    at = core.reshape(1).astype(jnp.int32)
    semaphores = pltpu.SemaphoreType.DMA

    mod_a = mods[:, : 2 * width]
    pair_mix = jnp.concatenate([pair_weight, pair_mix_other], axis=1).astype(F32)
    mix_rows = jnp.transpose(pair_mix).reshape(half_heads, 2, -1)
    part_shape = shaped((rows, half))
    operands = [after(x_in, moved, mods, hot, pens, member_far, gate_far, mix_rows, info), member, mod_a,
                qkv_weight]
    made = call(
        qkv_body,
        operands,
        [whole(a) for a in operands],
        [part_shape, shaped((rows, width)), shaped((rows, width))],
        [whole(part_shape), whole(shaped((rows, width))), whole(shaped((rows, width)))],
        [],
        3 * rows * width * width,
        "project",
    )
    queries, kv_own, normed_a = beside(made, right_own, left_in)
    kv_near, right_near = core_swap(kv_own), core_swap(right_own)
    factors = (right_own, right_near, pen_own, pen_near)
    made = attention_forward(0, mix_rows, queries, left_in, hot, kv_own, kv_near, *factors)
    made = beside(made, qkv_y)
    qkv_y = after(qkv_y, made[0])
    qkv_pieces = [qkv_y, core_swap(qkv_y)]
    first_half = (*made, queries, kv_own, kv_near)
    made = call(
        qkv_other_body,
        [at, after(normed_a, made[0]), *qkv_pieces],
        [IN_SMEM, whole(normed_a), whole(qkv_y), whole(qkv_y)],
        [part_shape, shaped((rows, width))],
        [whole(part_shape), whole(shaped((rows, width)))],
        [],
        3 * rows * width * width,
        "project_other",
    )
    queries, kv_own = beside(made, out_y)
    out_pieces = [out_y, core_swap(out_y)]
    kv_near = core_swap(kv_own)
    made = attention_forward(1, mix_rows, queries, left_in, hot, kv_own, kv_near, *factors)
    made = beside(made, *out_pieces)
    second_half = (*made, queries, kv_own, kv_near)
    attended, attended_other = first_half[0], second_half[0]
    wide = shaped((rows, width), F32)
    thin = shaped((rows, width))
    middle, branch, normed_f = call(
        branch_body,
        [at, attended, attended_other, out_weight, *out_pieces, x_in, member, mods],
        [IN_SMEM]
        + [whole(a) for a in (attended, attended_other, out_weight, *out_pieces, x_in, member, mods)],
        [wide, wide, thin],
        [whole(thin)] * 3,
        [],
        2 * rows * width * width,
        "branch",
    )

    normed_far = across(normed_f)
    gate_mod = mods[:, 5 * width :]
    block = FFN_BLOCK
    active = shaped((rows, hidden))
    turned = shaped((width, rows))

    def feed_forward(normed, dout, member, gate, sum_type):
        column = pl.BlockSpec((rows, block), lambda i: (0, i))
        summed = shaped((rows, width), sum_type)
        part = shaped((rows // 2, width), sum_type)
        return call(
            ffn_body,
            [normed, dout, member, gate, moved, gate_up_weight, down_weight],
            [whole(a) for a in (normed, dout, member, gate, moved)]
            + [
                pl.BlockSpec((2, width, block), lambda i: (0, 0, i)),
                pl.BlockSpec((block, width), lambda i: (i, 0)),
            ],
            [summed, part, part, turned, turned, active, active, active],
            [whole(thin), whole(part), whole(part), whole(turned), whole(turned), column, column, column],
            [
                pltpu.VMEM((rows, width), F32), pltpu.VMEM((rows, width), F32),
                pltpu.VMEM((rows, width), BF16),
            ],
            12 * rows * width * hidden,
            "feed_forward",
            (hidden // block,),
        )

    made = feed_forward(normed_f, dout, member, gate_mod, F32)
    ffn, d_normed_top, d_normed_low, normed_t, d_ffn_t, d_gate, d_up, hid = made
    normed_far, dout_far = lax.optimization_barrier((normed_far, dout_far, *made))[:2]
    ffn_for, top_for, low_for, normed_t_far, d_ffn_t_far, d_gate_far, d_up_far, hid_far = feed_forward(
        normed_far, dout_far, member_far, gate_far, BF16
    )
    top_far, low_far = across(top_for), across(low_for)

    grad = shaped((3, half, hidden))
    grad_block = pl.BlockSpec((3, half, GRAD_BLOCK), lambda i: (0, 0, i))
    column = pl.BlockSpec((rows, GRAD_BLOCK), lambda i: (0, i))
    turned_half = [normed_t, normed_t_far, d_ffn_t, d_ffn_t_far]
    sides = [d_gate, d_gate_far, d_up, d_up_far, hid, hid_far]

    def ffn_grads(part, *earlier):
        row_half = pl.BlockSpec((half, rows), lambda i: (part, 0))
        return call(
            ffn_grad_body,
            [after(turned_half[0], *earlier), *turned_half[1:], *sides],
            [row_half] * 4 + [column] * 6,
            [grad],
            [grad_block],
            [],
            6 * rows * width * hidden,
            "feed_forward_grads",
            (hidden // GRAD_BLOCK,),
        )[0]

    (send,) = beside((ffn_grads(1),), top_far)
    far = core_swap(send)
    (keep,) = beside((ffn_grads(0, send),), far, low_far)
    ffn_far = across(after(ffn_for, keep))

    def plus(kept, received):
        return (kept.astype(F32) + received.astype(F32)).astype(BF16)

    def halves(array, upper):
        size = array.shape[-2] // 2
        return array[..., size:, :] if upper else array[..., :size, :]

    def y_part(kept, received):
        return plus(kept[1], received[1])

    def y_rest(kept, received):
        return plus(kept[0], received[0])

    def bit_part(kept, received):
        return plus(halves(kept, True), halves(received, True))

    def bit_rest(kept, received):
        return plus(halves(kept, False), halves(received, False))

    steps = 2
    row_block = pl.BlockSpec((rows // steps, width), lambda i: (i, 0))
    member_block = pl.BlockSpec((rows // steps, 2 * slots), lambda i: (i, 0))
    mods_early = shaped((2 * slots, 3 * width), F32)
    made = call(
        middle_back_body,
        [at, after(d_normed_top, keep), d_normed_low, top_far, low_far, middle, branch, dout,
         member, mods, out_weight, *out_pieces],
        [IN_SMEM] + [whole(d_normed_top)] * 4 + [row_block] * 3
        + [member_block, whole(mods), whole(out_weight), whole(out_y), whole(out_y)],
        [wide, thin, thin, mods_early],
        [row_block, row_block, row_block, whole(mods_early)],
        [],
        4 * rows * width * width,
        "middle_back",
        (steps,),
    )
    d_middle, d_attended, d_attn, d_mods = made
    side = hidden // 2
    shape_a, shape_b = (3, half // 2, side), (3, 2, half // 4, side)
    block_a = pl.BlockSpec((1, *shape_a[1:]), lambda i: (i, 0, 0))
    block_b = pl.BlockSpec((1, *shape_b[1:]), lambda i: (i, 0, 0, 0))
    sent, rest, sent_b, rest_b = call(
        first_sum_body,
        [keep, far],
        [pl.BlockSpec((1, half, hidden), lambda i: (i, 0, 0))] * 2,
        [shaped(shape_a), shaped(shape_a), shaped(shape_b), shaped(shape_b)],
        [block_a, block_a, block_b, block_b],
        [],
        0,
        "first_sum",
        (3,),
    )
    got, got_b = flip(1)(sent), flip(2)(sent_b)

    def finish(bit, kept, sent):
        while bit < bits:
            received = flip(bit)(sent)
            bit += 1
            if bit < bits:
                kept, sent = bit_rest(kept, received), bit_part(kept, received)
        return kept.astype(F32) + received.astype(F32)

    near_bits = [-1, 1] if bits > 1 else [-1]
    far_bits = list(range(2, bits))

    def several(group):
        moves = []
        for chosen in range(1, 1 << len(group)):
            mask, over = 0, 0
            for k, bit in enumerate(group):
                if chosen >> k & 1:
                    mask, over = (mask, 1) if bit < 0 else (mask | 1 << bit, over)
            moves.append((mask, over))
        return moves

    def gather_step(group, held):
        return jnp.concatenate(
            [held] + [to(mask, over)(held) for mask, over in several(group)], axis=0
        )

    made = attention_backward(
        mix_rows, after(d_attended, sent, sent_b), (first_half, second_half), left_in, *factors
    )
    d_query, d_own, d_far, d_left = beside(made[:4], ffn_far, got, got_b)

    def second_cut(rest, got, rest_b, got_b):
        total, total_b = added(rest, got), added(rest_b, got_b)
        rows = total.shape[1] // 2
        return total[:, rows:], total[:, :rows], total_b[:, 1], total_b[:, 0]

    shape = (3, half // 4, side)
    sent, rest, sent_b, rest_b = adder(
        second_cut, [rest, got, rest_b, got_b], [shape] * 4, "second_sum"
    )
    got, got_b = flip(2)(sent), flip(1)(sent_b)
    d_mix = made[4]
    far_kv = core_swap(d_far)

    known = shaped((slots, 4 * width + d_mix.shape[1] + info.shape[1]))
    mixed, known = call(
        mix_body,
        [after(middle, d_far, sent, sent_b), ffn, ffn_far, dout, member, gate_mod, d_mods, d_mix,
         info],
        [row_block] * 4 + [member_block] + [whole(a) for a in (gate_mod, d_mods, d_mix, info)],
        [thin, known],
        [row_block, whole(known)],
        [pltpu.VMEM((2 * slots, width), F32)],
        4 * rows * 16 * width,
        "mix",
        (steps,),
    )
    mixed, known = beside((mixed, known), far_kv)
    mixed_own, mixed = mixed, turn(mixed)
    early = lax.all_gather(known, AXES, axis=0, tiled=False)

    proj_grad = shaped((rows, 3 * width))
    back = shaped((rows, 2 * pair_width))
    grad = shaped((2, 4, half, half))
    operands = [d_query, d_own, far_kv, d_left, after(normed_a, known), d_attn, attended,
                attended_other, moved]
    outs = [proj_grad, back, grad, grad]
    made = call(
        attention_grad_body,
        operands,
        [whole(a) for a in operands],
        outs,
        [whole(a) for a in outs],
        [],
        12 * rows * width * width,
        "attention_grads",
    )
    d_proj, back, keep_qkvo, send_qkvo = beside(made, got, got_b, mixed)
    far_qkvo = core_swap(send_qkvo)
    stay_flag = stays.reshape(1).astype(jnp.int32)

    def delivered(own, came, widths):
        blocks = [pl.BlockSpec((rows // 2, w), lambda i: (i, 0)) for w in [own.shape[1]] * 2 + widths]
        return call(
            deliver_body,
            [stay_flag, own, came],
            [IN_SMEM, *blocks[:2]],
            [shaped((rows, w)) for w in widths],
            blocks[2:],
            [],
            0,
            "deliver",
            (2,),
        )

    (mixed,) = delivered(mixed_own, after(mixed, d_proj), [width])
    keep_qkvo = after(keep_qkvo, mixed)
    back_own, back = back, turn(back)

    def third_cut(rest, got, rest_b, got_b):
        total = jnp.concatenate([added(rest, got), added(rest_b, got_b)], axis=2)
        rows = total.shape[1] // 2
        return total[:, rows:], total[:, :rows]

    shape = (3, half // 8, hidden)
    sent, rest = adder(third_cut, [rest, got, rest_b, got_b], [shape] * 2, "third_sum")

    def qkvo_cut(keep, far):
        total = added(keep, far)
        rows = half // 2
        return total[1, :2], total[0, :2], total[:, 2:, rows:], total[:, 2:, :rows]

    shape, shape_vo = (2, half, half), (2, 2, half // 2, half)
    sent_qk, rest_qk, sent_vo, rest_vo = adder(
        qkvo_cut, [keep_qkvo, far_qkvo], [shape, shape, shape_vo, shape_vo], "qkvo_sum"
    )
    got_qk, got_vo = across(sent_qk), flip(1)(sent_vo)
    mods_late = shaped((slots, 2 * width))
    operands = [at, after(d_proj, sent_qk, sent_vo, sent), x_in, d_middle, member, mod_a,
                qkv_weight, *qkv_pieces]
    made = call(
        input_back_body,
        operands,
        [IN_SMEM] + [whole(a) for a in operands[1:]],
        [thin, mods_late],
        [whole(thin), whole(mods_late)],
        [pltpu.VMEM((rows, width), F32)],
        6 * rows * width * width,
        "input_back",
    )
    tokens_out, held = beside(made, got_qk, got_vo)
    got = flip(3)(sent)

    def together(*arrays):
        return lax.optimization_barrier(arrays)

    def qkvo_second(rest_qk, got_qk, rest_vo, got_vo):
        total, total_vo = added(rest_qk, got_qk), added(rest_vo, got_vo)
        rows = half // 2
        return total[:, rows:], total[:, :rows], total_vo[1], total_vo[0]

    shape = (2, half // 2, half)
    sent_qk, rest_qk, sent_vo, rest_vo = adder(
        qkvo_second, [after(rest_qk, tokens_out), got_qk, rest_vo, got_vo], [shape] * 4, "qkvo_second"
    )
    got_qk, got_vo = flip(1)(sent_qk), across(sent_vo)
    token_gradient = turn(after(tokens_out, sent_vo))
    held = gather_step(far_bits, held)

    def qkvo_third(rest_qk, got_qk, rest_vo, got_vo):
        total = jnp.concatenate([added(rest_qk, got_qk), added(rest_vo, got_vo)], axis=0)
        rows = half // 4
        return total[:, rows:], total[:, :rows]

    shape = (4, half // 4, half)
    sent_qkvo, qkvo = adder(
        qkvo_third, [rest_qk, got_qk, rest_vo, got_vo], [shape] * 2, "qkvo_third"
    )
    left_grad, right_grad = delivered(back_own, after(back, tokens_out), [pair_width, pair_width])
    held, qkvo, sent_qkvo, token_gradient = together(
        held, qkvo, sent_qkvo, token_gradient, left_grad, right_grad
    )[:4]
    held = gather_step(near_bits, held)
    got_qkvo = flip(2)(sent_qkvo)
    here = ((dp_at >> 1) * 2 + mp_at).reshape(1).astype(jnp.int32)
    early = early.reshape(dp_count // 2, 2, 2 * slots, -1)
    late_to = 2 * width
    weight_shape = shaped(mod_weight.shape, F32)
    bias_shape = shaped((1, 6 * width), F32)
    cond_shape = shaped((dp_count * slots, cond_width), F32)
    mix_shape = shaped((half_heads // 2, 2 * pair_width), F32)
    later = lambda i: (0, 1 + i)
    early = after(early, tokens_out, sent_qkvo)
    early_weight, early_bias, early_cond, mix_sum = call(
        early_chain_body,
        [here, early, mod_weight],
        [IN_SMEM, whole(early), pl.BlockSpec((cond_width, late_to), later)],
        [weight_shape, bias_shape, cond_shape, mix_shape],
        [
            pl.BlockSpec((cond_width, late_to), later), pl.BlockSpec((1, late_to), later),
            whole(cond_shape), whole(mix_shape),
        ],
        [],
        0,
        "early_chains",
        (2,),
    )
    mix_sum = mix_sum.reshape(half_heads, -1)
    taken = mix_sum.shape[1] // dp_count
    pair_sum = jnp.transpose(lax.dynamic_slice_in_dim(mix_sum, dp_at * taken, taken, 1))
    def last_sums(kept, got):
        for bit in range(4, bits):
            kept, got = bit_rest(kept, got), flip(bit)(bit_part(kept, got))
        total = kept[:-1].astype(F32) + got[:-1].astype(F32)
        return total, jnp.transpose(kept[-1].astype(F32) + got[-1].astype(F32))

    ffn_sum, down_sum = last_sums(rest, got)
    (token_gradient,) = delivered(tokens_out, token_gradient, [width])
    held, got_qkvo = together(
        held, got_qkvo, early_weight, pair_sum, ffn_sum, down_sum, token_gradient
    )[:2]
    near = core_swap(held)
    sent_qkvo, qkvo = bit_part(qkvo, got_qkvo), bit_rest(qkvo, got_qkvo)
    got_qkvo = flip(3)(sent_qkvo)

    late_bias_shape = shaped((1, late_to), F32)
    operands = [here, early, held, near]
    time_shape, cath_shape = shaped((cond_width, cond_width), F32), shaped(cath_table.shape, F32)
    first_columns = pl.BlockSpec((cond_width, late_to), lambda i: (0, 0))
    mod_weight_sum, late_bias, time_sum, cath_sum = pl.pallas_call(
        functools.partial(late_chain_body, dp_count // 4, mix_shape.shape[1]),
        grid=(1,),
        in_specs=[IN_SMEM]
        + [whole(a) for a in operands[1:]]
        + [first_columns, whole(cond_shape), ANYWHERE],
        out_specs=[first_columns, whole(late_bias_shape), whole(time_shape), whole(cath_shape)],
        out_shape=[weight_shape, late_bias_shape, time_shape, cath_shape],
        input_output_aliases={6: 0},
        compiler_params=pltpu.CompilerParams(vmem_limit_bytes=VMEM_LIMIT),
        name="late_chains",
    )(*operands, mod_weight, early_cond, early_weight)
    mod_bias_sum = jnp.concatenate([late_bias, early_bias[:, late_to:]], axis=1).reshape(-1)

    got_qkvo, _ = together(got_qkvo, mod_weight_sum)
    qkv_sum, out_sum = last_sums(qkvo, got_qkvo)

    return (
        mixed,
        token_gradient,
        left_grad,
        right_grad,
        cath_sum,
        time_sum,
        mod_weight_sum,
        mod_bias_sum,
        qkv_sum,
        pair_sum,
        out_sum,
        ffn_sum,
        down_sum,
    )


def solution(mesh):
    by_rows = P(AXES, None)
    placed = (
        by_rows,
        by_rows,
        by_rows,
        P("dp", None),
        P("dp", None),
        P("dp", None),
        P(),
        P(),
        P(),
        P(),
        P(None, None, "mp"),
        P(None, "mp"),
        P("mp", None),
        P(None, None, "mp"),
        P("mp", None),
        by_rows,
    )
    return jax.shard_map(
        shards,
        mesh=mesh,
        in_specs=placed,
        out_specs=(
            by_rows,
            by_rows,
            by_rows,
            by_rows,
            P(),
            P(),
            P(),
            P(),
            P(None, "dp", "mp"),
            P("dp", "mp"),
            P("mp", "dp"),
            P(None, "dp", "mp"),
            P("mp", "dp"),
        ),
        check_vma=False,
    )
```
